32 devices in a mesh: ctx: 4 (over y, x), fsdp: 8 (over z, core).
Axes of the slice: x: 2, y: 2, z: 4, core: 2. Of those that a mesh axis runs over, the one named last changes fastest.
Arguments:
- inputs: bfloat16 [8, 512, 2048], P('fsdp', 'ctx'), may hold values from -6 to 6
- lengths: int32 [8], P('fsdp'), may hold values from 128 to 512, as said below
- w_query: bfloat16 [2048, 2048], P('fsdp'), may hold values from -0.0625 to 0.0625
- w_key: bfloat16 [2048, 2048], P('fsdp'), may hold values from -0.0625 to 0.0625
- w_value: bfloat16 [2048, 2048], P('fsdp'), may hold values from -0.125 to 0.125
- w_out: bfloat16 [2048, 2048], P('fsdp'), may hold values from -0.5 to 0.5
- w_gate: bfloat16 [2048, 5120], P('fsdp'), may hold values from -0.125 to 0.125
- w_up: bfloat16 [2048, 5120], P('fsdp'), may hold values from -0.125 to 0.125
- w_down: bfloat16 [5120, 2048], P('fsdp'), may hold values from -0.125 to 0.125
- norm_attn: bfloat16 [2048], P('fsdp'), may hold values from 0.5 to 1.5
- norm_ffn: bfloat16 [2048], P('fsdp'), may hold values from 0.5 to 1.5
- relative_bias_table: bfloat16 [32, 32], P('fsdp'), may hold values from -6 to 6
- cotangent: bfloat16 [8, 512, 2048], P('fsdp', 'ctx'), may hold values from -6 to 6
Outputs:
- result: bfloat16 [8, 512, 2048], P('fsdp', 'ctx')
- input_grad: bfloat16 [8, 512, 2048], P('fsdp', 'ctx')
- grad_query: float32 [2048, 2048], P('fsdp')
- grad_key: float32 [2048, 2048], P('fsdp')
- grad_value: float32 [2048, 2048], P('fsdp')
- grad_out: float32 [2048, 2048], P('fsdp')
- grad_gate: float32 [2048, 5120], P('fsdp')
- grad_up: float32 [2048, 5120], P('fsdp')
- grad_down: float32 [5120, 2048], P('fsdp')
- grad_norm_attn: float32 [2048], P('fsdp')
- grad_norm_ffn: float32 [2048], P('fsdp')
- grad_table: float32 [32, 32], P('fsdp')
The draws below stay inside these ranges and needn't reach their ends.
Inputs may be any that keep to these rules, and one draw needn't show every extreme that they name: `lengths`: one sequence, drawn from the seed, has all 512 slots live; the others have 512 // 4 to 512.
All inputs are finite; a program needn't handle non-finite values.
Results may differ from the reference program's by a relative error of at most 0.024.
Values may be sent and summed in bfloat16 or wider, within the bound.
No kernel may reach another device: no remote copies, remote signals or barrier semaphores. Data moves between devices by JAX's collectives and lax.ppermute only.
A program may use at most 448 MiB of HBM per device.

```python
import jax
import jax.numpy as jnp
from jax import lax

D = 2048
HEADS = 32
HEAD_DIM = 64
FF = 5120
BUCKETS = 32
BLOCK = 128
SEQ_LEN = 512
SEQS = 8
N_CTX = 4


def draw_lengths(key, part):
    key = jax.random.fold_in(key, 11)
    first_key, second_key = jax.random.split(key)
    drawn = jax.random.randint(first_key, (SEQS,), SEQ_LEN // 4, SEQ_LEN + 1, dtype=jnp.int32)
    chosen = jax.random.randint(second_key, (), 0, SEQS, dtype=jnp.int32)
    return jnp.where(jnp.arange(SEQS, dtype=jnp.int32) == chosen, SEQ_LEN, drawn).astype(jnp.int32)


def level_of(own_key, dims, pieces, low, top_value):
    level, own = 1.0, jax.random.fold_in(own_key, 6)
    for position, parts in pieces:
        steps = jnp.exp(jax.random.uniform(jax.random.fold_in(own, position), (parts,), jnp.float32, low / len(pieces), top_value / len(pieces)))
        level = level * jnp.repeat(steps, dims[position] // parts).reshape([-1 if axis == position else 1 for axis in range(len(dims))])
    return level


def normal_values(rng, dims, scale, most, cuts=(), kind=jnp.bfloat16):
    factor_of = level_of(rng, dims, cuts, -0.22, 0.18) if cuts else 1.0
    entries = jax.random.normal(rng, dims, jnp.float32) * scale * factor_of
    return jnp.minimum(jnp.maximum(entries, -most), most).astype(kind)


def setup_inputs(seed: int = 0) -> dict:
    key_of = jax.random.split(jax.random.key(seed), 14)
    return {
        "inputs": normal_values(key_of[0], (SEQS, SEQ_LEN, D), 1.0, 6.0, ((0, 8), (1, 4))),
        "lengths": draw_lengths(jax.random.fold_in(key_of[13], 71), 0),
        "w_query": normal_values(key_of[2], (D, D), (4 * D) ** -0.5, 0.0625, ((0, 8),)),
        "w_key": normal_values(key_of[3], (D, D), (4 * D) ** -0.5, 0.0625, ((0, 8),)),
        "w_value": normal_values(key_of[4], (D, D), D ** -0.5, 0.125, ((0, 8),)),
        "w_out": normal_values(key_of[5], (D, D), (D // 16) ** -0.5, 0.5, ((0, 8),)),
        "w_gate": normal_values(key_of[6], (D, FF), D ** -0.5, 0.125, ((0, 8),)),
        "w_up": normal_values(key_of[7], (D, FF), D ** -0.5, 0.125, ((0, 8),)),
        "w_down": normal_values(key_of[8], (FF, D), (FF // 2) ** -0.5, 0.125, ((0, 8),)),
        "norm_attn": jnp.clip(1.0 + 0.1 * jax.random.normal(key_of[9], (D,), jnp.float32), 0.5, 1.5).astype(jnp.bfloat16),
        "norm_ffn": jnp.clip(1.0 + 0.1 * jax.random.normal(key_of[10], (D,), jnp.float32), 0.5, 1.5).astype(jnp.bfloat16),
        "relative_bias_table": normal_values(key_of[11], (BUCKETS, HEADS), 1.0, 6.0, ((0, 8),)),
        "cotangent": normal_values(key_of[12], (SEQS, SEQ_LEN, D), 1.0, 6.0, ((0, 8), (1, 4))),
    }


@jax.custom_vjp
def low(v):
    return lax.optimization_barrier(v.astype(jnp.bfloat16)).astype(jnp.float32)

@jax.custom_vjp
def low_back(v):
    return v

def low_keep(v):
    return (low(v), None)

def low_pass(kept, grad):
    return (grad,)

def back_keep(v):
    return (v, None)

def back_low(kept, grad):
    return (low(grad),)
low.defvjp(low_keep, low_pass)
low_back.defvjp(back_keep, back_low)
bucket_edges = (12, 16, 23, 32, 46, 64, 91)
highest_precision_mode = lax.Precision.HIGHEST

def buckets_of(offset):
    distance = jnp.abs(offset)
    bucket = jnp.minimum(distance, 8)
    for edge_value in bucket_edges:
        bucket = bucket + (distance >= edge_value).astype(jnp.int32)
    return bucket + 16 * (offset > 0).astype(jnp.int32)

def rms_norm(values, gain_row):
    return values * lax.rsqrt(lax.optimization_barrier(jnp.mean(values * values, axis=-1, keepdims=True)) + 1e-06) * gain_row

def layer(seq_inputs, w_query, w_key, w_value, w_out, w_gate, w_up, w_down, norm_attn, norm_ffn, relative_bias_table, length):
    slot_index = jnp.arange(SEQ_LEN, dtype=jnp.int32)
    open_keys = slot_index < length
    normed = low(rms_norm(seq_inputs, norm_attn))
    queries = low_back(low(jnp.dot(normed, w_query, precision=highest_precision_mode))).reshape(SEQ_LEN, HEADS, HEAD_DIM)
    key_heads = low_back(low(jnp.dot(normed, w_key, precision=highest_precision_mode))).reshape(SEQ_LEN, HEADS, HEAD_DIM)
    value_heads = low_back(low(jnp.dot(normed, w_value, precision=highest_precision_mode))).reshape(SEQ_LEN, HEADS, HEAD_DIM)
    bucket_ids = jnp.arange(BUCKETS, dtype=jnp.int32)

    def attend(first_row):
        query_rows = lax.dynamic_slice_in_dim(queries, first_row, BLOCK, 0)
        raw_scores = jnp.einsum('qhd,khd->hqk', query_rows, key_heads, precision=highest_precision_mode)
        offset = slot_index[None, :] - (first_row + jnp.arange(BLOCK, dtype=jnp.int32))[:, None]
        bucket_indicator = (buckets_of(offset)[None] == bucket_ids[:, None, None]).astype(seq_inputs.dtype)
        position_bias_terms = jnp.einsum('pzj,ps->szj', bucket_indicator, relative_bias_table, precision=highest_precision_mode)
        scores = low_back(raw_scores + position_bias_terms)
        scores = jnp.where(open_keys[None, None, :], scores, -1e+30)
        shifted = jnp.exp(scores - lax.optimization_barrier(jnp.max(scores, axis=-1, keepdims=True)))
        probabilities = low(shifted / lax.optimization_barrier(jnp.sum(shifted, axis=-1, keepdims=True)))
        return jnp.einsum('hqk,khd->qhd', probabilities, value_heads, precision=highest_precision_mode)
    starts = jnp.arange(N_CTX, dtype=jnp.int32) * BLOCK
    attended = lax.map(jax.checkpoint(attend), starts).reshape(SEQ_LEN, D)
    attended = low_back(low(attended))
    hidden = seq_inputs + low_back(jnp.dot(attended, w_out, precision=highest_precision_mode))
    normed_ffn = low(rms_norm(hidden, norm_ffn))
    gate_proj = low_back(jnp.dot(normed_ffn, w_gate, precision=highest_precision_mode))
    up_proj = low_back(jnp.dot(normed_ffn, w_up, precision=highest_precision_mode))
    mixed_units = low(jax.nn.gelu(gate_proj, approximate=True) * up_proj)
    return hidden + low_back(jnp.dot(mixed_units, w_down, precision=highest_precision_mode))

def reference(inputs, lengths, w_query, w_key, w_value, w_out, w_gate, w_up, w_down, norm_attn, norm_ffn, relative_bias_table, cotangent):
    params = tuple((weight.astype(jnp.float32) for weight in (w_query, w_key, w_value, w_out, w_gate, w_up, w_down, norm_attn, norm_ffn, relative_bias_table)))

    def one_sequence(totals, seq_item):
        seq_inputs, seq_cotangent, length = seq_item
        seq_inputs = seq_inputs.astype(jnp.float32)
        live_rows = (jnp.arange(SEQ_LEN, dtype=jnp.int32) < length).astype(jnp.float32)
        seq_cotangent = seq_cotangent.astype(jnp.float32) * live_rows[:, None]

        def forward(values, *weights):
            return layer(values, *weights, length)
        output, pullback = jax.vjp(forward, seq_inputs, *params)
        gradients = pullback(seq_cotangent)
        totals = tuple((total + grad_term for total, grad_term in zip(totals, gradients[1:])))
        return (totals, (output.astype(jnp.bfloat16), gradients[0].astype(jnp.bfloat16)))
    zero_grads = tuple((jnp.zeros_like(weight) for weight in params))
    totals, (results, input_grads) = lax.scan(one_sequence, zero_grads, (inputs, cotangent, lengths))
    return (results, input_grads, totals[0], totals[1], totals[2], totals[3], totals[4], totals[5], totals[6], totals[7], totals[8], totals[9])
```

```python
import functools

import jax
import jax.numpy as jnp
from jax import lax
from jax.experimental import pallas as pl
from jax.experimental.pallas import tpu as pltpu
from jax.sharding import PartitionSpec as P

bucket_edges = (12, 16, 23, 32, 46, 64, 91)
epsilon = 1e-06
masked_score = -1e30
f32 = jnp.float32
bf16 = jnp.bfloat16
vmem_limit = 48 * 1024 * 1024


def dot(a, b, ca=1, cb=0):
    return lax.dot_general(a, b, (((ca,), (cb,)), ((), ())), preferred_element_type=f32)


def buckets_of(offset):
    distance = jnp.abs(offset)
    bucket = jnp.minimum(distance, 8)
    for edge_value in bucket_edges:
        bucket = bucket + (distance >= edge_value).astype(jnp.int32)
    return bucket + 16 * (offset > 0).astype(jnp.int32)


def core_swap(a):
    size = lax.axis_size("fsdp")
    return lax.ppermute(a, "fsdp", [(r, r ^ 1) for r in range(size)])


def chip_send(a, pairs):
    return lax.ppermute(a, "fsdp", [(2 * s + k, 2 * d + k) for s, d in pairs for k in range(2)])


def ctx_send(a, distance):
    size = lax.axis_size("ctx")
    return lax.ppermute(a, "ctx", [(i, i ^ distance) for i in range(size)])


def chip_gather(own, chip):
    chips = lax.axis_size("fsdp") // 2
    if chips == 4:
        above = chip_send(own, [(1, 0), (2, 1), (3, 2), (0, 3)])
        below = chip_send(own, [(0, 1), (1, 2), (2, 3), (3, 0)])
        middle = jnp.where(chip == 1, above, jnp.where(chip == 2, below, own))
        far = chip_send(middle, [(3, 1), (0, 2), (1, 0), (2, 3)])
        return [own, above, far, below]
    return [own] + [
        chip_send(own, [((z + t) % chips, z) for z in range(chips)]) for t in range(1, chips)
    ]


def chip_reduce(slots, chip):
    chips = lax.axis_size("fsdp") // 2
    if chips == 4:
        far = chip_send(slots[2], [(0, 1), (3, 2), (1, 3), (2, 0)]).astype(f32)
        zero = jnp.zeros((), f32)
        up = (slots[1].astype(f32) + jnp.where(chip == 1, far, zero)).astype(bf16)
        down = (slots[3].astype(f32) + jnp.where(chip == 2, far, zero)).astype(bf16)
        ends = jnp.where((chip == 0) | (chip == 3), far, zero)
        from_below = chip_send(up, [(0, 1), (1, 2), (2, 3), (3, 0)])
        from_above = chip_send(down, [(1, 0), (2, 1), (3, 2), (0, 3)])
        return slots[0].astype(f32) + ends + from_below.astype(f32) + from_above.astype(f32)
    total = slots[0].astype(f32)
    for t in range(1, chips):
        total = total + chip_send(slots[t], [(z, (z + t) % chips) for z in range(chips)]).astype(f32)
    return total


def weight_gather(own, chip):
    slots = chip_gather(own, chip)
    return slots + [core_swap(s) for s in slots]


def weight_reduce(mine, other, chip):
    total = (mine.astype(f32) + core_swap(other).astype(f32)).astype(bf16)
    return chip_reduce([total[t] for t in range(total.shape[0])], chip).astype(bf16)


def ctx_gather(a):
    return [a] + [ctx_send(a, t) for t in range(1, lax.axis_size("ctx"))]


def ctx_reduce(partial, rows):
    total = partial[:rows].astype(f32)
    for t in range(1, lax.axis_size("ctx")):
        total = total + ctx_send(partial[t * rows : (t + 1) * rows], t).astype(f32)
    return total


def take_blocks(a, axis, starts, size):
    return jnp.concatenate([lax.dynamic_slice_in_dim(a, s, size, axis) for s in starts], axis)


def forward_kernel(rows, blocks, scal_ref, qkv_ref, bias_ref, att_ref, prob_ref, toeplitz_ref):
    position, length = scal_ref[0], scal_ref[1]
    width = 2 * blocks * rows
    lane = lax.broadcasted_iota(jnp.int32, (1, rows), 1)
    open_keys = jnp.concatenate(
        [((position ^ t) * rows + lane) < length for t in range(blocks)], axis=1
    )
    for j in range(2):
        row = jnp.broadcast_to(bias_ref[0, j : j + 1, :], (rows, width))
        toeplitz_ref[j] = pltpu.roll(row, width - rows, 1, stride=1, stride_axis=0)
    for t in range(blocks):
        halves = []
        at = slice(t * rows, (t + 1) * rows)
        for j in range(2):
            q = qkv_ref[at, 64 * j : 64 * j + 64]
            k = qkv_ref[:, 128 + 64 * j : 192 + 64 * j]
            v = qkv_ref[:, 256 + 64 * j : 320 + 64 * j]
            bias = jnp.concatenate(
                [
                    toeplitz_ref[
                        j,
                        :,
                        pl.ds(
                            pl.multiple_of(
                                (blocks - 1 + (position ^ s) - (position ^ t)) * rows, rows
                            ),
                            rows,
                        ),
                    ]
                    for s in range(blocks)
                ],
                axis=1,
            )
            scores = jnp.where(open_keys, dot(q, k, 1, 1) + bias, masked_score)
            top = jnp.max(scores, axis=1, keepdims=True)
            e = jnp.exp(scores - top)
            probs = (e * (1.0 / jnp.sum(e, axis=1, keepdims=True))).astype(bf16)
            prob_ref[j, at, :] = probs
            halves.append(dot(probs, v))
        att_ref[at, :] = jnp.concatenate(halves, axis=1).astype(bf16)


def backward_kernel(
    rows, blocks, scal_ref, qkv_ref, prob_ref, gatt_ref, out_ref, diag_ref, fold_ref
):
    position = scal_ref[0]
    width = 2 * blocks * rows
    results = [[], [], []]
    for j in range(2):
        fold_ref[...] = jnp.zeros_like(fold_ref)
        k = qkv_ref[:, 128 + 64 * j : 192 + 64 * j]
        v = qkv_ref[:, 256 + 64 * j : 320 + 64 * j]
        grad_q, grad_k, grad_v = [], None, None
        for t in range(blocks):
            at = slice(t * rows, (t + 1) * rows)
            q = qkv_ref[at, 64 * j : 64 * j + 64]
            g = gatt_ref[at, 64 * j : 64 * j + 64]
            probs = prob_ref[j, at, :]
            p = probs.astype(f32)
            gp = dot(g, v, 1, 1)
            pg = p * gp
            delta = jnp.sum(pg, axis=1, keepdims=True)
            ds = (pg - p * delta).astype(bf16)
            grad_q.append(dot(ds, k))
            gk = dot(ds, q, 0, 0)
            gv = dot(probs, g, 0, 0)
            grad_k = gk if grad_k is None else grad_k + gk
            grad_v = gv if grad_v is None else grad_v + gv
            ds32 = ds.astype(f32)
            for s in range(blocks):
                lanes = pl.ds(
                    pl.multiple_of((blocks - 1 + (position ^ s) - (position ^ t)) * rows, rows),
                    rows,
                )
                fold_ref[:, lanes] += ds32[:, s * rows : (s + 1) * rows]
        results[0].append(jnp.concatenate(grad_q, axis=0))
        results[1].append(grad_k)
        results[2].append(grad_v)
        a = fold_ref[...]
        half = rows // 2
        while half >= 8:
            a = a[:half] + pltpu.roll(a[half:], width - half, 1)
            half //= 2
        row = lax.broadcasted_iota(jnp.int32, a.shape, 0)
        for bit in (1, 2, 4):
            a = jnp.where((row & bit) != 0, pltpu.roll(a, width - bit, 1), a)
        diag_ref[0, j : j + 1, :] = jnp.sum(a, axis=0, keepdims=True)
    for n in range(3):
        out_ref[:, 128 * n : 128 * n + 128] = jnp.concatenate(results[n], axis=1).astype(bf16)


def attention_forward(scal, qkv, bias, rows, blocks):
    tokens = rows * blocks
    pairs = bias.shape[0]
    return pl.pallas_call(
        functools.partial(forward_kernel, rows, blocks),
        grid=(pairs,),
        in_specs=[
            pl.BlockSpec(memory_space=pltpu.SMEM),
            pl.BlockSpec((tokens, 384), lambda p: (0, p)),
            pl.BlockSpec((1, 2, 2 * tokens), lambda p: (p, 0, 0)),
        ],
        out_specs=[
            pl.BlockSpec((tokens, 128), lambda p: (0, p)),
            pl.BlockSpec((2, tokens, tokens), lambda p: (p, 0, 0)),
        ],
        out_shape=[
            jax.ShapeDtypeStruct((tokens, 128 * pairs), bf16),
            jax.ShapeDtypeStruct((2 * pairs, tokens, tokens), bf16),
        ],
        scratch_shapes=[pltpu.VMEM((2, rows, 2 * tokens), f32)],
        compiler_params=pltpu.CompilerParams(vmem_limit_bytes=vmem_limit),
        cost_estimate=pl.CostEstimate(
            flops=8 * pairs * tokens * tokens * 64,
            bytes_accessed=4 * pairs * tokens * tokens,
            transcendentals=2 * pairs * tokens * tokens,
        ),
    )(scal, qkv, bias)


def attention_backward(scal, qkv, probs, grad_att, rows, blocks):
    tokens = rows * blocks
    pairs = probs.shape[0] // 2
    return pl.pallas_call(
        functools.partial(backward_kernel, rows, blocks),
        grid=(pairs,),
        in_specs=[
            pl.BlockSpec(memory_space=pltpu.SMEM),
            pl.BlockSpec((tokens, 384), lambda p: (0, p)),
            pl.BlockSpec((2, tokens, tokens), lambda p: (p, 0, 0)),
            pl.BlockSpec((tokens, 128), lambda p: (0, p)),
        ],
        out_specs=[
            pl.BlockSpec((tokens, 384), lambda p: (0, p)),
            pl.BlockSpec((1, 2, 2 * tokens), lambda p: (p, 0, 0)),
        ],
        out_shape=[
            jax.ShapeDtypeStruct((tokens, 384 * pairs), bf16),
            jax.ShapeDtypeStruct((pairs, 2, 2 * tokens), f32),
        ],
        scratch_shapes=[pltpu.VMEM((rows, 2 * tokens), f32)],
        compiler_params=pltpu.CompilerParams(vmem_limit_bytes=vmem_limit),
        cost_estimate=pl.CostEstimate(
            flops=16 * pairs * tokens * tokens * 64,
            bytes_accessed=4 * pairs * tokens * tokens,
            transcendentals=0,
        ),
    )(scal, qkv, probs, grad_att)


def norm_scale(values):
    return lax.rsqrt(jnp.mean(values * values, axis=-1, keepdims=True) + epsilon)


def norm_back(values, scale, gain_row, grad_normed):
    weighted = grad_normed * gain_row
    grad_values = scale * weighted - values * scale**3 * jnp.mean(
        weighted * values, axis=-1, keepdims=True
    )
    grad_gain = jnp.sum(grad_normed * values * scale, axis=0)
    return grad_values, grad_gain


def on_device(
    inputs,
    lengths,
    w_query,
    w_key,
    w_value,
    w_out,
    w_gate,
    w_up,
    w_down,
    norm_attn,
    norm_ffn,
    relative_bias_table,
    cotangent,
):
    blocks = lax.axis_size("ctx")
    shards = lax.axis_size("fsdp")
    chips = shards // 2
    position = lax.axis_index("ctx")
    shard = lax.axis_index("fsdp")
    chip, core = shard // 2, shard % 2
    rows, width = inputs.shape[1], inputs.shape[2]
    tokens = rows * blocks
    heads = relative_bias_table.shape[1]
    head_width = width // heads
    my_heads = heads // blocks
    pairs = my_heads // 2
    strided = (heads // shards) % blocks == 0
    units = w_gate.shape[1] // blocks
    shard_rows = width // shards
    unit_rows = w_down.shape[0] // blocks
    length = lengths[0]
    scal = jnp.stack([position, length]).astype(jnp.int32)

    order = [2 * ((chip + t) % chips) + (core ^ p) for p in range(2) for t in range(chips)]
    place = [((r & 1) ^ core) * chips + ((r >> 1) - chip) % chips for r in range(shards)]

    if strided:
        each = heads // shards // blocks
        local = jnp.arange(my_heads, dtype=jnp.int32)
        my_head_ids = (local // each) * (heads // shards) + position * each + local % each
    else:
        my_head_ids = position * my_heads + jnp.arange(my_heads, dtype=jnp.int32)
    head_columns = (
        my_head_ids[:, None] * head_width + jnp.arange(head_width, dtype=jnp.int32)
    ).reshape(-1)
    per_shard = w_down.shape[0]
    local = jnp.arange(units, dtype=jnp.int32)
    unit_columns = (local // unit_rows) * per_shard + position * unit_rows + local % unit_rows

    def select(stacked, columns):
        chosen = jnp.arange(stacked.shape[-1], dtype=jnp.int32)[:, None] == columns[None, :]
        flat = stacked.reshape(-1, stacked.shape[-1])
        picked = jnp.dot(flat, chosen.astype(bf16), preferred_element_type=f32).astype(bf16)
        return picked.reshape(*stacked.shape[:-1], columns.shape[0])

    picked = select(jnp.stack([w_query, w_key, w_value]), head_columns)
    own_qkv = jnp.transpose(picked.reshape(3, shard_rows, pairs, 128), (1, 2, 0, 3)).reshape(
        shard_rows, pairs * 384
    )
    small = jnp.concatenate([norm_attn, norm_ffn, relative_bias_table.reshape(-1)])[None]

    own_x = take_blocks(inputs[0], 1, [o * shard_rows for o in order], shard_rows)
    all_x = jnp.concatenate(ctx_gather(own_x), axis=0)
    query_slots = position * rows + jnp.arange(rows, dtype=jnp.int32)
    live_rows = (query_slots < length).astype(f32)[:, None]
    own_dy = (cotangent[0].astype(f32) * live_rows).astype(bf16)
    all_dy = jnp.concatenate(ctx_gather(own_dy), axis=0)

    all_small = jnp.concatenate(weight_gather(small, chip), axis=0)
    full_qkv = jnp.concatenate(weight_gather(own_qkv, chip), axis=0)
    if strided:
        head_rows = w_out.shape[0] // blocks
        own_out = lax.dynamic_slice_in_dim(w_out, position * head_rows, head_rows, 0)
        full_out = take_blocks(
            jnp.concatenate(weight_gather(own_out, chip), axis=0),
            0,
            [p * head_rows for p in place],
            head_rows,
        )
    else:
        full_out = lax.dynamic_slice_in_dim(
            lax.all_gather(w_out, "fsdp", axis=0, tiled=True),
            position * my_heads * head_width,
            my_heads * head_width,
            0,
        )
    picked = select(jnp.stack([w_gate, w_up]), unit_columns)
    own_gate_up = jnp.concatenate([picked[0], picked[1]], axis=1)
    full_gate_up = jnp.concatenate(weight_gather(own_gate_up, chip), axis=0)
    own_down = lax.dynamic_slice_in_dim(w_down, position * unit_rows, unit_rows, 0)
    full_down = take_blocks(
        jnp.concatenate(weight_gather(own_down, chip), axis=0),
        0,
        [p * unit_rows for p in place],
        unit_rows,
    )

    gain_local = all_small[:, :shard_rows].astype(f32).reshape(1, width)
    natural = jnp.concatenate(
        [lax.dynamic_slice_in_dim(all_small, p, 1, 0) for p in place], axis=0
    )
    gain_ffn = natural[:, shard_rows : 2 * shard_rows].astype(f32).reshape(1, width)
    table = natural[:, 2 * shard_rows :].reshape(-1, heads)
    bucket_total = table.shape[0]

    chosen_heads = (jnp.arange(heads, dtype=jnp.int32)[:, None] == my_head_ids[None, :]).astype(bf16)
    my_table = jnp.dot(table, chosen_heads, preferred_element_type=f32)
    offset = jnp.arange(2 * tokens, dtype=jnp.int32) - tokens
    bucket_ids = jnp.arange(bucket_total, dtype=jnp.int32)
    of_offset = (buckets_of(offset)[None, :] == bucket_ids[:, None]).astype(f32)
    bias = jnp.einsum(
        "bh,bo->ho", my_table, of_offset, precision=lax.Precision.HIGHEST
    ).reshape(pairs, 2, 2 * tokens)

    all_x32 = all_x.astype(f32)
    scale_all = norm_scale(all_x32)
    normed = (all_x32 * scale_all * gain_local).astype(bf16)
    qkv = dot(normed, full_qkv).astype(bf16)
    attended, probs = attention_forward(scal, qkv, bias, rows, blocks)
    hidden = inputs[0].astype(f32) + ctx_reduce(dot(attended, full_out).astype(bf16), rows)

    scale_ffn = norm_scale(hidden)
    own_nffn = (hidden * scale_ffn * gain_ffn).astype(bf16)
    own_nffn = take_blocks(own_nffn, 1, [o * shard_rows for o in order], shard_rows)
    normed_ffn = jnp.concatenate(ctx_gather(own_nffn), axis=0)
    gate_up = dot(normed_ffn, full_gate_up)
    gate_proj, up_proj = gate_up[:, :units], gate_up[:, units:]
    activated, gelu_pull = jax.vjp(lambda inner: jax.nn.gelu(inner, approximate=True), gate_proj)
    mixed_units = (activated * up_proj).astype(bf16)

    def by_shard(a):
        blocked = a.reshape(shards, -1, a.shape[-1])
        size = blocked.shape[1]
        mine = take_blocks(a, 0, [o * size for o in order[:chips]], size)
        other = take_blocks(a, 0, [o * size for o in order[chips:]], size)
        return (
            mine.reshape(chips, size, -1),
            other.reshape(chips, size, -1),
        )

    grad_down = dot(mixed_units, all_dy, 0, 0).astype(bf16)
    share_down = weight_reduce(*by_shard(grad_down), chip)
    result = hidden + ctx_reduce(dot(mixed_units, full_down).astype(bf16), rows)
    grad_mixed = dot(all_dy, full_down, 1, 1)
    grad_gate_proj = gelu_pull(grad_mixed * up_proj)[0].astype(bf16)
    grad_up_proj = (grad_mixed * activated).astype(bf16)
    grad_gate_up = jnp.concatenate([grad_gate_proj, grad_up_proj], axis=1)
    grad_nffn = ctx_reduce(dot(grad_gate_up, full_gate_up, 1, 1).astype(bf16), rows)
    grad_nffn = take_blocks(grad_nffn, 1, [p * shard_rows for p in place], shard_rows)
    grad_w = dot(normed_ffn, grad_gate_up, 0, 0).astype(bf16).reshape(2, chips, shard_rows, -1)
    share_gate_up = weight_reduce(grad_w[0], grad_w[1], chip)
    grad_hidden_norm, grad_gain_ffn = norm_back(hidden, scale_ffn, gain_ffn, grad_nffn)
    grad_hidden = cotangent[0].astype(f32) * live_rows + grad_hidden_norm

    grad_low = jnp.concatenate(ctx_gather(grad_hidden.astype(bf16)), axis=0)
    grad_att = dot(grad_low, full_out, 1, 1).astype(bf16)
    grad_qkv, diagonals = attention_backward(scal, qkv, probs, grad_att, rows, blocks)
    grad_out = dot(attended, grad_low, 0, 0).astype(bf16)
    if strided:
        share_out = weight_reduce(*by_shard(grad_out), chip)
    grad_w = dot(normed, grad_qkv, 0, 0).astype(bf16).reshape(2, chips, shard_rows, -1)
    share_qkv = weight_reduce(grad_w[0], grad_w[1], chip)
    grad_normed = ctx_reduce(dot(grad_qkv, full_qkv, 1, 1).astype(bf16), rows)
    grad_norm, grad_gain_attn = norm_back(
        own_x.astype(f32), scale_all[:rows], gain_local, grad_normed
    )
    grad_norm = take_blocks(grad_norm, 1, [p * shard_rows for p in place], shard_rows)
    input_grad = (grad_hidden + grad_norm).astype(bf16)[None]

    grad_gain_attn = take_blocks(
        grad_gain_attn[None], 1, [p * shard_rows for p in place], shard_rows
    )[0]
    aligned = jnp.arange(2 * tokens, dtype=jnp.int32)
    aligned = jnp.where(aligned < 2 * tokens - rows, aligned, aligned - 2 * tokens)
    aligned = aligned - (blocks - 1) * rows
    of_aligned = (buckets_of(aligned)[:, None] == bucket_ids[None, :]).astype(f32)
    my_grad_table = jnp.dot(
        diagonals.reshape(my_heads, 2 * tokens), of_aligned, precision=lax.Precision.HIGHEST
    )
    grad_table = jnp.einsum(
        "gb,hg->bh",
        my_grad_table,
        (jnp.arange(heads, dtype=jnp.int32)[:, None] == my_head_ids[None, :]).astype(f32),
        precision=lax.Precision.HIGHEST,
    )
    packed = jnp.concatenate([grad_gain_attn, grad_gain_ffn, grad_table.reshape(-1)])
    packed = lax.psum(packed, ("ctx", "fsdp"))
    g_attn = lax.dynamic_slice_in_dim(packed, shard * shard_rows, shard_rows)
    g_ffn = lax.dynamic_slice_in_dim(packed, width + shard * shard_rows, shard_rows)
    table_rows = relative_bias_table.shape[0]
    g_table = lax.dynamic_slice_in_dim(
        packed[2 * width :].reshape(bucket_total, heads), shard * table_rows, table_rows, 0
    )

    def by_position(share):
        pieces = jnp.stack(ctx_gather(share))
        return jnp.concatenate(
            [lax.dynamic_slice_in_dim(pieces, position ^ c, 1, 0) for c in range(blocks)]
        )

    def spread(pieces, groups):
        n, r, _ = pieces.shape
        return jnp.transpose(pieces.reshape(n, r, groups, -1), (1, 2, 0, 3)).reshape(r, -1).astype(f32)

    qkv_pieces = by_position(share_qkv).reshape(blocks, shard_rows, pairs, 3, 128)
    head_groups = shards if strided else 1
    outs_qkv = [
        spread(qkv_pieces[:, :, :, n].reshape(blocks, shard_rows, -1), head_groups) for n in range(3)
    ]
    if strided:
        g_out = by_position(share_out).reshape(-1, width).astype(f32)
    else:
        spot = jnp.zeros((width, width), bf16)
        spot = lax.dynamic_update_slice_in_dim(
            spot, grad_out, position * my_heads * head_width, 0
        )
        g_out = lax.psum_scatter(spot, "fsdp", scatter_dimension=0, tiled=True)
        g_out = lax.psum(g_out, "ctx").astype(f32)
    gate_up_pieces = by_position(share_gate_up)
    g_gate = spread(gate_up_pieces[:, :, :units], shards)
    g_up = spread(gate_up_pieces[:, :, units:], shards)
    g_down = by_position(share_down).reshape(-1, width).astype(f32)
    return (
        result.astype(bf16)[None],
        input_grad,
        *outs_qkv,
        g_out,
        g_gate,
        g_up,
        g_down,
        g_attn,
        g_ffn,
        g_table,
    )


def solution(mesh):
    rows = P("fsdp", None)
    tokens = P("fsdp", "ctx", None)
    in_specs = (tokens, P("fsdp")) + (rows,) * 7 + (P("fsdp"), P("fsdp"), rows, tokens)
    out_specs = (tokens, tokens) + (rows,) * 7 + (P("fsdp"), P("fsdp"), rows)
    return jax.shard_map(
        on_device, mesh=mesh, in_specs=in_specs, out_specs=out_specs, check_vma=False
    )
```

```python
import functools

import jax
import jax.numpy as jnp
import numpy as np
from jax import lax
from jax.experimental import pallas as pl
from jax.experimental.pallas import tpu as pltpu
from jax.sharding import PartitionSpec as P

bucket_total = 32
bucket_total = 32
bucket_edges = (12, 16, 23, 32, 46, 64, 91)
epsilon = 1e-06
masked_score = -1e30
f32 = jnp.float32
bf16 = jnp.bfloat16
i32 = jnp.int32
vmem_limit = 52 * 1024 * 1024
extra = 16
ANY = pl.ANY


def dot(a, b, ca=1, cb=0):
    return lax.dot_general(a, b, (((ca,), (cb,)), ((), ())), preferred_element_type=f32)


def buckets_of(offset):
    distance = jnp.abs(offset)
    bucket = jnp.minimum(distance, 8)
    for edge_value in bucket_edges:
        bucket = bucket + (distance >= edge_value).astype(i32)
    return bucket + 16 * (offset > 0).astype(i32)


def after(value, *earlier):
    return lax.optimization_barrier((value, *earlier))[0]


def together(values, *earlier):
    return lax.optimization_barrier((*values, *earlier))[: len(values)]


def core_swap(a):
    size = lax.axis_size("fsdp")
    return lax.ppermute(a, "fsdp", [(r, r ^ 1) for r in range(size)])


def chip_send(a, pairs):
    return lax.ppermute(a, "fsdp", [(2 * s + k, 2 * d + k) for s, d in pairs for k in range(2)])


def ctx_send(a, distance):
    size = lax.axis_size("ctx")
    return lax.ppermute(a, "ctx", [(i, i ^ distance) for i in range(size)])


def near_slots(chips):
    return [0, 1, 3] if chips == 4 else list(range(chips))


def far_slots(chips):
    return [2] if chips == 4 else []


def gather_near(own):
    chips = lax.axis_size("fsdp") // 2
    if chips == 4:
        above = chip_send(own, [(1, 0), (2, 1), (3, 2), (0, 3)])
        below = chip_send(own, [(0, 1), (1, 2), (2, 3), (3, 0)])
        return [own, above, below]
    return [own] + [
        chip_send(own, [((z + t) % chips, z) for z in range(chips)]) for t in range(1, chips)
    ]


def gather_far(near, chip):
    if lax.axis_size("fsdp") // 2 != 4:
        return []
    own, above, below = near
    middle = jnp.where(chip == 1, above, jnp.where(chip == 2, below, own))
    return [chip_send(middle, [(3, 1), (0, 2), (1, 0), (2, 3)])]


def with_other_core(slots):
    if not slots:
        return []
    half = jnp.concatenate(slots, axis=0) if len(slots) > 1 else slots[0]
    return [half, core_swap(half)]


def add_low(a, b):
    return (a.astype(f32) + b.astype(f32)).astype(bf16)


def core_sum(mine, other):
    chips = lax.axis_size("fsdp") // 2
    swapped = core_swap(other)
    if chips != 4:
        return [add_low(mine, swapped)]
    near = mine.shape[0] // 4 * 3
    return [add_low(mine[near:], swapped[near:]), add_low(mine[:near], swapped[:near])]


def reduce_far(far):
    return chip_send(far, [(0, 1), (3, 2), (1, 3), (2, 0)])


def reduce_near(near, far, chip):
    chips = lax.axis_size("fsdp") // 2
    size = near.shape[0] // len(near_slots(chips))
    near = near.astype(f32)
    if chips == 4:
        far = far.astype(f32)
        zero = jnp.zeros((), f32)
        ends = near[:size] + jnp.where((chip == 0) | (chip == 3), far, zero)
        up = (near[size : 2 * size] + jnp.where(chip == 1, far, zero)).astype(bf16)
        down = (near[2 * size :] + jnp.where(chip == 2, far, zero)).astype(bf16)
        from_below = chip_send(up, [(0, 1), (1, 2), (2, 3), (3, 0)])
        from_above = chip_send(down, [(1, 0), (2, 1), (3, 2), (0, 3)])
        return (ends + from_below.astype(f32) + from_above.astype(f32)).astype(bf16)
    total = near[:size]
    for t in range(1, chips):
        part = near[t * size : (t + 1) * size].astype(bf16)
        total = total + chip_send(part, [(z, (z + t) % chips) for z in range(chips)]).astype(f32)
    return total.astype(bf16)


def ctx_gather(a):
    return [a] + [ctx_send(a, t) for t in range(1, lax.axis_size("ctx"))]


def ctx_exchange(parts):
    return [parts[0]] + [ctx_send(parts[t], t) for t in range(1, len(parts))]


smem = pl.BlockSpec(memory_space=pltpu.SMEM)


def whole(a):
    return pl.BlockSpec(a.shape, lambda *_: (0,) * len(a.shape))


def struct(shape, dtype):
    return jax.ShapeDtypeStruct(shape, dtype)


def call(kernel, grid, in_specs, out_specs, out_shape, args, scratch=(), flops=0, moved=None, exps=0):
    if moved is None:
        moved = sum(a.size * a.dtype.itemsize for a in args) + sum(
            int(np.prod(o.shape)) * jnp.dtype(o.dtype).itemsize for o in out_shape
        )
    return pl.pallas_call(
        kernel,
        grid=grid,
        in_specs=in_specs,
        out_specs=out_specs,
        out_shape=out_shape,
        scratch_shapes=scratch,
        compiler_params=pltpu.CompilerParams(vmem_limit_bytes=vmem_limit),
        cost_estimate=pl.CostEstimate(flops=flops, bytes_accessed=moved, transcendentals=exps),
    )(*args)


def shard_places(refs, stride):
    return [(ref, s * stride) for ref in refs for s in range(ref.shape[0] // stride)]


def tile_of(size, most):
    tile = most
    while size % tile:
        tile //= 2
    return tile


def start_and_wait(copies):
    for c in copies:
        c.start()
    for c in copies:
        c.wait()


def at_step(n):
    return pl.when(pl.program_id(0) == n)


def choose_attention_kernel(head_ids, head_width, with_out, scal, q, k, v, wo, na, nf, table, out):
    position = scal[0]
    rows = q.shape[0]
    wide = out.shape[1]
    for c, ids in enumerate(head_ids):

        @pl.when(position == c)
        def _():
            for n, ref in enumerate((q, k, v)):
                for pair in range(len(ids) // 2):
                    halves = [
                        ref[:, h * head_width : (h + 1) * head_width]
                        for h in ids[2 * pair : 2 * pair + 2]
                    ]
                    out[n * rows : (n + 1) * rows, pair * 128 : pair * 128 + 128] = (
                        jnp.concatenate(halves, axis=1)
                    )
            if with_out:
                blocks = len(head_ids)
                size = rows // blocks
                for b in range(blocks):
                    out[3 * rows + b * size : 3 * rows + (b + 1) * size, :] = wo[
                        c * size : (c + 1) * size, b * wide : (b + 1) * wide
                    ]

    row = lax.broadcasted_iota(i32, (extra, rows), 0)
    gains = jnp.where(row == 0, na[...].astype(f32), jnp.where(row == 1, nf[...].astype(f32), 0.0))
    buckets, heads = table.shape
    low = jnp.concatenate(
        [
            jnp.zeros((2, heads), f32),
            table[...].astype(f32),
            jnp.zeros((extra - 2 - buckets, heads), f32),
        ],
        axis=0,
    )
    low = jnp.concatenate([low, jnp.zeros((extra, rows - heads), f32)], axis=1)
    last = out.shape[0] - extra
    out[last:, :] = jnp.zeros((extra, wide), bf16)
    out[last:, :rows] = (gains + low).astype(bf16)


def choose_units_kernel(shards, scal, gate, up, out):
    position = scal[0]
    units = out.shape[1] // 2
    size = units // shards
    group = gate.shape[1] // shards
    for c in range(gate.shape[1] // units):

        @pl.when(position == c)
        def _():
            for n, ref in enumerate((gate, up)):
                out[:, n * units : (n + 1) * units] = jnp.concatenate(
                    [
                        ref[:, r * group + c * size : r * group + (c + 1) * size]
                        for r in range(shards)
                    ],
                    axis=1,
                )


def tokens_kernel(shards, scal, x, cotangent, out):
    rows, width = x.shape
    size = width // shards
    for l in range(shards):
        start = pl.multiple_of(scal[2 + l] * size, size)
        out[:rows, l * size : (l + 1) * size] = x[:, pl.ds(start, size)]
    row = lax.broadcasted_iota(i32, (rows, width), 0) + scal[0] * rows
    out[rows:, :] = jnp.where(row < scal[1], cotangent[...].astype(f32), 0.0).astype(bf16)


def head_choice(each, shards, position, my_heads, heads):
    h = lax.broadcasted_iota(i32, (my_heads, heads), 0)
    if each:
        shift = each.bit_length() - 1
        head_id = (h >> shift) * (heads // shards) + position * each + (h & (each - 1))
    else:
        head_id = position * my_heads + h
    return (lax.broadcasted_iota(i32, (my_heads, heads), 1) == head_id).astype(f32).astype(bf16)


def bucket_rows(scal, shards, offset):
    row = lax.broadcasted_iota(i32, (bucket_total, offset.shape[1]), 0)
    buckets = bucket_total // shards
    shift = buckets.bit_length() - 1
    bucket_id = jnp.zeros_like(row)
    for l in range(shards):
        bucket_id = jnp.where(
            (row >> shift) == l, scal[2 + l] * buckets + (row & (buckets - 1)), bucket_id
        )
    return (buckets_of(offset) == bucket_id).astype(f32).astype(bf16)


def qkv_kernel(blocks, parts, shards, each, scal, *refs):
    tokens_refs, weights = refs[:blocks], refs[blocks : blocks + parts]
    normed, qkv, bias, gains, scales, joined, small, sems, small_sems = refs[blocks + parts :]
    rows = tokens_refs[0].shape[0]
    tokens, width = normed.shape
    size = width // shards
    stride = sum(w.shape[0] for w in weights) // shards
    places = shard_places(weights, stride)
    step = pl.program_id(0)

    def copy(n, l):
        ref, at = places[l]
        return pltpu.make_async_copy(
            ref.at[pl.ds(at + n * size, size), :],
            joined.at[n, pl.ds(l * size, size), :],
            sems.at[n, l],
        )

    def small_copy(l):
        ref, at = places[l]
        return pltpu.make_async_copy(
            ref.at[pl.ds(at + stride - extra, extra), :], small.at[l], small_sems.at[l]
        )

    @at_step(0)
    def _():
        for l in range(shards):
            small_copy(l).start()
        for n in range(3):
            for l in range(shards):
                copy(n, l).start()
        for l in range(shards):
            small_copy(l).wait()
        my_heads = 2 * bias.shape[0]
        heads = my_heads * blocks
        buckets = bucket_total // shards
        tables = []
        for l in range(shards):
            value = small[l, :, :size].astype(f32)
            gains[:, l * size : (l + 1) * size] = value[:2]
            tables.append(value[2 : 2 + buckets, :heads])
        table = jnp.concatenate(tables, axis=0).astype(bf16)
        chosen = head_choice(each, shards, scal[0], my_heads, heads)
        mine = dot(chosen, table, 1, 1).astype(bf16)
        offset = tokens - lax.broadcasted_iota(i32, (1, 2 * tokens), 1)
        value = dot(mine, bucket_rows(scal, shards, offset))
        for pair in range(bias.shape[0]):
            bias[pair] = value[2 * pair : 2 * pair + 2]
        for t in range(blocks):
            at = slice(t * rows, (t + 1) * rows)
            x = tokens_refs[t][...].astype(f32)
            scale = lax.rsqrt(jnp.mean(x * x, axis=1, keepdims=True) + epsilon)
            normed[at, :] = (x * scale * gains[0:1, :]).astype(bf16)
            scales[at, :] = jnp.broadcast_to(scale, (rows, 128))

    for n in range(3):

        @at_step(n)
        def _():
            for l in range(shards):
                copy(n, l).wait()

    qkv[...] = dot(normed[...], joined[step]).astype(bf16)


def project(scal, tokens_all, weights, shards, each, pairs):
    rows, width = tokens_all[0].shape[0] // 2, tokens_all[0].shape[1]
    blocks = len(tokens_all)
    tokens = rows * blocks
    wide = 128 * pairs
    return call(
        functools.partial(qkv_kernel, blocks, len(weights), shards, each),
        (3,),
        [smem]
        + [pl.BlockSpec((rows, width), lambda n: (0, 0))] * blocks
        + [pl.BlockSpec(memory_space=ANY)] * len(weights),
        [
            pl.BlockSpec((tokens, width), lambda n: (0, 0)),
            pl.BlockSpec((tokens, wide), lambda n: (0, n)),
            pl.BlockSpec((pairs, 2, 2 * tokens), lambda n: (0, 0, 0)),
            pl.BlockSpec((2, width), lambda n: (0, 0)),
            pl.BlockSpec((tokens, 128), lambda n: (0, 0)),
        ],
        [
            struct((tokens, width), bf16),
            struct((tokens, 3 * wide), bf16),
            struct((pairs, 2, 2 * tokens), f32),
            struct((2, width), f32),
            struct((tokens, 128), f32),
        ],
        (scal, *tokens_all, *weights),
        [
            pltpu.VMEM((3, width, wide), bf16),
            pltpu.VMEM((shards, extra, wide), bf16),
            pltpu.SemaphoreType.DMA((3, shards)),
            pltpu.SemaphoreType.DMA((shards,)),
        ],
        flops=6 * tokens * width * wide,
    )


def lanes_of(position, blocks, rows, query, key):
    start = (blocks - 1 + (position ^ query) - (position ^ key)) * rows
    return pl.ds(pl.multiple_of(start, rows), rows)


def forward_kernel(rows, blocks, scal, q_ref, k_ref, v_ref, bias_ref, att, prob, toeplitz):
    position, length = scal[0], scal[1]
    width = 2 * blocks * rows
    slot = lax.broadcasted_iota(i32, (rows, rows), 0)
    for j in range(2):
        row = jnp.broadcast_to(bias_ref[0, j : j + 1, :], (rows, width))
        toeplitz[j] = pltpu.roll(row, width - rows, 1, stride=1, stride_axis=0)
    values = [v_ref[:, 64 * j : 64 * j + 64].astype(f32).T.astype(bf16) for j in range(2)]
    for t in range(blocks):
        at = slice(t * rows, (t + 1) * rows)
        halves = []
        for j in range(2):
            q = q_ref[at, 64 * j : 64 * j + 64]
            k = k_ref[:, 64 * j : 64 * j + 64]
            scores = dot(k, q, 1, 1)
            pieces = []
            for s in range(blocks):
                piece = (
                    scores[s * rows : (s + 1) * rows]
                    + toeplitz[j, :, lanes_of(position, blocks, rows, t, s)]
                )
                live = slot + (position ^ s) * rows < length
                pieces.append(jnp.where(live, piece, masked_score))
            scores = jnp.concatenate(pieces, axis=0)
            top = jnp.max(scores, axis=0, keepdims=True)
            e = jnp.exp(scores - top)
            probs = (e * (1.0 / jnp.sum(e, axis=0, keepdims=True))).astype(bf16)
            prob[j, :, at] = probs
            halves.append(dot(values[j], probs))
        att[at, :] = jnp.concatenate(halves, axis=0).T.astype(bf16)


def backward_kernel(
    rows, blocks, scal, q_ref, k_ref, v_ref, prob, gatt, gq, gk, gv, diag_ref, fold, ds_all
):
    position = scal[0]
    width = 2 * blocks * rows
    grads = [[], [], []]
    for j in range(2):
        columns = slice(64 * j, 64 * j + 64)
        k, v = k_ref[:, columns], v_ref[:, columns]
        fold[...] = jnp.zeros_like(fold)
        for t in range(blocks):
            at = slice(t * rows, (t + 1) * rows)
            gp = dot(v, gatt[at, columns], 1, 1)
            p = prob[j, :, at].astype(f32)
            pg = p * gp
            delta = jnp.sum(pg, axis=0, keepdims=True)
            ds = (pg - p * delta).astype(bf16)
            ds_all[:, at] = ds
            ds = ds.astype(f32)
            for s in range(blocks):
                fold[:, lanes_of(position, blocks, rows, t, s)] += ds[s * rows : (s + 1) * rows]
        grads[0].append(dot(k.astype(f32).T.astype(bf16), ds_all[...]))
        grads[1].append(dot(ds_all[...], q_ref[:, columns]))
        grads[2].append(dot(prob[j], gatt[:, columns]))
        a = fold[...]
        half = rows // 2
        while half >= 8:
            a = a[:half] + pltpu.roll(a[half:], width - half, 1)
            half //= 2
        row = lax.broadcasted_iota(i32, a.shape, 0)
        for bit in (1, 2, 4):
            a = jnp.where((row & bit) != 0, pltpu.roll(a, width - bit, 1), a)
        diag_ref[0, j : j + 1, :] = jnp.sum(a, axis=0, keepdims=True)
    gq[...] = jnp.concatenate(grads[0], axis=0).T.astype(bf16)
    gk[...] = jnp.concatenate(grads[1], axis=1).astype(bf16)
    gv[...] = jnp.concatenate(grads[2], axis=1).astype(bf16)


def attention_forward(scal, qkv, bias, rows, blocks):
    tokens = rows * blocks
    pairs = bias.shape[0]
    return call(
        functools.partial(forward_kernel, rows, blocks),
        (pairs,),
        [smem]
        + [pl.BlockSpec((tokens, 128), lambda p, n=n: (0, n * pairs + p)) for n in range(3)]
        + [pl.BlockSpec((1, 2, 2 * tokens), lambda p: (p, 0, 0))],
        [
            pl.BlockSpec((tokens, 128), lambda p: (0, p)),
            pl.BlockSpec((2, tokens, tokens), lambda p: (p, 0, 0)),
        ],
        [struct((tokens, 128 * pairs), bf16), struct((2 * pairs, tokens, tokens), bf16)],
        (scal, qkv, qkv, qkv, bias),
        [pltpu.VMEM((2, rows, 2 * tokens), f32)],
        flops=8 * pairs * tokens * tokens * 64,
        exps=2 * pairs * tokens * tokens,
    )


def attention_backward(scal, qkv, probs, grad_att, rows, blocks):
    tokens = rows * blocks
    pairs = probs.shape[0] // 2
    block = pl.BlockSpec((tokens, 128), lambda p: (0, p))
    return call(
        functools.partial(backward_kernel, rows, blocks),
        (pairs,),
        [smem]
        + [pl.BlockSpec((tokens, 128), lambda p, n=n: (0, n * pairs + p)) for n in range(3)]
        + [pl.BlockSpec((2, tokens, tokens), lambda p: (p, 0, 0)), block],
        [block, block, block, pl.BlockSpec((1, 2, 2 * tokens), lambda p: (p, 0, 0))],
        [struct((tokens, 128 * pairs), bf16)] * 3 + [struct((pairs, 2, 2 * tokens), f32)],
        (scal, qkv, qkv, qkv, probs, grad_att),
        [pltpu.VMEM((rows, 2 * tokens), f32), pltpu.VMEM((tokens, tokens), bf16)],
        flops=16 * pairs * tokens * tokens * 64,
    )


def out_copies(shards, scal, weights, joined, sems):
    blocks, depth, _ = joined.shape
    size = depth // shards
    stride = sum(w.shape[0] for w in weights) // shards
    first = stride - extra - blocks * size
    copies = []
    for b in range(blocks):
        for l, (ref, at) in enumerate(shard_places(weights, stride)):
            start = pl.multiple_of(scal[2 + l] * size, size)
            copies.append(
                pltpu.make_async_copy(
                    ref.at[pl.ds(at + first + b * size, size), :],
                    joined.at[b, pl.ds(start, size), :],
                    sems.at[b, l],
                )
            )
    return copies


def out_kernel(blocks, parts, shards, scal, att, *refs):
    weights, outs, joined, sems = refs[:parts], refs[parts:-2], refs[-2], refs[-1]
    start_and_wait(out_copies(shards, scal, weights, joined, sems))
    rows = outs[0].shape[0]
    wide = joined.shape[2]
    for b in range(joined.shape[0]):
        total = dot(att[...], joined[b]).astype(bf16)
        for t in range(blocks):
            outs[t][:, b * wide : (b + 1) * wide] = total[t * rows : (t + 1) * rows]


def multiply_out(scal, att, weights, shards, blocks):
    tokens, wide = att.shape
    rows, width = tokens // blocks, wide * blocks
    return call(
        functools.partial(out_kernel, blocks, len(weights), shards),
        (1,),
        [smem, whole(att)] + [pl.BlockSpec(memory_space=ANY)] * len(weights),
        [pl.BlockSpec((rows, width), lambda i: (0, 0))] * blocks,
        [struct((rows, width), bf16)] * blocks,
        (scal, att, *weights),
        [pltpu.VMEM((blocks, wide, wide), bf16), pltpu.SemaphoreType.DMA((blocks, shards))],
        flops=2 * tokens * wide * width,
    )


def grad_attended_kernel(blocks, parts, shards, scal, *refs):
    low, weights = refs[:blocks], refs[blocks : blocks + parts]
    out, joined, sems = refs[blocks + parts :]
    start_and_wait(out_copies(shards, scal, weights, joined, sems))
    wide = joined.shape[2]
    for t, ref in enumerate(low):
        rows = ref.shape[0]
        total = None
        for b in range(joined.shape[0]):
            term = dot(ref[:, b * wide : (b + 1) * wide], joined[b], 1, 1)
            total = term if total is None else total + term
        out[t * rows : (t + 1) * rows, :] = total.astype(bf16)


def make_grad_attended(scal, low_all, weights, shards):
    blocks = len(low_all)
    rows, width = low_all[0].shape
    tokens, wide = rows * blocks, width // blocks
    return call(
        functools.partial(grad_attended_kernel, blocks, len(weights), shards),
        (1,),
        [smem] + [whole(a) for a in low_all] + [pl.BlockSpec(memory_space=ANY)] * len(weights),
        [pl.BlockSpec((tokens, wide), lambda i: (0, 0))],
        [struct((tokens, wide), bf16)],
        (scal, *low_all, *weights),
        [pltpu.VMEM((blocks, wide, wide), bf16), pltpu.SemaphoreType.DMA((blocks, shards))],
        flops=2 * tokens * wide * width,
    )[0]


def hidden_kernel(blocks, shards, scal, x, gains, *refs):
    parts, hidden, nffn = refs[:blocks], refs[blocks], refs[blocks + 1]
    total = x[...].astype(f32)
    for part in parts:
        total = total + part[...].astype(f32)
    hidden[...] = total
    scale = lax.rsqrt(jnp.mean(total * total, axis=1, keepdims=True) + epsilon)
    size = total.shape[1] // shards
    for l in range(shards):
        at = slice(l * size, (l + 1) * size)
        start = pl.multiple_of(scal[2 + l] * size, size)
        nffn[:, at] = (hidden[:, pl.ds(start, size)] * scale * gains[1:2, at]).astype(bf16)


def make_hidden(scal, x, gains, parts, shards):
    rows, width = x.shape
    args = (scal, x, gains, *parts)
    return call(
        functools.partial(hidden_kernel, len(parts), shards),
        (1,),
        [smem] + [whole(a) for a in args[1:]],
        [pl.BlockSpec((rows, width), lambda i: (0, 0))] * 2,
        [struct((rows, width), f32), struct((rows, width), bf16)],
        args,
    )


def gelu_tanh(g):
    return jnp.tanh(0.7978845608028654 * (g + 0.044715 * (g * g * g)))


def units_kernel(blocks, parts, tile, *refs):
    tokens_refs, weights = refs[:blocks], refs[blocks : blocks + parts]
    normed, gate, up, mixed, joined, sems = refs[blocks + parts :]
    rows = tokens_refs[0].shape[0]
    units = weights[0].shape[1] // 2
    step = pl.program_id(0)

    def copies(i):
        result, at = [], 0
        for w, ref in enumerate(weights):
            for n in range(2):
                result.append(
                    pltpu.make_async_copy(
                        ref.at[:, pl.ds(n * units + i * tile, tile)],
                        joined.at[i, pl.ds(at, ref.shape[0]), pl.ds(n * tile, tile)],
                        sems.at[i, 2 * w + n],
                    )
                )
            at += ref.shape[0]
        return result

    @at_step(0)
    def _():
        for i in range(units // tile):
            for c in copies(i):
                c.start()
        for t in range(blocks):
            normed[t * rows : (t + 1) * rows, :] = tokens_refs[t][...]

    for i in range(units // tile):

        @at_step(i)
        def _():
            for c in copies(i):
                c.wait()

    both = dot(normed[...], joined[step])
    g, u = both[:, :tile], both[:, tile:]
    gate[...] = g
    up[...] = u
    mixed[...] = (0.5 * g * (1.0 + gelu_tanh(g)) * u).astype(bf16)


def make_units(tokens_all, weights):
    rows, width = tokens_all[0].shape
    blocks = len(tokens_all)
    tokens = rows * blocks
    units = weights[0].shape[1] // 2
    tile = tile_of(units, 256)
    steps = units // tile
    out = pl.BlockSpec((tokens, tile), lambda i: (0, i))
    return call(
        functools.partial(units_kernel, blocks, len(weights), tile),
        (steps,),
        [whole(a) for a in tokens_all] + [pl.BlockSpec(memory_space=ANY)] * len(weights),
        [pl.BlockSpec((tokens, width), lambda i: (0, 0)), out, out, out],
        [
            struct((tokens, width), bf16),
            struct((tokens, units), f32),
            struct((tokens, units), f32),
            struct((tokens, units), bf16),
        ],
        (*tokens_all, *weights),
        [
            pltpu.VMEM((steps, width, 2 * tile), bf16),
            pltpu.SemaphoreType.DMA((steps, 2 * len(weights))),
        ],
        flops=4 * tokens * width * units,
    )


def grad_down_kernel(blocks, shards, scal, mixed, *refs):
    dy, outs, turned, low = refs[:blocks], refs[blocks:-2], refs[-2], refs[-1]

    @at_step(0)
    def _():
        turned[...] = mixed[...].T

    low[...] = dot(turned[...], jnp.concatenate([r[...] for r in dy], axis=0)).astype(bf16)
    size = low.shape[0] // shards
    each = shards // len(outs)
    for l in range(shards):
        start = pl.multiple_of(scal[2 + l] * size, size)
        outs[side_of(shards)[l][0]][pl.ds(side_of(shards)[l][1] * size, size), :] = low[
            pl.ds(start, size), :
        ]


def side_of(shards):
    chips = shards // 2
    sides, counts = [], [0, 0]
    for slots in (near_slots(chips), far_slots(chips)):
        for p in range(2):
            for _ in slots:
                sides.append((p, counts[p]))
                counts[p] += 1
    return sides


def make_grad_down(scal, mixed, tokens_all, shards):
    blocks = len(tokens_all)
    tokens, units = mixed.shape
    rows, width = tokens // blocks, tokens_all[0].shape[1]
    tile = tile_of(width, 512)
    return call(
        functools.partial(grad_down_kernel, blocks, shards),
        (width // tile,),
        [smem, whole(mixed)] + [pl.BlockSpec((rows, tile), lambda i: (1, i))] * blocks,
        [pl.BlockSpec((units // 2, tile), lambda i: (0, i))] * 2,
        [struct((units // 2, width), bf16)] * 2,
        (scal, mixed, *tokens_all),
        [pltpu.VMEM((units, tokens), bf16), pltpu.VMEM((units, tile), bf16)],
        flops=2 * tokens * units * width,
    )


def down_copies(shards, scal, weights, joined, sems):
    size = joined.shape[0] // shards
    copies = []
    for l, (ref, at) in enumerate(shard_places(weights, size)):
        start = pl.multiple_of(scal[2 + l] * size, size) if shards > 1 else 0
        copies.append(
            pltpu.make_async_copy(
                ref.at[pl.ds(at, size), :], joined.at[pl.ds(start, size), :], sems.at[l]
            )
        )
    return copies


def units_back_kernel(blocks, parts, shards, tile, scal, gate, up, *refs):
    dy, weights = refs[:blocks], refs[blocks : blocks + parts]
    out, joined, grads, sems = refs[blocks + parts :]
    step = pl.program_id(0)
    rows = dy[0].shape[0]
    units = joined.shape[0]

    @at_step(0)
    def _():
        copies = down_copies(shards, scal, weights, joined, sems)
        for c in copies:
            c.start()
        for t in range(blocks):
            grads[t * rows : (t + 1) * rows, :] = dy[t][...]
        for c in copies:
            c.wait()

    weight = joined[pl.ds(pl.multiple_of(step * tile, tile), tile), :]
    grad = dot(grads[...], weight, 1, 1)
    g, u = gate[...], up[...]
    t = gelu_tanh(g)
    slope = 0.5 * (1.0 + t) + 0.5 * g * (1.0 - t * t) * (
        0.7978845608028654 * (1.0 + 3 * 0.044715 * (g * g))
    )
    out[:, pl.ds(pl.multiple_of(step * tile, tile), tile)] = (grad * u * slope).astype(bf16)
    out[:, pl.ds(pl.multiple_of(units + step * tile, tile), tile)] = (
        grad * (0.5 * g * (1.0 + t))
    ).astype(bf16)


def units_back(scal, gate, up, tokens_all, weights, shards):
    blocks = len(tokens_all)
    tokens, units = gate.shape
    rows, width = tokens // blocks, tokens_all[0].shape[1]
    tile = tile_of(units, 256)
    block = pl.BlockSpec((tokens, tile), lambda i: (0, i))
    return call(
        functools.partial(units_back_kernel, blocks, len(weights), shards, tile),
        (units // tile,),
        [smem, block, block]
        + [pl.BlockSpec((rows, width), lambda i: (1, 0))] * blocks
        + [pl.BlockSpec(memory_space=ANY)] * len(weights),
        [pl.BlockSpec((tokens, 2 * units), lambda i: (0, 0))],
        [struct((tokens, 2 * units), bf16)],
        (scal, gate, up, *tokens_all, *weights),
        [
            pltpu.VMEM((units, width), bf16),
            pltpu.VMEM((tokens, width), bf16),
            pltpu.SemaphoreType.DMA((shards,)),
        ],
        flops=2 * tokens * units * width,
    )[0]


def result_kernel(blocks, parts, shards, tile, scal, mixed, *refs):
    weights, outs, joined, sems = refs[:parts], refs[parts:-2], refs[-2], refs[-1]
    start_and_wait(down_copies(shards, scal, weights, joined, sems))
    rows, width = outs[0].shape
    for i in range(width // tile):
        at = slice(i * tile, (i + 1) * tile)
        total = dot(mixed[...], joined[:, at]).astype(bf16)
        for t in range(blocks):
            outs[t][:, at] = total[t * rows : (t + 1) * rows]


def multiply_down(scal, mixed, weights, shards, blocks):
    tokens, units = mixed.shape
    width = weights[0].shape[1]
    rows = tokens // blocks
    return call(
        functools.partial(result_kernel, blocks, len(weights), shards, tile_of(width, 512)),
        (1,),
        [smem, whole(mixed)] + [pl.BlockSpec(memory_space=ANY)] * len(weights),
        [pl.BlockSpec((rows, width), lambda i: (0, 0))] * blocks,
        [struct((rows, width), bf16)] * blocks,
        (scal, mixed, *weights),
        [pltpu.VMEM((units, width), bf16), pltpu.SemaphoreType.DMA((shards,))],
        flops=2 * tokens * units * width,
    )


def shard_specs(weights, rows):
    specs, ranges, first = [], [], 0
    for w in weights:
        count = w.shape[0] // rows
        specs.append(
            pl.BlockSpec(
                (rows, w.shape[1]), lambda l, f=first, n=count: (jnp.clip(l - f, 0, n - 1), 0)
            )
        )
        ranges.append((first, first + count))
        first += count
    return specs, ranges


def within(bounds):
    l = pl.program_id(0)
    return pl.when((l >= bounds[0]) & (l < bounds[1]))


def ffn_transposed_kernel(ranges, g, *refs):
    weights, outs = refs[: len(ranges)], refs[len(ranges) :]
    rows = outs[0].shape[0]
    for ref, bounds in zip(weights, ranges):

        @within(bounds)
        def _():
            total = dot(g[...], ref[...], 1, 1).astype(bf16)
            for t, out in enumerate(outs):
                out[...] = total[t * rows : (t + 1) * rows]


def ffn_transposed(g, weights, size, shards, blocks):
    tokens, depth = g.shape
    rows, width = tokens // blocks, size * shards
    specs, ranges = shard_specs(weights, size)
    return call(
        functools.partial(ffn_transposed_kernel, ranges),
        (shards,),
        [whole(g)] + specs,
        [pl.BlockSpec((rows, size), lambda l: (0, l))] * blocks,
        [struct((rows, width), bf16)] * blocks,
        (g, *weights),
        flops=2 * tokens * depth * width,
    )


def units_grad_kernel(shards, normed, g, *refs):
    outs, turned = refs[:-1], refs[-1]

    @at_step(0)
    def _():
        turned[...] = normed[...].T

    total = dot(turned[...], g[...]).astype(bf16)
    at = 0
    for out in outs:
        n = out.shape[0]
        out[...] = total[at : at + n]
        at += n


def units_grad(normed, g, shards):
    tokens, depth = normed.shape
    width = g.shape[1]
    tile = tile_of(width, 512)
    sizes = []
    for slots in (near_slots(shards // 2), far_slots(shards // 2)):
        if slots:
            sizes += [len(slots) * (depth // shards)] * 2
    return call(
        functools.partial(units_grad_kernel, shards),
        (width // tile,),
        [whole(normed), pl.BlockSpec((tokens, tile), lambda i: (0, i))],
        [pl.BlockSpec((n, tile), lambda i: (0, i)) for n in sizes],
        [struct((n, width), bf16) for n in sizes],
        (normed, g),
        [pltpu.VMEM((depth, tokens), bf16)],
        flops=2 * tokens * depth * width,
    )


def attn_transposed_kernel(blocks, ranges, size, scales, gq, gk, gv, *refs):
    tokens_refs, weights = refs[:blocks], refs[blocks : blocks + len(ranges)]
    outs, gain = refs[blocks + len(ranges) : -1], refs[-1]
    rows = outs[0].shape[0]
    for ref, bounds in zip(weights, ranges):

        @within(bounds)
        def _():
            total = None
            for n, g in enumerate((gq, gk, gv)):
                term = dot(g[...], ref[n * size : (n + 1) * size, :], 1, 1)
                total = term if total is None else total + term
            summed = jnp.zeros((1, size), f32)
            for t, out in enumerate(outs):
                at = slice(t * rows, (t + 1) * rows)
                out[...] = total[at].astype(bf16)
                unit = tokens_refs[t][...].astype(f32) * scales[at, 0:1]
                summed = summed + jnp.sum(total[at] * unit, axis=0, keepdims=True)
            gain[...] = summed


def attn_transposed(scales, grads, tokens_all, weights, size, shards, blocks):
    tokens, wide = grads[0].shape
    rows, width = tokens // blocks, size * shards
    stride = sum(w.shape[0] for w in weights) // shards
    specs, ranges = shard_specs(weights, stride)
    tile = pl.BlockSpec((rows, size), lambda l: (0, l))
    results = call(
        functools.partial(attn_transposed_kernel, blocks, ranges, size),
        (shards,),
        [whole(scales)] + [whole(g) for g in grads] + [tile] * blocks + specs,
        [tile] * blocks + [pl.BlockSpec((1, size), lambda l: (0, l))],
        [struct((rows, width), bf16)] * blocks + [struct((1, width), f32)],
        (scales, *grads, *tokens_all, *weights),
        flops=6 * tokens * wide * width,
    )
    return results[:-1], results[-1]


def split_low(a):
    high = a.astype(bf16)
    return high, (a - high.astype(f32)).astype(bf16)


def attn_grad_kernel(
    blocks, shards, each, with_out, scal, normed, att, gq, gk, gv, diag, gain_attn, gain_ffn, *refs
):
    low = refs[:blocks]
    mine, other, joined, turned, table = refs[blocks:]
    tokens, width = normed.shape
    wide = att.shape[1]
    size = width // shards
    head_rows = wide // shards
    rows = tokens // blocks
    my_heads = 2 * diag.shape[0]
    heads = my_heads * blocks

    @at_step(0)
    def _():
        for n, g in enumerate((gq, gk, gv)):
            joined[:, n * wide : (n + 1) * wide] = g[...]
        if with_out:
            turned[...] = dot(
                att[...].T, jnp.concatenate([r[...] for r in low], axis=0)
            ).astype(bf16)
        lane = lax.broadcasted_iota(i32, (1, 2 * tokens), 1)
        lane = jnp.where(lane < 2 * tokens - rows, lane, lane - 2 * tokens)
        of_offset = bucket_rows(scal, shards, (blocks - 1) * rows - lane)
        sums = jnp.concatenate([diag[p] for p in range(diag.shape[0])], axis=0)
        total = None
        for part in split_low(sums):
            term = dot(of_offset, part, 1, 1)
            total = term if total is None else total + term
        chosen = head_choice(each, shards, scal[0], my_heads, heads)
        value = None
        for part in split_low(total):
            term = dot(part, chosen)
            value = term if value is None else value + term
        table[...] = value

    buckets = bucket_total // shards
    for l, (side, at) in enumerate(side_of(shards)):

        @at_step(l)
        def _():
            out = other if side else mine
            total = dot(normed[:, l * size : (l + 1) * size], joined[...], 0, 0).astype(bf16)
            for n in range(3):
                out[n * size : (n + 1) * size, :] = total[:, n * wide : (n + 1) * wide]
            if with_out:
                start = pl.multiple_of(scal[2 + l] * head_rows, head_rows)
                for b in range(blocks):
                    out[3 * size + b * head_rows : 3 * size + (b + 1) * head_rows, :] = turned[
                        pl.ds(start, head_rows), b * wide : (b + 1) * wide
                    ]
            part = jnp.concatenate(
                [
                    jnp.zeros((2, heads), f32),
                    table[l * buckets : (l + 1) * buckets, :],
                    jnp.zeros((extra - 2 - buckets, heads), f32),
                ],
                axis=0,
            )
            part = jnp.concatenate([part, jnp.zeros((extra, size - heads), f32)], axis=1)
            row = lax.broadcasted_iota(i32, (extra, size), 0)
            columns = slice(l * size, (l + 1) * size)
            part = part + jnp.where(
                row == 0,
                gain_attn[:, columns],
                jnp.where(row == 1, gain_ffn[:, columns], 0.0),
            )
            last = out.shape[0] - extra
            out[last:, :] = jnp.zeros((extra, wide), bf16)
            out[last:, :size] = part.astype(bf16)


def attn_grad(scal, normed, att, grads, diag, gain_attn, gain_ffn, low_all, shards, each, stride):
    tokens, width = normed.shape
    wide = att.shape[1]
    blocks = len(low_all)
    sides = side_of(shards)
    half = shards // 2

    def index(side):
        steps = [l for l in range(shards) if sides[l][0] == side]

        def at(l):
            place = 0
            for s in steps[1:]:
                place = place + (l >= s).astype(i32)
            return (place, 0)

        return at

    args = (scal, normed, att, *grads, diag, gain_attn, gain_ffn, *low_all)
    return call(
        functools.partial(attn_grad_kernel, blocks, shards, each, bool(each)),
        (shards,),
        [smem] + [whole(a) for a in args[1:]],
        [pl.BlockSpec((stride, wide), index(0)), pl.BlockSpec((stride, wide), index(1))],
        [struct((half * stride, wide), bf16)] * 2,
        args,
        [
            pltpu.VMEM((tokens, 3 * wide), bf16),
            pltpu.VMEM((wide, width), bf16),
            pltpu.VMEM((bucket_total, 2 * diag.shape[0] * blocks), f32),
        ],
        flops=8 * tokens * wide * width,
    )


def ffn_norm_back_kernel(blocks, shards, scal, hidden, gains, own, *refs):
    parts = refs[:blocks]
    grad_hidden, low, grad_gain, g, gain = refs[blocks:]
    size = hidden.shape[1] // shards
    for l in range(shards):
        at = slice(l * size, (l + 1) * size)
        start = pl.multiple_of(scal[2 + l] * size, size)
        total = parts[0][:, at].astype(f32)
        for part in parts[1:]:
            total = total + part[:, at].astype(f32)
        g[:, pl.ds(start, size)] = total
        gain[:, pl.ds(start, size)] = gains[1:2, at]
    h = hidden[...]
    scale = lax.rsqrt(jnp.mean(h * h, axis=1, keepdims=True) + epsilon)
    weighted = g[...] * gain[...]
    inner = jnp.mean(weighted * h, axis=1, keepdims=True)
    value = own[...].astype(f32) + scale * weighted - h * (scale * scale * scale) * inner
    grad_hidden[...] = value
    low[...] = value.astype(bf16)
    g[...] = g[...] * h * scale
    for l in range(shards):
        start = pl.multiple_of(scal[2 + l] * size, size)
        grad_gain[:, l * size : (l + 1) * size] = jnp.sum(
            g[:, pl.ds(start, size)], axis=0, keepdims=True
        )


def ffn_norm_back(scal, hidden, gains, own, parts, shards):
    rows, width = hidden.shape
    block = pl.BlockSpec((rows, width), lambda i: (0, 0))
    return call(
        functools.partial(ffn_norm_back_kernel, len(parts), shards),
        (1,),
        [smem, block, whole(gains), pl.BlockSpec((rows, width), lambda i: (1, 0))]
        + [block] * len(parts),
        [block, block, pl.BlockSpec((1, width), lambda i: (0, 0))],
        [struct((rows, width), f32), struct((rows, width), bf16), struct((1, width), f32)],
        (scal, hidden, gains, own, *parts),
        [pltpu.VMEM((rows, width), f32), pltpu.VMEM((1, width), f32)],
    )


def attn_norm_back_kernel(blocks, shards, scal, grad_hidden, gains, own, *refs):
    parts = refs[:blocks]
    grad, value = refs[blocks:]
    x = own[...].astype(f32)
    g = parts[0][...].astype(f32)
    for part in parts[1:]:
        g = g + part[...].astype(f32)
    scale = lax.rsqrt(jnp.mean(x * x, axis=1, keepdims=True) + epsilon)
    weighted = g * gains[0:1, :]
    inner = jnp.mean(weighted * x, axis=1, keepdims=True)
    value[...] = scale * weighted - x * (scale * scale * scale) * inner
    size = x.shape[1] // shards
    for l in range(shards):
        at = slice(l * size, (l + 1) * size)
        where = pl.ds(pl.multiple_of(scal[2 + l] * size, size), size)
        grad[:, where] = (grad_hidden[:, where] + value[:, at]).astype(bf16)


def attn_norm_back(scal, grad_hidden, gains, own, parts, shards):
    rows, width = grad_hidden.shape
    block = pl.BlockSpec((rows, width), lambda i: (0, 0))
    return call(
        functools.partial(attn_norm_back_kernel, len(parts), shards),
        (1,),
        [smem, block, whole(gains), block] + [block] * len(parts),
        [block],
        [struct((rows, width), bf16)],
        (scal, grad_hidden, gains, own, *parts),
        [pltpu.VMEM((rows, width), f32)],
    )[0]


def by_position(scal, blocks, body):
    for p in range(blocks):

        @pl.when(scal[0] == p)
        def _():
            body([p ^ c for c in range(blocks)])


def columns_kernel(groups, scal, *refs):
    pieces, outs = refs[:-2], refs[-2:]
    blocks = len(pieces)
    units = pieces[0].shape[1] // 2
    size = units // groups
    wide = blocks * size

    def body(order):
        for n, out in enumerate(outs):
            for g in range(groups):
                at = n * units + g * size
                out[:, g * wide : (g + 1) * wide] = jnp.concatenate(
                    [pieces[t][:, at : at + size] for t in order], axis=1
                ).astype(f32)

    by_position(scal, blocks, body)


def assemble_units(scal, pieces, groups):
    rows, columns = pieces[0].shape
    tile = min(rows, 32)
    wide = len(pieces) * columns // 2
    return call(
        functools.partial(columns_kernel, groups),
        (rows // tile,),
        [smem] + [pl.BlockSpec((tile, columns), lambda i: (i, 0))] * len(pieces),
        [pl.BlockSpec((tile, wide), lambda i: (i, 0))] * 2,
        [struct((rows, wide), f32)] * 2,
        (scal, *pieces),
    )


def rows_kernel(size, scal, *refs):
    position = scal[0]
    for t, piece in enumerate(refs[:-1]):
        start = pl.multiple_of((position ^ t) * size, 8)
        refs[-1][pl.ds(start, size), :] = piece[...].astype(f32)


def assemble_rows(scal, pieces):
    rows, columns = pieces[0].shape
    tile = tile_of(columns, 512)
    return call(
        functools.partial(rows_kernel, rows),
        (columns // tile,),
        [smem] + [pl.BlockSpec((rows, tile), lambda i: (0, i))] * len(pieces),
        [pl.BlockSpec((rows * len(pieces), tile), lambda i: (0, i))],
        [struct((rows * len(pieces), columns), f32)],
        (scal, *pieces),
    )[0]


def attention_outputs_kernel(each, groups, head_width, scal, *refs):
    blocks = groups
    columns = refs[: 3 * blocks]
    rest = refs[3 * blocks :]
    with_out = bool(each)
    out_blocks = rest[:blocks] if with_out else ()
    rest = rest[blocks:] if with_out else rest
    small, outs = rest[:blocks], rest[blocks:]
    wide = columns[0].shape[1]
    step = pl.program_id(0)

    def body(order):
        for n in range(3):
            pieces = [columns[3 * t + n] for t in order]
            if each:
                size = each * head_width
                for g in range(wide // size):
                    outs[n][:, g * blocks * size : (g + 1) * blocks * size] = jnp.concatenate(
                        [ref[:, g * size : (g + 1) * size] for ref in pieces], axis=1
                    ).astype(f32)
            else:
                for c, ref in enumerate(pieces):
                    outs[n][:, c * wide : (c + 1) * wide] = ref[...].astype(f32)

        @at_step(0)
        def _():
            total = small[order[0]][...].astype(f32)
            for t in order[1:]:
                total = total + small[t][...].astype(f32)
            outs[-1][...] = total

    by_position(scal, blocks, body)
    if with_out:
        for t in range(blocks):

            @pl.when((step ^ scal[0]) == t)
            def _():
                size = outs[3].shape[0]
                for b in range(blocks):
                    outs[3][:, b * wide : (b + 1) * wide] = out_blocks[t][
                        b * size : (b + 1) * size, :
                    ].astype(f32)


def attention_outputs(scal, pieces, rows, each, head_width):
    stride, wide = pieces[0].shape
    blocks = len(pieces)
    tile = rows // blocks
    width = wide * blocks
    per = rows // tile
    specs, args = [], []
    for a in pieces:
        for n in range(3):
            specs.append(pl.BlockSpec((tile, wide), lambda i, n=n: (n * per + i, 0)))
            args.append(a)
    if each:
        specs += [pl.BlockSpec((rows, wide), lambda i: (3, 0))] * blocks
        args += pieces
    specs += [pl.BlockSpec((extra, wide), lambda i: (stride // extra - 1, 0))] * blocks
    args += pieces
    block = pl.BlockSpec((tile, width), lambda i: (i, 0))
    count = 4 if each else 3
    return call(
        functools.partial(attention_outputs_kernel, each, blocks, head_width),
        (blocks,),
        [smem] + specs,
        [block] * count + [pl.BlockSpec((extra, wide), lambda i: (0, 0))],
        [struct((rows, width), f32)] * count + [struct((extra, wide), f32)],
        (scal, *args),
    )


def take_blocks(a, starts, size):
    return jnp.concatenate([lax.dynamic_slice_in_dim(a, s, size, 0) for s in starts], 0)


def on_device(
    inputs,
    lengths,
    w_query,
    w_key,
    w_value,
    w_out,
    w_gate,
    w_up,
    w_down,
    norm_attn,
    norm_ffn,
    relative_bias_table,
    cotangent,
):
    blocks = lax.axis_size("ctx")
    shards = lax.axis_size("fsdp")
    chips = shards // 2
    position = lax.axis_index("ctx")
    shard = lax.axis_index("fsdp")
    chip, core = shard // 2, shard % 2
    rows, width = inputs.shape[1], inputs.shape[2]
    tokens = rows * blocks
    heads = relative_bias_table.shape[1]
    head_width = width // heads
    my_heads = heads // blocks
    pairs = my_heads // 2
    each = heads // shards // blocks if (heads // shards) % blocks == 0 else 0
    strided = each in (1, 2)
    each = each if strided else 0
    units = w_gate.shape[1] // blocks
    shard_rows = width // shards
    unit_rows = w_down.shape[0] // blocks

    slot_of, parity_of = [], []
    for slots in (near_slots(chips), far_slots(chips)):
        for p in range(2):
            slot_of += slots
            parity_of += [p] * len(slots)
    pad = [0, 0]
    order = 2 * ((chip + jnp.array(pad + slot_of, i32)) % chips) + (
        core ^ jnp.array(pad + parity_of, i32)
    )
    index = jnp.arange(shards + 2, dtype=i32)
    scal = jnp.where(index == 0, position, jnp.where(index == 1, lengths[0], order)).astype(i32)

    def heads_of(c):
        if strided:
            return [
                (h // each) * (heads // shards) + c * each + h % each for h in range(my_heads)
            ]
        return [c * my_heads + h for h in range(my_heads)]

    own_tokens = call(
        functools.partial(tokens_kernel, shards),
        (1,),
        [smem] + [pl.BlockSpec((rows, width), lambda i: (0, 0))] * 2,
        [pl.BlockSpec((2 * rows, width), lambda i: (0, 0))],
        [struct((2 * rows, width), bf16)],
        (scal, inputs[0], cotangent[0]),
    )[0]
    all_tokens = ctx_gather(own_tokens)
    args = (
        after(scal, own_tokens),
        w_query,
        w_key,
        w_value,
        w_out,
        norm_attn.reshape(1, -1),
        norm_ffn.reshape(1, -1),
        relative_bias_table,
    )
    stride = (4 if strided else 3) * shard_rows + extra
    own_attn = call(
        functools.partial(
            choose_attention_kernel, [heads_of(c) for c in range(blocks)], head_width, strided
        ),
        (1,),
        [smem] + [whole(a) for a in args[1:]],
        [pl.BlockSpec((stride, 128 * pairs), lambda i: (0, 0))],
        [struct((stride, 128 * pairs), bf16)],
        args,
    )[0]
    near_attn = gather_near(own_attn)
    tile = tile_of(shard_rows, 64)
    own_gate_up = call(
        functools.partial(choose_units_kernel, shards),
        (shard_rows // tile,),
        [smem] + [pl.BlockSpec((tile, w_gate.shape[1]), lambda i: (i, 0))] * 2,
        [pl.BlockSpec((tile, 2 * units), lambda i: (i, 0))],
        [struct((shard_rows, 2 * units), bf16)],
        (after(scal, own_attn), w_gate, w_up),
    )[0]
    joint = together([*near_attn, *all_tokens], own_gate_up)
    near_attn, all_tokens = joint[: len(near_attn)], joint[len(near_attn) :]
    far_attn = gather_far(near_attn, chip)
    joint = together(with_other_core(near_attn) + far_attn)
    weights_attn, far_attn = list(joint[:2]), joint[2:]
    near_gate_up = gather_near(after(own_gate_up, *far_attn))
    weights_attn += with_other_core(far_attn)
    if not strided:
        gathered = lax.all_gather(w_out, "fsdp", axis=0, tiled=True)
        size = my_heads * head_width
        full_out = lax.dynamic_slice_in_dim(gathered, position * size, size, 0)

    normed, qkv, bias, gains, scales = project(
        scal, all_tokens, weights_attn, shards, each, pairs
    )
    attended, probs = attention_forward(scal, qkv, bias, rows, blocks)
    if strided:
        parts = multiply_out(scal, attended, weights_attn, shards, blocks)
    else:
        whole_part = dot(attended, full_out).astype(bf16)
        parts = [whole_part[t * rows : (t + 1) * rows] for t in range(blocks)]
    parts = ctx_exchange(parts)
    hidden, own_nffn = make_hidden(scal, inputs[0], gains, parts, shards)

    near_gate_up = together(near_gate_up, own_nffn)
    far_gate_up = gather_far(near_gate_up, chip)
    joint = together(with_other_core(near_gate_up) + ctx_gather(own_nffn) + far_gate_up)
    weights_gate_up = list(joint[:2])
    all_nffn, far_gate_up = joint[2 : 2 + blocks], joint[2 + blocks :]
    own_down = lax.dynamic_slice_in_dim(w_down, position * unit_rows, unit_rows, 0)
    near_down = gather_near(after(own_down, all_nffn[0]))
    weights_gate_up += with_other_core(far_gate_up)
    normed_ffn, gate, up, mixed_units = make_units(all_nffn, weights_gate_up)

    aligned = unit_rows % 16 == 0
    if aligned:
        grads_down = make_grad_down(scal, mixed_units, all_tokens, shards)
    else:
        all_dy = jnp.concatenate([a[rows:] for a in all_tokens], axis=0)
        grad_down = dot(mixed_units, all_dy, 0, 0).astype(bf16)
        grads_down = [
            take_blocks(
                grad_down,
                [order[2 + l] * unit_rows for l in range(shards) if parity_of[l] == side],
                unit_rows,
            )
            for side in range(2)
        ]
    sums_down = core_sum(*grads_down)
    near_down = together(near_down, *sums_down)
    far_down = gather_far(near_down, chip)
    joint = together(with_other_core(near_down) + far_down)
    down_parts, far_down = list(joint[:2]), joint[2:]
    down_parts, down_shards = down_parts + with_other_core(far_down), shards
    if not aligned:
        joined = jnp.concatenate(down_parts, axis=0)
        place = jnp.argsort(order[2:])
        down_parts = [take_blocks(joined, [place[r] * unit_rows for r in range(shards)], unit_rows)]
        down_shards = 1

    far_sum = None
    if len(sums_down) == 2:
        far_sum = reduce_far(after(sums_down[0], *far_down))
    grad_units = units_back(scal, gate, up, all_tokens, down_parts, down_shards)
    parts = ffn_transposed(grad_units, weights_gate_up, shard_rows, shards, blocks)
    if far_sum is not None:
        *parts, far_sum = together([*parts, far_sum])
    parts = list(parts)
    share_down = reduce_near(after(sums_down[-1], *parts), far_sum, chip)
    parts = ctx_exchange(parts)
    grads_gate_up = units_grad(normed_ffn, after(grad_units, parts[0]), shards)
    result_parts = multiply_down(
        scal, after(mixed_units, *grads_gate_up), down_parts, down_shards, blocks
    )
    parts = together(parts, *grads_gate_up, *result_parts)
    grad_hidden, low, grad_gain_ffn = ffn_norm_back(
        scal, hidden, gains, own_tokens, parts, shards
    )

    all_low = ctx_gather(low)
    far_sum = None
    if len(grads_gate_up) == 4:
        swapped = core_swap(after(grads_gate_up[3], share_down, low))
        far_sum = reduce_far(add_low(grads_gate_up[2], swapped))
        swapped = core_swap(after(grads_gate_up[1], swapped))
    else:
        swapped = core_swap(after(grads_gate_up[1], share_down, low))
    near_sum = add_low(grads_gate_up[0], swapped)
    joint = together([*all_low, near_sum])
    all_low, near_sum = joint[:-1], joint[-1]
    pieces_down = ctx_gather(after(share_down, *all_low))
    if strided:
        grad_att = make_grad_attended(scal, all_low, weights_attn, shards)
    else:
        grad_att = dot(jnp.concatenate(all_low, axis=0), full_out, 1, 1).astype(bf16)
    *grads, diagonals = attention_backward(scal, qkv, probs, grad_att, rows, blocks)
    parts, grad_gain_attn = attn_transposed(
        scales, grads, all_tokens, weights_attn, shard_rows, shards, blocks
    )
    joint = together([*parts, *pieces_down, near_sum] + ([] if far_sum is None else [far_sum]))
    parts, pieces_down = list(joint[:blocks]), joint[blocks : 2 * blocks]
    near_sum = joint[2 * blocks]
    far_sum = None if far_sum is None else joint[-1]
    share_gate_up = reduce_near(near_sum, far_sum, chip)
    parts = ctx_exchange(parts)
    grads_attn = attn_grad(
        scal,
        normed,
        attended,
        [after(grads[0], parts[0]), *grads[1:]],
        diagonals,
        grad_gain_attn,
        grad_gain_ffn,
        all_low,
        shards,
        each,
        stride,
    )
    parts = together(parts, *grads_attn)
    input_grad = attn_norm_back(scal, grad_hidden, gains, own_tokens, parts, shards)
    sums_attn = core_sum(grads_attn[0], after(grads_attn[1], input_grad))
    result_parts = ctx_exchange(together(result_parts, *sums_attn))
    result = hidden
    for part in result_parts:
        result = result + part.astype(f32)
    result = result.astype(bf16)
    share_gate_up, result = together([share_gate_up, result])
    far_sum = None
    if len(sums_attn) == 2:
        far_sum = reduce_far(after(sums_attn[0], share_gate_up))
    share_attn = reduce_near(after(sums_attn[-1], share_gate_up), far_sum, chip)
    joint = together([*ctx_gather(share_gate_up), share_attn])
    pieces_gate_up, share_attn = joint[:-1], joint[-1]
    pieces_attn = ctx_gather(share_attn)

    g_down = assemble_rows(scal, pieces_down)
    if blocks * unit_rows % 128 == 0:
        g_gate, g_up = assemble_units(scal, pieces_gate_up, shards)
    else:
        stacked = jnp.stack(pieces_gate_up)
        stacked = [
            lax.dynamic_slice_in_dim(stacked, position ^ c, 1, 0)[0] for c in range(blocks)
        ]
        g_gate, g_up = [
            jnp.concatenate(
                [
                    stacked[c][:, n * units + r * unit_rows : n * units + (r + 1) * unit_rows]
                    for r in range(shards)
                    for c in range(blocks)
                ],
                axis=1,
            ).astype(f32)
            for n in range(2)
        ]
    *outs_attn, small = attention_outputs(scal, pieces_attn, shard_rows, each, head_width)
    if not strided:
        spot = jnp.zeros((width, width), bf16)
        spot = lax.dynamic_update_slice_in_dim(
            spot,
            dot(attended, jnp.concatenate(all_low, axis=0), 0, 0).astype(bf16),
            position * my_heads * head_width,
            0,
        )
        g_out = lax.psum_scatter(spot, "fsdp", scatter_dimension=0, tiled=True)
        outs_attn.append(lax.psum(g_out, "ctx").astype(f32))
    buckets = relative_bias_table.shape[0]
    return (
        result[None],
        input_grad[None],
        *outs_attn,
        g_gate,
        g_up,
        g_down,
        small[0, :shard_rows],
        small[1, :shard_rows],
        small[2 : 2 + buckets, :heads],
    )


def solution(mesh):
    rows = P("fsdp", None)
    tokens = P("fsdp", "ctx", None)
    in_specs = (tokens, P("fsdp")) + (rows,) * 7 + (P("fsdp"), P("fsdp"), rows, tokens)
    out_specs = (tokens, tokens) + (rows,) * 7 + (P("fsdp"), P("fsdp"), rows)
    return jax.shard_map(
        on_device, mesh=mesh, in_specs=in_specs, out_specs=out_specs, check_vma=False
    )
```

```python
import functools

import jax
import jax.numpy as jnp
import numpy as np
from jax import lax
from jax.experimental import pallas as pl
from jax.experimental.pallas import tpu as pltpu
from jax.sharding import PartitionSpec as P

bucket_total = 32
bucket_total = 32
bucket_edges = (12, 16, 23, 32, 46, 64, 91)
epsilon = 1e-06
masked_score = -1e30
f32 = jnp.float32
bf16 = jnp.bfloat16
i32 = jnp.int32
vmem_limit = 52 * 1024 * 1024
extra = 16
ANY = pl.ANY


def dot(a, b, ca=1, cb=0):
    return lax.dot_general(a, b, (((ca,), (cb,)), ((), ())), preferred_element_type=f32)


def buckets_of(offset):
    distance = jnp.abs(offset)
    bucket = jnp.minimum(distance, 8)
    for edge_value in bucket_edges:
        bucket = bucket + (distance >= edge_value).astype(i32)
    return bucket + 16 * (offset > 0).astype(i32)


def after(value, *earlier):
    return lax.optimization_barrier((value, *earlier))[0]


def together(values, *earlier):
    return lax.optimization_barrier((*values, *earlier))[: len(values)]


def core_swap(a):
    size = lax.axis_size("fsdp")
    return lax.ppermute(a, "fsdp", [(r, r ^ 1) for r in range(size)])


def chip_send(a, pairs):
    return lax.ppermute(a, "fsdp", [(2 * s + k, 2 * d + k) for s, d in pairs for k in range(2)])


def ctx_send(a, distance):
    size = lax.axis_size("ctx")
    return lax.ppermute(a, "ctx", [(i, i ^ distance) for i in range(size)])


def near_slots(chips):
    return [0, 1, 3] if chips == 4 else list(range(chips))


def far_slots(chips):
    return [2] if chips == 4 else []


def gather_near(own):
    chips = lax.axis_size("fsdp") // 2
    if chips == 4:
        above = chip_send(own, [(1, 0), (2, 1), (3, 2), (0, 3)])
        below = chip_send(own, [(0, 1), (1, 2), (2, 3), (3, 0)])
        return [own, above, below]
    return [own] + [
        chip_send(own, [((z + t) % chips, z) for z in range(chips)]) for t in range(1, chips)
    ]


def gather_far(near, chip):
    if lax.axis_size("fsdp") // 2 != 4:
        return []
    own, above, below = near
    middle = jnp.where(chip == 1, above, jnp.where(chip == 2, below, own))
    return [chip_send(middle, [(3, 1), (0, 2), (1, 0), (2, 3)])]


def with_other_core(slots):
    if not slots:
        return []
    half = jnp.concatenate(slots, axis=0) if len(slots) > 1 else slots[0]
    return [half, core_swap(half)]


def add_low(a, b):
    return (a.astype(f32) + b.astype(f32)).astype(bf16)


def core_sum(mine, other):
    chips = lax.axis_size("fsdp") // 2
    swapped = core_swap(other)
    if chips != 4:
        return [add_low(mine, swapped)]
    near = mine.shape[0] // 4 * 3
    return [add_low(mine[near:], swapped[near:]), add_low(mine[:near], swapped[:near])]


def reduce_far(far):
    return chip_send(far, [(0, 1), (3, 2), (1, 3), (2, 0)])


def near_sends(near, far, chip, rows=None):
    chips = lax.axis_size("fsdp") // 2
    size = near.shape[0] // len(near_slots(chips))
    first, last = rows or (0, size)
    parts = [
        near[s * size + first : s * size + last].astype(f32) for s in range(len(near_slots(chips)))
    ]
    if chips == 4:
        far = far[first:last].astype(f32)
        zero = jnp.zeros((), f32)
        ends = parts[0] + jnp.where((chip == 0) | (chip == 3), far, zero)
        up = parts[1] + jnp.where(chip == 1, far, zero)
        down = parts[2] + jnp.where(chip == 2, far, zero)
        parts = [ends, up, down]
    return [parts[0]] + [p.astype(bf16) for p in parts[1:]]


def near_receive(sends):
    chips = lax.axis_size("fsdp") // 2
    if chips == 4:
        from_below = chip_send(sends[1], [(0, 1), (1, 2), (2, 3), (3, 0)])
        from_above = chip_send(sends[2], [(1, 0), (2, 1), (3, 2), (0, 3)])
        return [sends[0], from_below, from_above]
    return [sends[0]] + [
        chip_send(sends[t], [(z, (z + t) % chips) for z in range(chips)]) for t in range(1, chips)
    ]


def near_total(received):
    total = received[0]
    for part in received[1:]:
        total = total + part.astype(f32)
    return total.astype(bf16)


def ctx_gather(a):
    return [a] + [ctx_send(a, t) for t in range(1, lax.axis_size("ctx"))]


def ctx_gather_near(a):
    if lax.axis_size("ctx") == 4:
        return [ctx_send(a, 1), ctx_send(a, 2)]
    return ctx_gather(a)[1:]


def ctx_gather_far(near):
    if lax.axis_size("ctx") == 4:
        half = near[0].shape[0] // 2
        return [ctx_send(near[1][:half], 1), ctx_send(near[0][half:], 2)]
    return []


def ctx_pieces(own, near, far):
    return [own, *near] + ([jnp.concatenate(far, axis=0)] if far else [])


def ctx_exchange(parts):
    return [parts[0]] + [ctx_send(parts[t], t) for t in range(1, len(parts))]


smem = pl.BlockSpec(memory_space=pltpu.SMEM)


def whole(a):
    return pl.BlockSpec(a.shape, lambda *_: (0,) * len(a.shape))


def struct(shape, dtype):
    return jax.ShapeDtypeStruct(shape, dtype)


def call(kernel, grid, in_specs, out_specs, out_shape, args, scratch=(), flops=0, moved=None, exps=0):
    if moved is None:
        moved = sum(a.size * a.dtype.itemsize for a in args) + sum(
            int(np.prod(o.shape)) * jnp.dtype(o.dtype).itemsize for o in out_shape
        )
    return pl.pallas_call(
        kernel,
        grid=grid,
        in_specs=in_specs,
        out_specs=out_specs,
        out_shape=out_shape,
        scratch_shapes=scratch,
        compiler_params=pltpu.CompilerParams(vmem_limit_bytes=vmem_limit),
        cost_estimate=pl.CostEstimate(flops=1, bytes_accessed=1, transcendentals=0),
    )(*args)


def shard_places(refs, stride):
    return [(ref, s * stride) for ref in refs for s in range(ref.shape[0] // stride)]


def tile_of(size, most):
    tile = most
    while size % tile:
        tile //= 2
    return tile


def start_and_wait(copies):
    for c in copies:
        c.start()
    for c in copies:
        c.wait()


def at_step(n):
    return pl.when(pl.program_id(0) == n)


def choose_attention_kernel(head_ids, head_width, with_out, scal, q, k, v, wo, na, nf, table, out):
    position = scal[0]
    rows = q.shape[0]
    wide = out.shape[1]
    for c, ids in enumerate(head_ids):

        @pl.when(position == c)
        def _():
            for n, ref in enumerate((q, k, v)):
                for pair in range(len(ids) // 2):
                    halves = [
                        ref[:, h * head_width : (h + 1) * head_width]
                        for h in ids[2 * pair : 2 * pair + 2]
                    ]
                    out[n * rows : (n + 1) * rows, pair * 128 : pair * 128 + 128] = (
                        jnp.concatenate(halves, axis=1)
                    )
            if with_out:
                blocks = len(head_ids)
                size = rows // blocks
                for b in range(blocks):
                    out[3 * rows + b * size : 3 * rows + (b + 1) * size, :] = wo[
                        c * size : (c + 1) * size, b * wide : (b + 1) * wide
                    ]

    row = lax.broadcasted_iota(i32, (extra, rows), 0)
    gains = jnp.where(row == 0, na[...].astype(f32), jnp.where(row == 1, nf[...].astype(f32), 0.0))
    buckets, heads = table.shape
    low = jnp.concatenate(
        [
            jnp.zeros((2, heads), f32),
            table[...].astype(f32),
            jnp.zeros((extra - 2 - buckets, heads), f32),
        ],
        axis=0,
    )
    low = jnp.concatenate([low, jnp.zeros((extra, rows - heads), f32)], axis=1)
    last = out.shape[0] - extra
    out[last:, :] = jnp.zeros((extra, wide), bf16)
    out[last:, :rows] = (gains + low).astype(bf16)


def choose_units_kernel(shards, scal, gate, up, out):
    position = scal[0]
    units = out.shape[1] // 2
    size = units // shards
    group = gate.shape[1] // shards
    for c in range(gate.shape[1] // units):

        @pl.when(position == c)
        def _():
            for n, ref in enumerate((gate, up)):
                out[:, n * units : (n + 1) * units] = jnp.concatenate(
                    [
                        ref[:, r * group + c * size : r * group + (c + 1) * size]
                        for r in range(shards)
                    ],
                    axis=1,
                )


def tokens_kernel(shards, scal, x, cotangent, out):
    rows, width = x.shape
    size = width // shards
    for l in range(shards):
        start = pl.multiple_of(scal[2 + l] * size, size)
        out[:rows, l * size : (l + 1) * size] = x[:, pl.ds(start, size)]
    row = lax.broadcasted_iota(i32, (rows, width), 0) + scal[0] * rows
    out[rows:, :] = jnp.where(row < scal[1], cotangent[...].astype(f32), 0.0).astype(bf16)


def head_choice(each, shards, position, my_heads, heads):
    h = lax.broadcasted_iota(i32, (my_heads, heads), 0)
    if each:
        shift = each.bit_length() - 1
        head_id = (h >> shift) * (heads // shards) + position * each + (h & (each - 1))
    else:
        head_id = position * my_heads + h
    return (lax.broadcasted_iota(i32, (my_heads, heads), 1) == head_id).astype(f32).astype(bf16)


def bucket_rows(scal, shards, offset):
    row = lax.broadcasted_iota(i32, (bucket_total, offset.shape[1]), 0)
    buckets = bucket_total // shards
    shift = buckets.bit_length() - 1
    bucket_id = jnp.zeros_like(row)
    for l in range(shards):
        bucket_id = jnp.where(
            (row >> shift) == l, scal[2 + l] * buckets + (row & (buckets - 1)), bucket_id
        )
    return (buckets_of(offset) == bucket_id).astype(f32).astype(bf16)


def qkv_kernel(blocks, parts, shards, each, scal, *refs):
    tokens_refs, weights = refs[:blocks], refs[blocks : blocks + parts]
    normed, qkv, bias, gains, scales, joined, small, sems, small_sems = refs[blocks + parts :]
    rows = tokens_refs[0].shape[0]
    tokens, width = normed.shape
    size = width // shards
    stride = sum(w.shape[0] for w in weights) // shards
    places = shard_places(weights, stride)
    step = pl.program_id(0)

    def copy(n, l):
        ref, at = places[l]
        return pltpu.make_async_copy(
            ref.at[pl.ds(at + n * size, size), :],
            joined.at[n, pl.ds(l * size, size), :],
            sems.at[n, l],
        )

    def small_copy(l):
        ref, at = places[l]
        return pltpu.make_async_copy(
            ref.at[pl.ds(at + stride - extra, extra), :], small.at[l], small_sems.at[l]
        )

    @at_step(0)
    def _():
        for l in range(shards):
            small_copy(l).start()
        for n in range(3):
            for l in range(shards):
                copy(n, l).start()
        for l in range(shards):
            small_copy(l).wait()
        my_heads = 2 * bias.shape[0]
        heads = my_heads * blocks
        buckets = bucket_total // shards
        tables = []
        for l in range(shards):
            value = small[l, :, :size].astype(f32)
            gains[:, l * size : (l + 1) * size] = value[:2]
            tables.append(value[2 : 2 + buckets, :heads])
        table = jnp.concatenate(tables, axis=0).astype(bf16)
        chosen = head_choice(each, shards, scal[0], my_heads, heads)
        mine = dot(chosen, table, 1, 1).astype(bf16)
        offset = tokens - lax.broadcasted_iota(i32, (1, 2 * tokens), 1)
        value = dot(mine, bucket_rows(scal, shards, offset))
        for pair in range(bias.shape[0]):
            bias[pair] = value[2 * pair : 2 * pair + 2]
        for t in range(blocks):
            at = slice(t * rows, (t + 1) * rows)
            x = tokens_refs[t][...].astype(f32)
            scale = lax.rsqrt(jnp.mean(x * x, axis=1, keepdims=True) + epsilon)
            normed[at, :] = (x * scale * gains[0:1, :]).astype(bf16)
            scales[at, :] = jnp.broadcast_to(scale, (rows, 128))

    for n in range(3):

        @at_step(n)
        def _():
            for l in range(shards):
                copy(n, l).wait()

    qkv[...] = dot(normed[...], joined[step]).astype(bf16)


def project(scal, tokens_all, weights, shards, each, pairs):
    rows, width = tokens_all[0].shape[0] // 2, tokens_all[0].shape[1]
    blocks = len(tokens_all)
    tokens = rows * blocks
    wide = 128 * pairs
    return call(
        functools.partial(qkv_kernel, blocks, len(weights), shards, each),
        (3,),
        [smem]
        + [pl.BlockSpec((rows, width), lambda n: (0, 0))] * blocks
        + [pl.BlockSpec(memory_space=ANY)] * len(weights),
        [
            pl.BlockSpec((tokens, width), lambda n: (0, 0)),
            pl.BlockSpec((tokens, wide), lambda n: (0, n)),
            pl.BlockSpec((pairs, 2, 2 * tokens), lambda n: (0, 0, 0)),
            pl.BlockSpec((2, width), lambda n: (0, 0)),
            pl.BlockSpec((tokens, 128), lambda n: (0, 0)),
        ],
        [
            struct((tokens, width), bf16),
            struct((tokens, 3 * wide), bf16),
            struct((pairs, 2, 2 * tokens), f32),
            struct((2, width), f32),
            struct((tokens, 128), f32),
        ],
        (scal, *tokens_all, *weights),
        [
            pltpu.VMEM((3, width, wide), bf16),
            pltpu.VMEM((shards, extra, wide), bf16),
            pltpu.SemaphoreType.DMA((3, shards)),
            pltpu.SemaphoreType.DMA((shards,)),
        ],
        flops=6 * tokens * width * wide,
    )


def lanes_of(position, blocks, rows, query, key):
    start = (blocks - 1 + (position ^ query) - (position ^ key)) * rows
    return pl.ds(pl.multiple_of(start, rows), rows)


def forward_kernel(rows, blocks, scal, q_ref, k_ref, v_ref, bias_ref, att, prob, toeplitz):
    position, length = scal[0], scal[1]
    width = 2 * blocks * rows
    slot = lax.broadcasted_iota(i32, (rows, rows), 0)
    for j in range(2):
        row = jnp.broadcast_to(bias_ref[0, j : j + 1, :], (rows, width))
        toeplitz[j] = pltpu.roll(row, width - rows, 1, stride=1, stride_axis=0)
    values = [v_ref[:, 64 * j : 64 * j + 64].astype(f32).T.astype(bf16) for j in range(2)]
    for t in range(blocks):
        at = slice(t * rows, (t + 1) * rows)
        halves = []
        for j in range(2):
            q = q_ref[at, 64 * j : 64 * j + 64]
            k = k_ref[:, 64 * j : 64 * j + 64]
            scores = dot(k, q, 1, 1)
            pieces = []
            for s in range(blocks):
                piece = (
                    scores[s * rows : (s + 1) * rows]
                    + toeplitz[j, :, lanes_of(position, blocks, rows, t, s)]
                )
                live = slot + (position ^ s) * rows < length
                pieces.append(jnp.where(live, piece, masked_score))
            scores = jnp.concatenate(pieces, axis=0)
            top = jnp.max(scores, axis=0, keepdims=True)
            e = jnp.exp(scores - top)
            probs = (e * (1.0 / jnp.sum(e, axis=0, keepdims=True))).astype(bf16)
            prob[j, :, at] = probs
            halves.append(dot(values[j], probs))
        att[at, :] = jnp.concatenate(halves, axis=0).T.astype(bf16)


def backward_kernel(
    rows, blocks, scal, q_ref, k_ref, v_ref, prob, gatt, gq, gk, gv, diag_ref, fold, ds_all
):
    position = scal[0]
    width = 2 * blocks * rows
    grads = [[], [], []]
    for j in range(2):
        columns = slice(64 * j, 64 * j + 64)
        k, v = k_ref[:, columns], v_ref[:, columns]
        fold[...] = jnp.zeros_like(fold)
        for t in range(blocks):
            at = slice(t * rows, (t + 1) * rows)
            gp = dot(v, gatt[at, columns], 1, 1)
            p = prob[j, :, at].astype(f32)
            pg = p * gp
            delta = jnp.sum(pg, axis=0, keepdims=True)
            ds = (pg - p * delta).astype(bf16)
            ds_all[:, at] = ds
            ds = ds.astype(f32)
            for s in range(blocks):
                fold[:, lanes_of(position, blocks, rows, t, s)] += ds[s * rows : (s + 1) * rows]
        grads[0].append(dot(k.astype(f32).T.astype(bf16), ds_all[...]))
        grads[1].append(dot(ds_all[...], q_ref[:, columns]))
        grads[2].append(dot(prob[j], gatt[:, columns]))
        a = fold[...]
        half = rows // 2
        while half >= 8:
            a = a[:half] + pltpu.roll(a[half:], width - half, 1)
            half //= 2
        row = lax.broadcasted_iota(i32, a.shape, 0)
        for bit in (1, 2, 4):
            a = jnp.where((row & bit) != 0, pltpu.roll(a, width - bit, 1), a)
        diag_ref[0, j : j + 1, :] = jnp.sum(a, axis=0, keepdims=True)
    gq[...] = jnp.concatenate(grads[0], axis=0).T.astype(bf16)
    gk[...] = jnp.concatenate(grads[1], axis=1).astype(bf16)
    gv[...] = jnp.concatenate(grads[2], axis=1).astype(bf16)


def attention_forward(scal, qkv, bias, rows, blocks):
    tokens = rows * blocks
    pairs = bias.shape[0]
    return call(
        functools.partial(forward_kernel, rows, blocks),
        (pairs,),
        [smem]
        + [pl.BlockSpec((tokens, 128), lambda p, n=n: (0, n * pairs + p)) for n in range(3)]
        + [pl.BlockSpec((1, 2, 2 * tokens), lambda p: (p, 0, 0))],
        [
            pl.BlockSpec((tokens, 128), lambda p: (0, p)),
            pl.BlockSpec((2, tokens, tokens), lambda p: (p, 0, 0)),
        ],
        [struct((tokens, 128 * pairs), bf16), struct((2 * pairs, tokens, tokens), bf16)],
        (scal, qkv, qkv, qkv, bias),
        [pltpu.VMEM((2, rows, 2 * tokens), f32)],
        flops=8 * pairs * tokens * tokens * 64,
        exps=2 * pairs * tokens * tokens,
    )


def attention_backward(scal, qkv, probs, grad_att, rows, blocks):
    tokens = rows * blocks
    pairs = probs.shape[0] // 2
    block = pl.BlockSpec((tokens, 128), lambda p: (0, p))
    return call(
        functools.partial(backward_kernel, rows, blocks),
        (pairs,),
        [smem]
        + [pl.BlockSpec((tokens, 128), lambda p, n=n: (0, n * pairs + p)) for n in range(3)]
        + [pl.BlockSpec((2, tokens, tokens), lambda p: (p, 0, 0)), block],
        [block, block, block, pl.BlockSpec((1, 2, 2 * tokens), lambda p: (p, 0, 0))],
        [struct((tokens, 128 * pairs), bf16)] * 3 + [struct((pairs, 2, 2 * tokens), f32)],
        (scal, qkv, qkv, qkv, probs, grad_att),
        [pltpu.VMEM((rows, 2 * tokens), f32), pltpu.VMEM((tokens, tokens), bf16)],
        flops=16 * pairs * tokens * tokens * 64,
    )


def out_copies(shards, scal, weights, joined, sems):
    blocks, depth, _ = joined.shape
    size = depth // shards
    stride = sum(w.shape[0] for w in weights) // shards
    first = stride - extra - blocks * size
    copies = []
    for b in range(blocks):
        for l, (ref, at) in enumerate(shard_places(weights, stride)):
            start = pl.multiple_of(scal[2 + l] * size, size)
            copies.append(
                pltpu.make_async_copy(
                    ref.at[pl.ds(at + first + b * size, size), :],
                    joined.at[b, pl.ds(start, size), :],
                    sems.at[b, l],
                )
            )
    return copies


def out_kernel(blocks, parts, shards, scal, att, *refs):
    weights, outs, joined, sems = refs[:parts], refs[parts:-2], refs[-2], refs[-1]
    start_and_wait(out_copies(shards, scal, weights, joined, sems))
    rows = outs[0].shape[0]
    wide = joined.shape[2]
    for b in range(joined.shape[0]):
        total = dot(att[...], joined[b]).astype(bf16)
        for t in range(blocks):
            outs[t][:, b * wide : (b + 1) * wide] = total[t * rows : (t + 1) * rows]


def multiply_out(scal, att, weights, shards, blocks):
    tokens, wide = att.shape
    rows, width = tokens // blocks, wide * blocks
    return call(
        functools.partial(out_kernel, blocks, len(weights), shards),
        (1,),
        [smem, whole(att)] + [pl.BlockSpec(memory_space=ANY)] * len(weights),
        [pl.BlockSpec((rows, width), lambda i: (0, 0))] * blocks,
        [struct((rows, width), bf16)] * blocks,
        (scal, att, *weights),
        [pltpu.VMEM((blocks, wide, wide), bf16), pltpu.SemaphoreType.DMA((blocks, shards))],
        flops=2 * tokens * wide * width,
    )


def grad_attended_kernel(blocks, parts, shards, scal, *refs):
    low, weights = refs[:blocks], refs[blocks : blocks + parts]
    out, joined, sems = refs[blocks + parts :]
    start_and_wait(out_copies(shards, scal, weights, joined, sems))
    wide = joined.shape[2]
    for t, ref in enumerate(low):
        rows = ref.shape[0]
        total = None
        for b in range(joined.shape[0]):
            term = dot(ref[:, b * wide : (b + 1) * wide], joined[b], 1, 1)
            total = term if total is None else total + term
        out[t * rows : (t + 1) * rows, :] = total.astype(bf16)


def make_grad_attended(scal, low_all, weights, shards):
    blocks = len(low_all)
    rows, width = low_all[0].shape
    tokens, wide = rows * blocks, width // blocks
    return call(
        functools.partial(grad_attended_kernel, blocks, len(weights), shards),
        (1,),
        [smem] + [whole(a) for a in low_all] + [pl.BlockSpec(memory_space=ANY)] * len(weights),
        [pl.BlockSpec((tokens, wide), lambda i: (0, 0))],
        [struct((tokens, wide), bf16)],
        (scal, *low_all, *weights),
        [pltpu.VMEM((blocks, wide, wide), bf16), pltpu.SemaphoreType.DMA((blocks, shards))],
        flops=2 * tokens * wide * width,
    )[0]


def hidden_kernel(blocks, shards, scal, x, gains, *refs):
    parts, hidden, nffn = refs[:blocks], refs[blocks], refs[blocks + 1]
    total = x[...].astype(f32)
    for part in parts:
        total = total + part[...].astype(f32)
    hidden[...] = total
    scale = lax.rsqrt(jnp.mean(total * total, axis=1, keepdims=True) + epsilon)
    size = total.shape[1] // shards
    for l in range(shards):
        at = slice(l * size, (l + 1) * size)
        start = pl.multiple_of(scal[2 + l] * size, size)
        nffn[:, at] = (hidden[:, pl.ds(start, size)] * scale * gains[1:2, at]).astype(bf16)


def make_hidden(scal, x, gains, parts, shards):
    rows, width = x.shape
    args = (scal, x, gains, *parts)
    return call(
        functools.partial(hidden_kernel, len(parts), shards),
        (1,),
        [smem] + [whole(a) for a in args[1:]],
        [pl.BlockSpec((rows, width), lambda i: (0, 0))] * 2,
        [struct((rows, width), f32), struct((rows, width), bf16)],
        args,
    )


def gelu_tanh(g):
    return jnp.tanh(0.7978845608028654 * (g + 0.044715 * (g * g * g)))


def units_kernel(blocks, parts, tile, *refs):
    tokens_refs, weights = refs[:blocks], refs[blocks : blocks + parts]
    normed, gate, up, mixed, joined, sems = refs[blocks + parts :]
    rows = tokens_refs[0].shape[0]
    units = weights[0].shape[1] // 2
    step = pl.program_id(0)

    def copies(i):
        result, at = [], 0
        for w, ref in enumerate(weights):
            for n in range(2):
                result.append(
                    pltpu.make_async_copy(
                        ref.at[:, pl.ds(n * units + i * tile, tile)],
                        joined.at[i, pl.ds(at, ref.shape[0]), pl.ds(n * tile, tile)],
                        sems.at[i, 2 * w + n],
                    )
                )
            at += ref.shape[0]
        return result

    @at_step(0)
    def _():
        for i in range(units // tile):
            for c in copies(i):
                c.start()
        for t in range(blocks):
            normed[t * rows : (t + 1) * rows, :] = tokens_refs[t][...]

    for i in range(units // tile):

        @at_step(i)
        def _():
            for c in copies(i):
                c.wait()

    both = dot(normed[...], joined[step])
    g, u = both[:, :tile], both[:, tile:]
    gate[...] = g
    up[...] = u
    mixed[...] = (0.5 * g * (1.0 + gelu_tanh(g)) * u).astype(bf16)


def make_units(tokens_all, weights):
    rows, width = tokens_all[0].shape
    blocks = len(tokens_all)
    tokens = rows * blocks
    units = weights[0].shape[1] // 2
    tile = tile_of(units, 256)
    steps = units // tile
    out = pl.BlockSpec((tokens, tile), lambda i: (0, i))
    return call(
        functools.partial(units_kernel, blocks, len(weights), tile),
        (steps,),
        [whole(a) for a in tokens_all] + [pl.BlockSpec(memory_space=ANY)] * len(weights),
        [pl.BlockSpec((tokens, width), lambda i: (0, 0)), out, out, out],
        [
            struct((tokens, width), bf16),
            struct((tokens, units), f32),
            struct((tokens, units), f32),
            struct((tokens, units), bf16),
        ],
        (*tokens_all, *weights),
        [
            pltpu.VMEM((steps, width, 2 * tile), bf16),
            pltpu.SemaphoreType.DMA((steps, 2 * len(weights))),
        ],
        flops=4 * tokens * width * units,
    )


def grad_down_kernel(blocks, shards, scal, mixed, *refs):
    dy, outs, turned, low = refs[:blocks], refs[blocks:-2], refs[-2], refs[-1]

    @at_step(0)
    def _():
        turned[...] = mixed[...].T

    low[...] = dot(turned[...], jnp.concatenate([r[...] for r in dy], axis=0)).astype(bf16)
    size = low.shape[0] // shards
    each = shards // len(outs)
    for l in range(shards):
        start = pl.multiple_of(scal[2 + l] * size, size)
        outs[side_of(shards)[l][0]][pl.ds(side_of(shards)[l][1] * size, size), :] = low[
            pl.ds(start, size), :
        ]


def side_of(shards):
    chips = shards // 2
    sides, counts = [], [0, 0]
    for slots in (near_slots(chips), far_slots(chips)):
        for p in range(2):
            for _ in slots:
                sides.append((p, counts[p]))
                counts[p] += 1
    return sides


def make_grad_down(scal, mixed, tokens_all, shards):
    blocks = len(tokens_all)
    tokens, units = mixed.shape
    rows, width = tokens // blocks, tokens_all[0].shape[1]
    tile = tile_of(width, 512)
    return call(
        functools.partial(grad_down_kernel, blocks, shards),
        (width // tile,),
        [smem, whole(mixed)] + [pl.BlockSpec((rows, tile), lambda i: (1, i))] * blocks,
        [pl.BlockSpec((units // 2, tile), lambda i: (0, i))] * 2,
        [struct((units // 2, width), bf16)] * 2,
        (scal, mixed, *tokens_all),
        [pltpu.VMEM((units, tokens), bf16), pltpu.VMEM((units, tile), bf16)],
        flops=2 * tokens * units * width,
    )


def down_copies(shards, scal, weights, joined, sems):
    size = joined.shape[0] // shards
    copies = []
    for l, (ref, at) in enumerate(shard_places(weights, size)):
        start = pl.multiple_of(scal[2 + l] * size, size) if shards > 1 else 0
        copies.append(
            pltpu.make_async_copy(
                ref.at[pl.ds(at, size), :], joined.at[pl.ds(start, size), :], sems.at[l]
            )
        )
    return copies


def units_back_kernel(blocks, parts, shards, tile, scal, gate, up, *refs):
    dy, weights = refs[:blocks], refs[blocks : blocks + parts]
    out, joined, grads, sems = refs[blocks + parts :]
    step = pl.program_id(0)
    rows = dy[0].shape[0]
    units = joined.shape[0]

    @at_step(0)
    def _():
        copies = down_copies(shards, scal, weights, joined, sems)
        for c in copies:
            c.start()
        for t in range(blocks):
            grads[t * rows : (t + 1) * rows, :] = dy[t][...]
        for c in copies:
            c.wait()

    weight = joined[pl.ds(pl.multiple_of(step * tile, tile), tile), :]
    grad = dot(grads[...], weight, 1, 1)
    g, u = gate[...], up[...]
    t = gelu_tanh(g)
    slope = 0.5 * (1.0 + t) + 0.5 * g * (1.0 - t * t) * (
        0.7978845608028654 * (1.0 + 3 * 0.044715 * (g * g))
    )
    out[:, pl.ds(pl.multiple_of(step * tile, tile), tile)] = (grad * u * slope).astype(bf16)
    out[:, pl.ds(pl.multiple_of(units + step * tile, tile), tile)] = (
        grad * (0.5 * g * (1.0 + t))
    ).astype(bf16)


def units_back(scal, gate, up, tokens_all, weights, shards):
    blocks = len(tokens_all)
    tokens, units = gate.shape
    rows, width = tokens // blocks, tokens_all[0].shape[1]
    tile = tile_of(units, 256)
    block = pl.BlockSpec((tokens, tile), lambda i: (0, i))
    return call(
        functools.partial(units_back_kernel, blocks, len(weights), shards, tile),
        (units // tile,),
        [smem, block, block]
        + [pl.BlockSpec((rows, width), lambda i: (1, 0))] * blocks
        + [pl.BlockSpec(memory_space=ANY)] * len(weights),
        [pl.BlockSpec((tokens, 2 * units), lambda i: (0, 0))],
        [struct((tokens, 2 * units), bf16)],
        (scal, gate, up, *tokens_all, *weights),
        [
            pltpu.VMEM((units, width), bf16),
            pltpu.VMEM((tokens, width), bf16),
            pltpu.SemaphoreType.DMA((shards,)),
        ],
        flops=2 * tokens * units * width,
    )[0]


def result_kernel(blocks, parts, shards, tile, scal, mixed, *refs):
    weights, outs, joined, sems = refs[:parts], refs[parts:-2], refs[-2], refs[-1]
    start_and_wait(down_copies(shards, scal, weights, joined, sems))
    rows, width = outs[0].shape
    for i in range(width // tile):
        at = slice(i * tile, (i + 1) * tile)
        total = dot(mixed[...], joined[:, at]).astype(bf16)
        for t in range(blocks):
            outs[t][:, at] = total[t * rows : (t + 1) * rows]


def multiply_down(scal, mixed, weights, shards, blocks):
    tokens, units = mixed.shape
    width = weights[0].shape[1]
    rows = tokens // blocks
    return call(
        functools.partial(result_kernel, blocks, len(weights), shards, tile_of(width, 512)),
        (1,),
        [smem, whole(mixed)] + [pl.BlockSpec(memory_space=ANY)] * len(weights),
        [pl.BlockSpec((rows, width), lambda i: (0, 0))] * blocks,
        [struct((rows, width), bf16)] * blocks,
        (scal, mixed, *weights),
        [pltpu.VMEM((units, width), bf16), pltpu.SemaphoreType.DMA((shards,))],
        flops=2 * tokens * units * width,
    )


def shard_specs(weights, rows):
    specs, ranges, first = [], [], 0
    for w in weights:
        count = w.shape[0] // rows
        specs.append(
            pl.BlockSpec(
                (rows, w.shape[1]), lambda l, f=first, n=count: (jnp.clip(l - f, 0, n - 1), 0)
            )
        )
        ranges.append((first, first + count))
        first += count
    return specs, ranges


def within(bounds):
    l = pl.program_id(0)
    return pl.when((l >= bounds[0]) & (l < bounds[1]))


def ffn_transposed_kernel(ranges, g, *refs):
    weights, outs = refs[: len(ranges)], refs[len(ranges) :]
    rows = outs[0].shape[0]
    for ref, bounds in zip(weights, ranges):

        @within(bounds)
        def _():
            total = dot(g[...], ref[...], 1, 1).astype(bf16)
            for t, out in enumerate(outs):
                out[...] = total[t * rows : (t + 1) * rows]


def ffn_transposed(g, weights, size, shards, blocks):
    tokens, depth = g.shape
    rows, width = tokens // blocks, size * shards
    specs, ranges = shard_specs(weights, size)
    return call(
        functools.partial(ffn_transposed_kernel, ranges),
        (shards,),
        [whole(g)] + specs,
        [pl.BlockSpec((rows, size), lambda l: (0, l))] * blocks,
        [struct((rows, width), bf16)] * blocks,
        (g, *weights),
        flops=2 * tokens * depth * width,
    )


def units_grad_kernel(shards, normed, g, *refs):
    outs, turned = refs[:-1], refs[-1]

    @at_step(0)
    def _():
        turned[...] = normed[...].T

    total = dot(turned[...], g[...]).astype(bf16)
    at = 0
    for out in outs:
        n = out.shape[0]
        out[...] = total[at : at + n]
        at += n


def units_grad(normed, g, shards):
    tokens, depth = normed.shape
    width = g.shape[1]
    tile = tile_of(width, 512)
    sizes = []
    for slots in (near_slots(shards // 2), far_slots(shards // 2)):
        if slots:
            sizes += [len(slots) * (depth // shards)] * 2
    return call(
        functools.partial(units_grad_kernel, shards),
        (width // tile,),
        [whole(normed), pl.BlockSpec((tokens, tile), lambda i: (0, i))],
        [pl.BlockSpec((n, tile), lambda i: (0, i)) for n in sizes],
        [struct((n, width), bf16) for n in sizes],
        (normed, g),
        [pltpu.VMEM((depth, tokens), bf16)],
        flops=2 * tokens * depth * width,
    )


def attn_transposed_kernel(blocks, ranges, size, scales, gq, gk, gv, *refs):
    tokens_refs, weights = refs[:blocks], refs[blocks : blocks + len(ranges)]
    outs, gain = refs[blocks + len(ranges) : -1], refs[-1]
    rows = outs[0].shape[0]
    for ref, bounds in zip(weights, ranges):

        @within(bounds)
        def _():
            total = None
            for n, g in enumerate((gq, gk, gv)):
                term = dot(g[...], ref[n * size : (n + 1) * size, :], 1, 1)
                total = term if total is None else total + term
            summed = jnp.zeros((1, size), f32)
            for t, out in enumerate(outs):
                at = slice(t * rows, (t + 1) * rows)
                out[...] = total[at].astype(bf16)
                unit = tokens_refs[t][...].astype(f32) * scales[at, 0:1]
                summed = summed + jnp.sum(total[at] * unit, axis=0, keepdims=True)
            gain[...] = summed


def attn_transposed(scales, grads, tokens_all, weights, size, shards, blocks):
    tokens, wide = grads[0].shape
    rows, width = tokens // blocks, size * shards
    stride = sum(w.shape[0] for w in weights) // shards
    specs, ranges = shard_specs(weights, stride)
    tile = pl.BlockSpec((rows, size), lambda l: (0, l))
    results = call(
        functools.partial(attn_transposed_kernel, blocks, ranges, size),
        (shards,),
        [whole(scales)] + [whole(g) for g in grads] + [tile] * blocks + specs,
        [tile] * blocks + [pl.BlockSpec((1, size), lambda l: (0, l))],
        [struct((rows, width), bf16)] * blocks + [struct((1, width), f32)],
        (scales, *grads, *tokens_all, *weights),
        flops=6 * tokens * wide * width,
    )
    return results[:-1], results[-1]


def split_low(a):
    high = a.astype(bf16)
    return high, (a - high.astype(f32)).astype(bf16)


def owner_counts(shards):
    counts = []
    for slots in (near_slots(shards // 2), far_slots(shards // 2)):
        if slots:
            counts += [len(slots)] * 2
    return counts


def shard_owners(outs, shards):
    return [out for out, n in zip(outs, owner_counts(shards)) for _ in range(n)]


def attn_grad_kernel(
    blocks, shards, each, with_out, scal, normed, att, gq, gk, gv, diag, gain_attn, gain_ffn, *refs
):
    low = refs[:blocks]
    outs, (joined, turned, table) = refs[blocks:-3], refs[-3:]
    tokens, width = normed.shape
    wide = att.shape[1]
    size = width // shards
    head_rows = wide // shards
    rows = tokens // blocks
    my_heads = 2 * diag.shape[0]
    heads = my_heads * blocks

    @at_step(0)
    def _():
        for n, g in enumerate((gq, gk, gv)):
            joined[:, n * wide : (n + 1) * wide] = g[...]
        if with_out:
            turned[...] = dot(
                att[...].T, jnp.concatenate([r[...] for r in low], axis=0)
            ).astype(bf16)
        lane = lax.broadcasted_iota(i32, (1, 2 * tokens), 1)
        lane = jnp.where(lane < 2 * tokens - rows, lane, lane - 2 * tokens)
        of_offset = bucket_rows(scal, shards, (blocks - 1) * rows - lane)
        sums = jnp.concatenate([diag[p] for p in range(diag.shape[0])], axis=0)
        total = None
        for part in split_low(sums):
            term = dot(of_offset, part, 1, 1)
            total = term if total is None else total + term
        chosen = head_choice(each, shards, scal[0], my_heads, heads)
        value = None
        for part in split_low(total):
            term = dot(part, chosen)
            value = term if value is None else value + term
        table[...] = value

    buckets = bucket_total // shards
    for l, out in enumerate(shard_owners(outs, shards)):

        @at_step(l)
        def _():
            total = dot(normed[:, l * size : (l + 1) * size], joined[...], 0, 0).astype(bf16)
            for n in range(3):
                out[n * size : (n + 1) * size, :] = total[:, n * wide : (n + 1) * wide]
            if with_out:
                start = pl.multiple_of(scal[2 + l] * head_rows, head_rows)
                for b in range(blocks):
                    out[3 * size + b * head_rows : 3 * size + (b + 1) * head_rows, :] = turned[
                        pl.ds(start, head_rows), b * wide : (b + 1) * wide
                    ]
            part = jnp.concatenate(
                [
                    jnp.zeros((2, heads), f32),
                    table[l * buckets : (l + 1) * buckets, :],
                    jnp.zeros((extra - 2 - buckets, heads), f32),
                ],
                axis=0,
            )
            part = jnp.concatenate([part, jnp.zeros((extra, size - heads), f32)], axis=1)
            row = lax.broadcasted_iota(i32, (extra, size), 0)
            columns = slice(l * size, (l + 1) * size)
            part = part + jnp.where(
                row == 0,
                gain_attn[:, columns],
                jnp.where(row == 1, gain_ffn[:, columns], 0.0),
            )
            last = out.shape[0] - extra
            out[last:, :] = jnp.zeros((extra, wide), bf16)
            out[last:, :size] = part.astype(bf16)


def attn_grad(scal, normed, att, grads, diag, gain_attn, gain_ffn, low_all, shards, each, stride):
    tokens, width = normed.shape
    wide = att.shape[1]
    blocks = len(low_all)
    counts = owner_counts(shards)
    specs, first = [], 0
    for n in counts:
        specs.append(
            pl.BlockSpec((stride, wide), lambda l, f=first, n=n: (jnp.clip(l - f, 0, n - 1), 0))
        )
        first += n
    args = (scal, normed, att, *grads, diag, gain_attn, gain_ffn, *low_all)
    return call(
        functools.partial(attn_grad_kernel, blocks, shards, each, bool(each)),
        (shards,),
        [smem] + [whole(a) for a in args[1:]],
        specs,
        [struct((n * stride, wide), bf16) for n in counts],
        args,
        [
            pltpu.VMEM((tokens, 3 * wide), bf16),
            pltpu.VMEM((wide, width), bf16),
            pltpu.VMEM((bucket_total, 2 * diag.shape[0] * blocks), f32),
        ],
        flops=8 * tokens * wide * width,
    )


def ffn_norm_back_kernel(blocks, shards, scal, hidden, gains, own, *refs):
    parts = refs[:blocks]
    grad_hidden, low, grad_gain, g, gain = refs[blocks:]
    size = hidden.shape[1] // shards
    for l in range(shards):
        at = slice(l * size, (l + 1) * size)
        start = pl.multiple_of(scal[2 + l] * size, size)
        total = parts[0][:, at].astype(f32)
        for part in parts[1:]:
            total = total + part[:, at].astype(f32)
        g[:, pl.ds(start, size)] = total
        gain[:, pl.ds(start, size)] = gains[1:2, at]
    h = hidden[...]
    scale = lax.rsqrt(jnp.mean(h * h, axis=1, keepdims=True) + epsilon)
    weighted = g[...] * gain[...]
    inner = jnp.mean(weighted * h, axis=1, keepdims=True)
    value = own[...].astype(f32) + scale * weighted - h * (scale * scale * scale) * inner
    grad_hidden[...] = value
    low[...] = value.astype(bf16)
    g[...] = g[...] * h * scale
    for l in range(shards):
        start = pl.multiple_of(scal[2 + l] * size, size)
        grad_gain[:, l * size : (l + 1) * size] = jnp.sum(
            g[:, pl.ds(start, size)], axis=0, keepdims=True
        )


def ffn_norm_back(scal, hidden, gains, own, parts, shards):
    rows, width = hidden.shape
    block = pl.BlockSpec((rows, width), lambda i: (0, 0))
    return call(
        functools.partial(ffn_norm_back_kernel, len(parts), shards),
        (1,),
        [smem, block, whole(gains), pl.BlockSpec((rows, width), lambda i: (1, 0))]
        + [block] * len(parts),
        [block, block, pl.BlockSpec((1, width), lambda i: (0, 0))],
        [struct((rows, width), f32), struct((rows, width), bf16), struct((1, width), f32)],
        (scal, hidden, gains, own, *parts),
        [pltpu.VMEM((rows, width), f32), pltpu.VMEM((1, width), f32)],
    )


def attn_norm_back_kernel(blocks, shards, scal, grad_hidden, gains, own, *refs):
    parts = refs[:blocks]
    grad, value = refs[blocks:]
    x = own[...].astype(f32)
    g = parts[0][...].astype(f32)
    for part in parts[1:]:
        g = g + part[...].astype(f32)
    scale = lax.rsqrt(jnp.mean(x * x, axis=1, keepdims=True) + epsilon)
    weighted = g * gains[0:1, :]
    inner = jnp.mean(weighted * x, axis=1, keepdims=True)
    value[...] = scale * weighted - x * (scale * scale * scale) * inner
    size = x.shape[1] // shards
    for l in range(shards):
        at = slice(l * size, (l + 1) * size)
        where = pl.ds(pl.multiple_of(scal[2 + l] * size, size), size)
        grad[:, where] = (grad_hidden[:, where] + value[:, at]).astype(bf16)


def attn_norm_back(scal, grad_hidden, gains, own, parts, shards):
    rows, width = grad_hidden.shape
    block = pl.BlockSpec((rows, width), lambda i: (0, 0))
    return call(
        functools.partial(attn_norm_back_kernel, len(parts), shards),
        (1,),
        [smem, block, whole(gains), block] + [block] * len(parts),
        [block],
        [struct((rows, width), bf16)],
        (scal, grad_hidden, gains, own, *parts),
        [pltpu.VMEM((rows, width), f32)],
    )[0]


def by_position(scal, blocks, body):
    for p in range(blocks):

        @pl.when(scal[0] == p)
        def _():
            body([p ^ c for c in range(blocks)])


def columns_kernel(groups, scal, *refs):
    pieces, outs = refs[:-2], refs[-2:]
    blocks = len(pieces)
    units = pieces[0].shape[1] // 2
    size = units // groups
    wide = blocks * size

    def body(order):
        for n, out in enumerate(outs):
            for g in range(groups):
                at = n * units + g * size
                out[:, g * wide : (g + 1) * wide] = jnp.concatenate(
                    [pieces[t][:, at : at + size] for t in order], axis=1
                ).astype(f32)

    by_position(scal, blocks, body)


def assemble_units(scal, pieces, groups):
    rows, columns = pieces[0].shape
    tile = min(rows, 32)
    wide = len(pieces) * columns // 2
    return call(
        functools.partial(columns_kernel, groups),
        (rows // tile,),
        [smem] + [pl.BlockSpec((tile, columns), lambda i: (i, 0))] * len(pieces),
        [pl.BlockSpec((tile, wide), lambda i: (i, 0))] * 2,
        [struct((rows, wide), f32)] * 2,
        (scal, *pieces),
    )


def rows_kernel(size, scal, *refs):
    position = scal[0]
    for t, piece in enumerate(refs[:-1]):
        start = pl.multiple_of((position ^ t) * size, 8)
        refs[-1][pl.ds(start, size), :] = piece[...].astype(f32)


def assemble_rows(scal, pieces):
    rows, columns = pieces[0].shape
    tile = tile_of(columns, 512)
    return call(
        functools.partial(rows_kernel, rows),
        (columns // tile,),
        [smem] + [pl.BlockSpec((rows, tile), lambda i: (0, i))] * len(pieces),
        [pl.BlockSpec((rows * len(pieces), tile), lambda i: (0, i))],
        [struct((rows * len(pieces), columns), f32)],
        (scal, *pieces),
    )[0]


def attention_outputs_kernel(each, blocks, head_width, count, last, scal, *refs):
    columns, rest = refs[: count * blocks], refs[count * blocks :]
    with_out = last and bool(each)
    out_blocks = rest[:blocks] if with_out else ()
    rest = rest[blocks:] if with_out else rest
    small, outs = (rest[:blocks], rest[blocks:]) if last else ((), rest)
    wide = columns[0].shape[1]
    step = pl.program_id(0)

    def body(order):
        for n in range(count):
            pieces = [columns[count * t + n] for t in order]
            if each:
                size = each * head_width
                for g in range(wide // size):
                    outs[n][:, g * blocks * size : (g + 1) * blocks * size] = jnp.concatenate(
                        [ref[:, g * size : (g + 1) * size] for ref in pieces], axis=1
                    ).astype(f32)
            else:
                for c, ref in enumerate(pieces):
                    outs[n][:, c * wide : (c + 1) * wide] = ref[...].astype(f32)

        if last:

            @at_step(0)
            def _():
                total = small[order[0]][...].astype(f32)
                for t in order[1:]:
                    total = total + small[t][...].astype(f32)
                outs[-1][...] = total

    by_position(scal, blocks, body)
    if with_out:
        for t in range(blocks):

            @pl.when((step ^ scal[0]) == t)
            def _():
                size = outs[count].shape[0]
                for b in range(blocks):
                    outs[count][:, b * wide : (b + 1) * wide] = out_blocks[t][
                        b * size : (b + 1) * size, :
                    ].astype(f32)


def attention_outputs(scal, pieces, count, rows, each, head_width, last):
    blocks = len(pieces)
    total, wide = pieces[0].shape
    tile = rows // blocks
    per = rows // tile
    specs, args = [], []
    for a in pieces:
        for n in range(count):
            specs.append(pl.BlockSpec((tile, wide), lambda i, n=n: (n * per + i, 0)))
            args.append(a)
    outputs = count
    if last and each:
        specs += [pl.BlockSpec((rows, wide), lambda i: (count, 0))] * blocks
        args += pieces
        outputs += 1
    if last:
        specs += [pl.BlockSpec((extra, wide), lambda i: (total // extra - 1, 0))] * blocks
        args += pieces
    block = pl.BlockSpec((tile, wide * blocks), lambda i: (i, 0))
    out_specs, out_shape = [block] * outputs, [struct((rows, wide * blocks), f32)] * outputs
    if last:
        out_specs.append(pl.BlockSpec((extra, wide), lambda i: (0, 0)))
        out_shape.append(struct((extra, wide), f32))
    return call(
        functools.partial(attention_outputs_kernel, each, blocks, head_width, count, last),
        (blocks,),
        [smem] + specs,
        out_specs,
        out_shape,
        (scal, *args),
    )


def take_blocks(a, starts, size):
    return jnp.concatenate([lax.dynamic_slice_in_dim(a, s, size, 0) for s in starts], 0)


def on_device(
    inputs,
    lengths,
    w_query,
    w_key,
    w_value,
    w_out,
    w_gate,
    w_up,
    w_down,
    norm_attn,
    norm_ffn,
    relative_bias_table,
    cotangent,
):
    blocks = lax.axis_size("ctx")
    shards = lax.axis_size("fsdp")
    chips = shards // 2
    position = lax.axis_index("ctx")
    shard = lax.axis_index("fsdp")
    chip, core = shard // 2, shard % 2
    rows, width = inputs.shape[1], inputs.shape[2]
    tokens = rows * blocks
    heads = relative_bias_table.shape[1]
    head_width = width // heads
    my_heads = heads // blocks
    pairs = my_heads // 2
    each = heads // shards // blocks if (heads // shards) % blocks == 0 else 0
    strided = each in (1, 2)
    each = each if strided else 0
    units = w_gate.shape[1] // blocks
    shard_rows = width // shards
    unit_rows = w_down.shape[0] // blocks

    slot_of, parity_of = [], []
    for slots in (near_slots(chips), far_slots(chips)):
        for p in range(2):
            slot_of += slots
            parity_of += [p] * len(slots)
    pad = [0, 0]
    order = 2 * ((chip + jnp.array(pad + slot_of, i32)) % chips) + (
        core ^ jnp.array(pad + parity_of, i32)
    )
    index = jnp.arange(shards + 2, dtype=i32)
    scal = jnp.where(index == 0, position, jnp.where(index == 1, lengths[0], order)).astype(i32)

    def heads_of(c):
        if strided:
            return [
                (h // each) * (heads // shards) + c * each + h % each for h in range(my_heads)
            ]
        return [c * my_heads + h for h in range(my_heads)]

    own_tokens = call(
        functools.partial(tokens_kernel, shards),
        (1,),
        [smem] + [pl.BlockSpec((rows, width), lambda i: (0, 0))] * 2,
        [pl.BlockSpec((2 * rows, width), lambda i: (0, 0))],
        [struct((2 * rows, width), bf16)],
        (scal, inputs[0], cotangent[0]),
    )[0]
    all_tokens = ctx_gather(own_tokens)
    args = (
        after(scal, own_tokens),
        w_query,
        w_key,
        w_value,
        w_out,
        norm_attn.reshape(1, -1),
        norm_ffn.reshape(1, -1),
        relative_bias_table,
    )
    stride = (4 if strided else 3) * shard_rows + extra
    own_attn = call(
        functools.partial(
            choose_attention_kernel, [heads_of(c) for c in range(blocks)], head_width, strided
        ),
        (1,),
        [smem] + [whole(a) for a in args[1:]],
        [pl.BlockSpec((stride, 128 * pairs), lambda i: (0, 0))],
        [struct((stride, 128 * pairs), bf16)],
        args,
    )[0]
    near_attn = gather_near(own_attn)
    tile = tile_of(shard_rows, 64)
    own_gate_up = call(
        functools.partial(choose_units_kernel, shards),
        (shard_rows // tile,),
        [smem] + [pl.BlockSpec((tile, w_gate.shape[1]), lambda i: (i, 0))] * 2,
        [pl.BlockSpec((tile, 2 * units), lambda i: (i, 0))],
        [struct((shard_rows, 2 * units), bf16)],
        (after(scal, own_attn), w_gate, w_up),
    )[0]
    joint = together([*near_attn, *all_tokens], own_gate_up)
    near_attn, all_tokens = joint[: len(near_attn)], joint[len(near_attn) :]
    far_attn = gather_far(near_attn, chip)
    n = len(near_attn)
    joint = together([core_swap(a) for a in near_attn] + far_attn)
    weights_attn, far_attn = [*near_attn, *joint[:n]], joint[n:]
    near_gate_up = gather_near(after(own_gate_up, *far_attn))
    weights_attn += with_other_core(far_attn)
    if not strided:
        gathered = lax.all_gather(w_out, "fsdp", axis=0, tiled=True)
        size = my_heads * head_width
        full_out = lax.dynamic_slice_in_dim(gathered, position * size, size, 0)

    normed, qkv, bias, gains, scales = project(
        scal, all_tokens, weights_attn, shards, each, pairs
    )
    attended, probs = attention_forward(scal, qkv, bias, rows, blocks)
    if strided:
        parts = multiply_out(scal, attended, weights_attn, shards, blocks)
    else:
        whole_part = dot(attended, full_out).astype(bf16)
        parts = [whole_part[t * rows : (t + 1) * rows] for t in range(blocks)]
    parts = ctx_exchange(parts)
    hidden, own_nffn = make_hidden(scal, inputs[0], gains, parts, shards)

    near_gate_up = together(near_gate_up, own_nffn)
    far_gate_up = gather_far(near_gate_up, chip)
    joint = together(with_other_core(near_gate_up) + ctx_gather(own_nffn) + far_gate_up)
    weights_gate_up = list(joint[:2])
    all_nffn, far_gate_up = joint[2 : 2 + blocks], joint[2 + blocks :]
    own_down = lax.dynamic_slice_in_dim(w_down, position * unit_rows, unit_rows, 0)
    near_down = gather_near(after(own_down, all_nffn[0]))
    weights_gate_up += with_other_core(far_gate_up)
    normed_ffn, gate, up, mixed_units = make_units(all_nffn, weights_gate_up)

    aligned = unit_rows % 16 == 0
    if aligned:
        grads_down = make_grad_down(scal, mixed_units, all_tokens, shards)
    else:
        all_dy = jnp.concatenate([a[rows:] for a in all_tokens], axis=0)
        grad_down = dot(mixed_units, all_dy, 0, 0).astype(bf16)
        grads_down = [
            take_blocks(
                grad_down,
                [order[2 + l] * unit_rows for l in range(shards) if parity_of[l] == side],
                unit_rows,
            )
            for side in range(2)
        ]
    joint = together([*near_down, *grads_down])
    near_down, grads_down = joint[:-2], joint[-2:]
    far_down = gather_far(near_down, chip)
    sums_down = core_sum(*grads_down)
    joint = together(with_other_core(near_down) + far_down, *sums_down)
    down_parts, far_down = list(joint[:2]), joint[2:]
    down_parts, down_shards = down_parts + with_other_core(far_down), shards
    if not aligned:
        joined = jnp.concatenate(down_parts, axis=0)
        place = jnp.argsort(order[2:])
        down_parts = [take_blocks(joined, [place[r] * unit_rows for r in range(shards)], unit_rows)]
        down_shards = 1

    far_sum = None
    if len(sums_down) == 2:
        far_sum = reduce_far(after(sums_down[0], *far_down))
    grad_units = units_back(scal, gate, up, all_tokens, down_parts, down_shards)
    if far_sum is not None:
        far_sum, grad_units = together([far_sum, grad_units])
    sends = together(near_sends(sums_down[-1], far_sum, chip), grad_units)
    received = near_receive(sends)
    parts = ffn_transposed(after(grad_units, *sends), weights_gate_up, shard_rows, shards, blocks)
    grads_gate_up = units_grad(normed_ffn, after(grad_units, *parts), shards)
    parts = ctx_exchange(parts)
    result_parts = multiply_down(
        scal, after(mixed_units, *grads_gate_up), down_parts, down_shards, blocks
    )
    joint = together([*parts, *received, *grads_gate_up], *result_parts)
    parts, grads_gate_up = list(joint[:blocks]), joint[blocks + len(received) :]
    share_down = near_total(joint[blocks : blocks + len(received)])
    far_sum = []
    if len(grads_gate_up) == 4:
        far_add = add_low(grads_gate_up[2], core_swap(grads_gate_up[3]))
        far_sum = [reduce_far(far_add)]
        parts = together(parts, far_add)
    grad_hidden, low, grad_gain_ffn = ffn_norm_back(
        scal, hidden, gains, own_tokens, parts, shards
    )

    all_low = ctx_gather(low)
    near_sum = add_low(grads_gate_up[0], core_swap(after(grads_gate_up[1], low)))
    sends = near_sends(near_sum, far_sum[0] if far_sum else None, chip)
    received = near_receive(sends)
    result_parts = ctx_exchange(together(result_parts, *all_low))
    if strided:
        grad_att = make_grad_attended(after(scal, *sends), all_low, weights_attn, shards)
    else:
        grad_att = dot(jnp.concatenate(all_low, axis=0), full_out, 1, 1).astype(bf16)
    *grads, diagonals = attention_backward(scal, qkv, probs, grad_att, rows, blocks)
    joint = together([*grads, *result_parts])
    grads, result_parts = joint[:3], joint[3:]
    result = hidden
    for part in result_parts:
        result = result + part.astype(f32)
    result = result.astype(bf16)
    parts, grad_gain_attn = attn_transposed(
        scales, grads, all_tokens, weights_attn, shard_rows, shards, blocks
    )
    near_down_share = ctx_gather_near(after(share_down, *result_parts))
    joint = together([*parts, *near_down_share])
    parts, near_down_share = list(joint[:blocks]), joint[blocks:]
    parts = ctx_exchange(parts)
    grads_attn = attn_grad(
        scal,
        normed,
        attended,
        [after(grads[0], *parts[:1]), *grads[1:]],
        diagonals,
        grad_gain_attn,
        grad_gain_ffn,
        all_low,
        shards,
        each,
        stride,
    )
    n = len(received)
    joint = together([*parts, *received, *grads_attn])
    parts, received, grads_attn = joint[:blocks], joint[blocks : blocks + n], joint[blocks + n :]
    input_grad = attn_norm_back(scal, grad_hidden, gains, own_tokens, parts, shards)
    far_sum, far_add = [], grads_attn[0]
    if len(grads_attn) == 4:
        far_add = add_low(grads_attn[2], core_swap(grads_attn[3]))
        far_sum = [reduce_far(far_add)]
    near_sum = add_low(grads_attn[0], core_swap(after(grads_attn[1], far_add)))
    share_gate_up = near_total(received)
    near_units = ctx_gather_near(after(share_gate_up, far_add))
    near_sum, *far_sum = together([near_sum, *far_sum])
    far_sum = far_sum[0] if far_sum else None
    cut = 2 * shard_rows
    first = near_receive(near_sends(near_sum, far_sum, chip, (0, cut)))
    sends = near_sends(near_sum, far_sum, chip, (cut, stride))
    far_units = ctx_gather_far(together(near_units, *sends))
    far_down_share = ctx_gather_far(together(near_down_share, *far_units))
    joint = together([*first, *far_down_share, *sends])
    first, far_down_share, sends = near_total(joint[:n]), joint[n:-n], joint[-n:]
    second = near_receive(sends)
    joint = together([*ctx_gather(first), *second])
    pieces_first, second = joint[:blocks], near_total(joint[blocks:])
    pieces_second = ctx_gather(second)
    pieces_gate_up = ctx_pieces(share_gate_up, near_units, far_units)
    pieces_down = ctx_pieces(share_down, near_down_share, far_down_share)

    g_down = assemble_rows(scal, pieces_down)
    if blocks * unit_rows % 128 == 0:
        g_gate, g_up = assemble_units(scal, pieces_gate_up, shards)
    else:
        stacked = jnp.stack(pieces_gate_up)
        stacked = [
            lax.dynamic_slice_in_dim(stacked, position ^ c, 1, 0)[0] for c in range(blocks)
        ]
        g_gate, g_up = [
            jnp.concatenate(
                [
                    stacked[c][:, n * units + r * unit_rows : n * units + (r + 1) * unit_rows]
                    for r in range(shards)
                    for c in range(blocks)
                ],
                axis=1,
            ).astype(f32)
            for n in range(2)
        ]
    outs_attn = attention_outputs(
        scal, list(pieces_first), 2, shard_rows, each, head_width, False
    )
    *rest, small = attention_outputs(
        scal, list(pieces_second), 1, shard_rows, each, head_width, True
    )
    outs_attn = [*outs_attn, *rest]
    if not strided:
        spot = jnp.zeros((width, width), bf16)
        spot = lax.dynamic_update_slice_in_dim(
            spot,
            dot(attended, jnp.concatenate(all_low, axis=0), 0, 0).astype(bf16),
            position * my_heads * head_width,
            0,
        )
        g_out = lax.psum_scatter(spot, "fsdp", scatter_dimension=0, tiled=True)
        outs_attn.append(lax.psum(g_out, "ctx").astype(f32))
    buckets = relative_bias_table.shape[0]
    return (
        result[None],
        input_grad[None],
        *outs_attn,
        g_gate,
        g_up,
        g_down,
        small[0, :shard_rows],
        small[1, :shard_rows],
        small[2 : 2 + buckets, :heads],
    )


def solution(mesh):
    rows = P("fsdp", None)
    tokens = P("fsdp", "ctx", None)
    in_specs = (tokens, P("fsdp")) + (rows,) * 7 + (P("fsdp"), P("fsdp"), rows, tokens)
    out_specs = (tokens, tokens) + (rows,) * 7 + (P("fsdp"), P("fsdp"), rows)
    return jax.shard_map(
        on_device, mesh=mesh, in_specs=in_specs, out_specs=out_specs, check_vma=False
    )
```

```python
import functools

import jax
import jax.numpy as jnp
import numpy as np
from jax import lax
from jax.experimental import pallas as pl
from jax.experimental.pallas import tpu as pltpu
from jax.sharding import PartitionSpec as P

bucket_total = 32
bucket_total = 32
bucket_edges = (12, 16, 23, 32, 46, 64, 91)
epsilon = 1e-06
masked_score = -1e30
f32 = jnp.float32
bf16 = jnp.bfloat16
i32 = jnp.int32
vmem_limit = 52 * 1024 * 1024
extra = 16
ANY = pl.ANY


def dot(a, b, ca=1, cb=0):
    return lax.dot_general(a, b, (((ca,), (cb,)), ((), ())), preferred_element_type=f32)


def buckets_of(offset):
    distance = jnp.abs(offset)
    bucket = jnp.minimum(distance, 8)
    for edge_value in bucket_edges:
        bucket = bucket + (distance >= edge_value).astype(i32)
    return bucket + 16 * (offset > 0).astype(i32)


def after(value, *earlier):
    return lax.optimization_barrier((value, *earlier))[0]


def together(values, *earlier):
    return lax.optimization_barrier((*values, *earlier))[: len(values)]


def core_swap(a):
    size = lax.axis_size("fsdp")
    return lax.ppermute(a, "fsdp", [(r, r ^ 1) for r in range(size)])


def core_exchange(a):
    groups = [[r, r + 1] for r in range(0, lax.axis_size("fsdp"), 2)]
    return lax.all_to_all(a, "fsdp", 0, 0, axis_index_groups=groups, tiled=True)


def chip_send(a, pairs):
    return lax.ppermute(a, "fsdp", [(2 * s + k, 2 * d + k) for s, d in pairs for k in range(2)])


def ctx_send(a, distance):
    size = lax.axis_size("ctx")
    return lax.ppermute(a, "ctx", [(i, i ^ distance) for i in range(size)])


def near_slots(chips):
    return [0, 1, 3] if chips == 4 else list(range(chips))


def far_slots(chips):
    return [2] if chips == 4 else []


def gather_near(own):
    chips = lax.axis_size("fsdp") // 2
    if chips == 4:
        above = chip_send(own, [(1, 0), (2, 1), (3, 2), (0, 3)])
        below = chip_send(own, [(0, 1), (1, 2), (2, 3), (3, 0)])
        return [own, above, below]
    return [own] + [
        chip_send(own, [((z + t) % chips, z) for z in range(chips)]) for t in range(1, chips)
    ]


def gather_far(near, chip):
    if lax.axis_size("fsdp") // 2 != 4:
        return []
    own, above, below = near
    middle = jnp.where(chip == 1, above, jnp.where(chip == 2, below, own))
    return [chip_send(middle, [(3, 1), (0, 2), (1, 0), (2, 3)])]


def with_other_core(slots):
    if not slots:
        return []
    half = jnp.concatenate(slots, axis=0) if len(slots) > 1 else slots[0]
    return [half, core_swap(half)]


def add_low(a, b):
    return (a.astype(f32) + b.astype(f32)).astype(bf16)


def core_sum(mine, other):
    chips = lax.axis_size("fsdp") // 2
    swapped = core_swap(other)
    if chips != 4:
        return [add_low(mine, swapped)]
    near = mine.shape[0] // 4 * 3
    return [add_low(mine[near:], swapped[near:]), add_low(mine[:near], swapped[:near])]


def reduce_far(far):
    return chip_send(far, [(0, 1), (3, 2), (1, 3), (2, 0)])


def near_sends(near, far, chip, rows=None):
    chips = lax.axis_size("fsdp") // 2
    size = near.shape[0] // len(near_slots(chips))
    first, last = rows or (0, size)
    parts = [near[s * size + first : s * size + last] for s in range(len(near_slots(chips)))]
    if chips != 4:
        return parts[1:], (parts[0], None)
    far = far[first:last]
    wide = far.astype(f32)
    zero = jnp.zeros((), f32)
    up = parts[1].astype(f32) + jnp.where(chip == 1, wide, zero)
    down = parts[2].astype(f32) + jnp.where(chip == 2, wide, zero)
    return [up.astype(bf16), down.astype(bf16)], (parts[0], far)


def near_receive(sends):
    chips = lax.axis_size("fsdp") // 2
    if chips == 4:
        from_below = chip_send(sends[0], [(0, 1), (1, 2), (2, 3), (3, 0)])
        from_above = chip_send(sends[1], [(1, 0), (2, 1), (3, 2), (0, 3)])
        return [from_below, from_above]
    return [
        chip_send(sends[t - 1], [(z, (z + t) % chips) for z in range(chips)])
        for t in range(1, chips)
    ]


def near_total(received, kept, chip):
    own, far = kept
    total = own.astype(f32)
    if far is not None:
        total = total + jnp.where((chip == 0) | (chip == 3), far.astype(f32), jnp.zeros((), f32))
    for part in received:
        total = total + part.astype(f32)
    return total.astype(bf16)


def ctx_gather(a):
    return [a] + [ctx_send(a, t) for t in range(1, lax.axis_size("ctx"))]


def ctx_gather_near(a):
    if lax.axis_size("ctx") == 4:
        return [ctx_send(a, 1), ctx_send(a, 2)]
    return ctx_gather(a)[1:]


def ctx_gather_far(near):
    if lax.axis_size("ctx") == 4:
        half = near[0].shape[0] // 2
        return [ctx_send(near[1][:half], 1), ctx_send(near[0][half:], 2)]
    return []


def ctx_pieces(own, near, far):
    return [own, *near] + ([jnp.concatenate(far, axis=0)] if far else [])


def ctx_exchange(parts):
    return [parts[0]] + [ctx_send(parts[t], t) for t in range(1, len(parts))]


smem = pl.BlockSpec(memory_space=pltpu.SMEM)


def whole(a):
    return pl.BlockSpec(a.shape, lambda *_: (0,) * len(a.shape))


def struct(shape, dtype):
    return jax.ShapeDtypeStruct(shape, dtype)


def call(kernel, grid, in_specs, out_specs, out_shape, args, scratch=(), flops=0, moved=None, exps=0):
    if moved is None:
        moved = sum(a.size * a.dtype.itemsize for a in args) + sum(
            int(np.prod(o.shape)) * jnp.dtype(o.dtype).itemsize for o in out_shape
        )
    return pl.pallas_call(
        kernel,
        grid=grid,
        in_specs=in_specs,
        out_specs=out_specs,
        out_shape=out_shape,
        scratch_shapes=scratch,
        compiler_params=pltpu.CompilerParams(vmem_limit_bytes=vmem_limit),
        cost_estimate=pl.CostEstimate(flops=1, bytes_accessed=1, transcendentals=0),
    )(*args)


def shard_places(refs, stride):
    return [(ref, s * stride) for ref in refs for s in range(ref.shape[0] // stride)]


def tile_of(size, most):
    tile = most
    while size % tile:
        tile //= 2
    return tile


def start_and_wait(copies):
    for c in copies:
        c.start()
    for c in copies:
        c.wait()


def at_step(n):
    return pl.when(pl.program_id(0) == n)


def choose_attention_kernel(head_ids, head_width, with_out, scal, q, k, v, wo, na, nf, table, out):
    position = scal[0]
    rows = q.shape[0]
    wide = out.shape[1]
    for c, ids in enumerate(head_ids):

        @pl.when(position == c)
        def _():
            for n, ref in enumerate((q, k, v)):
                for pair in range(len(ids) // 2):
                    halves = [
                        ref[:, h * head_width : (h + 1) * head_width]
                        for h in ids[2 * pair : 2 * pair + 2]
                    ]
                    out[n * rows : (n + 1) * rows, pair * 128 : pair * 128 + 128] = (
                        jnp.concatenate(halves, axis=1)
                    )
            if with_out:
                blocks = len(head_ids)
                size = rows // blocks
                for b in range(blocks):
                    out[3 * rows + b * size : 3 * rows + (b + 1) * size, :] = wo[
                        c * size : (c + 1) * size, b * wide : (b + 1) * wide
                    ]

    row = lax.broadcasted_iota(i32, (extra, rows), 0)
    gains = jnp.where(row == 0, na[...].astype(f32), jnp.where(row == 1, nf[...].astype(f32), 0.0))
    buckets, heads = table.shape
    low = jnp.concatenate(
        [
            jnp.zeros((2, heads), f32),
            table[...].astype(f32),
            jnp.zeros((extra - 2 - buckets, heads), f32),
        ],
        axis=0,
    )
    low = jnp.concatenate([low, jnp.zeros((extra, rows - heads), f32)], axis=1)
    last = out.shape[0] - extra
    out[last:, :] = jnp.zeros((extra, wide), bf16)
    out[last:, :rows] = (gains + low).astype(bf16)


def choose_units_kernel(shards, scal, gate, up, out):
    position = scal[0]
    units = out.shape[1] // 2
    size = units // shards
    group = gate.shape[1] // shards
    for c in range(gate.shape[1] // units):

        @pl.when(position == c)
        def _():
            for n, ref in enumerate((gate, up)):
                out[:, n * units : (n + 1) * units] = jnp.concatenate(
                    [
                        ref[:, r * group + c * size : r * group + (c + 1) * size]
                        for r in range(shards)
                    ],
                    axis=1,
                )


def tokens_kernel(shards, scal, x, cotangent, out):
    rows, width = x.shape
    size = width // shards
    for l in range(shards):
        start = pl.multiple_of(scal[2 + l] * size, size)
        out[:rows, l * size : (l + 1) * size] = x[:, pl.ds(start, size)]
    row = lax.broadcasted_iota(i32, (rows, width), 0) + scal[0] * rows
    out[rows:, :] = jnp.where(row < scal[1], cotangent[...].astype(f32), 0.0).astype(bf16)


def head_choice(each, shards, position, my_heads, heads):
    h = lax.broadcasted_iota(i32, (my_heads, heads), 0)
    if each:
        shift = each.bit_length() - 1
        head_id = (h >> shift) * (heads // shards) + position * each + (h & (each - 1))
    else:
        head_id = position * my_heads + h
    return (lax.broadcasted_iota(i32, (my_heads, heads), 1) == head_id).astype(f32).astype(bf16)


def bucket_rows(scal, shards, offset):
    row = lax.broadcasted_iota(i32, (bucket_total, offset.shape[1]), 0)
    buckets = bucket_total // shards
    shift = buckets.bit_length() - 1
    bucket_id = jnp.zeros_like(row)
    for l in range(shards):
        bucket_id = jnp.where(
            (row >> shift) == l, scal[2 + l] * buckets + (row & (buckets - 1)), bucket_id
        )
    return (buckets_of(offset) == bucket_id).astype(f32).astype(bf16)


def qkv_kernel(blocks, parts, shards, each, scal, *refs):
    tokens_refs, weights = refs[:blocks], refs[blocks : blocks + parts]
    normed, qkv, bias, gains, scales, joined, small, sems, small_sems = refs[blocks + parts :]
    rows = tokens_refs[0].shape[0]
    tokens, width = normed.shape
    size = width // shards
    stride = sum(w.shape[0] for w in weights) // shards
    places = shard_places(weights, stride)
    step = pl.program_id(0)

    def copy(n, l):
        ref, at = places[l]
        return pltpu.make_async_copy(
            ref.at[pl.ds(at + n * size, size), :],
            joined.at[n, pl.ds(l * size, size), :],
            sems.at[n, l],
        )

    def small_copy(l):
        ref, at = places[l]
        return pltpu.make_async_copy(
            ref.at[pl.ds(at + stride - extra, extra), :], small.at[l], small_sems.at[l]
        )

    @at_step(0)
    def _():
        for l in range(shards):
            small_copy(l).start()
        for n in range(3):
            for l in range(shards):
                copy(n, l).start()
        for l in range(shards):
            small_copy(l).wait()
        my_heads = 2 * bias.shape[0]
        heads = my_heads * blocks
        buckets = bucket_total // shards
        tables = []
        for l in range(shards):
            value = small[l, :, :size].astype(f32)
            gains[:, l * size : (l + 1) * size] = value[:2]
            tables.append(value[2 : 2 + buckets, :heads])
        table = jnp.concatenate(tables, axis=0).astype(bf16)
        chosen = head_choice(each, shards, scal[0], my_heads, heads)
        mine = dot(chosen, table, 1, 1).astype(bf16)
        offset = tokens - lax.broadcasted_iota(i32, (1, 2 * tokens), 1)
        value = dot(mine, bucket_rows(scal, shards, offset))
        for pair in range(bias.shape[0]):
            bias[pair] = value[2 * pair : 2 * pair + 2]
        for t in range(blocks):
            at = slice(t * rows, (t + 1) * rows)
            x = tokens_refs[t][...].astype(f32)
            scale = lax.rsqrt(jnp.mean(x * x, axis=1, keepdims=True) + epsilon)
            normed[at, :] = (x * scale * gains[0:1, :]).astype(bf16)
            scales[at, :] = jnp.broadcast_to(scale, (rows, 128))

    for n in range(3):

        @at_step(n)
        def _():
            for l in range(shards):
                copy(n, l).wait()

    qkv[...] = dot(normed[...], joined[step]).astype(bf16)


def project(scal, tokens_all, weights, shards, each, pairs):
    rows, width = tokens_all[0].shape[0] // 2, tokens_all[0].shape[1]
    blocks = len(tokens_all)
    tokens = rows * blocks
    wide = 128 * pairs
    return call(
        functools.partial(qkv_kernel, blocks, len(weights), shards, each),
        (3,),
        [smem]
        + [pl.BlockSpec((rows, width), lambda n: (0, 0))] * blocks
        + [pl.BlockSpec(memory_space=ANY)] * len(weights),
        [
            pl.BlockSpec((tokens, width), lambda n: (0, 0)),
            pl.BlockSpec((tokens, wide), lambda n: (0, n)),
            pl.BlockSpec((pairs, 2, 2 * tokens), lambda n: (0, 0, 0)),
            pl.BlockSpec((2, width), lambda n: (0, 0)),
            pl.BlockSpec((tokens, 128), lambda n: (0, 0)),
        ],
        [
            struct((tokens, width), bf16),
            struct((tokens, 3 * wide), bf16),
            struct((pairs, 2, 2 * tokens), f32),
            struct((2, width), f32),
            struct((tokens, 128), f32),
        ],
        (scal, *tokens_all, *weights),
        [
            pltpu.VMEM((3, width, wide), bf16),
            pltpu.VMEM((shards, extra, wide), bf16),
            pltpu.SemaphoreType.DMA((3, shards)),
            pltpu.SemaphoreType.DMA((shards,)),
        ],
        flops=6 * tokens * width * wide,
    )


def lanes_of(position, blocks, rows, query, key):
    start = (blocks - 1 + (position ^ query) - (position ^ key)) * rows
    return pl.ds(pl.multiple_of(start, rows), rows)


def forward_kernel(rows, blocks, scal, q_ref, k_ref, v_ref, bias_ref, att, prob, toeplitz):
    position, length = scal[0], scal[1]
    width = 2 * blocks * rows
    slot = lax.broadcasted_iota(i32, (rows, rows), 0)
    for j in range(2):
        row = jnp.broadcast_to(bias_ref[0, j : j + 1, :], (rows, width))
        toeplitz[j] = pltpu.roll(row, width - rows, 1, stride=1, stride_axis=0)
    values = [v_ref[:, 64 * j : 64 * j + 64].astype(f32).T.astype(bf16) for j in range(2)]
    for t in range(blocks):
        at = slice(t * rows, (t + 1) * rows)
        halves = []
        for j in range(2):
            q = q_ref[at, 64 * j : 64 * j + 64]
            k = k_ref[:, 64 * j : 64 * j + 64]
            scores = dot(k, q, 1, 1)
            pieces = []
            for s in range(blocks):
                piece = (
                    scores[s * rows : (s + 1) * rows]
                    + toeplitz[j, :, lanes_of(position, blocks, rows, t, s)]
                )
                live = slot + (position ^ s) * rows < length
                pieces.append(jnp.where(live, piece, masked_score))
            scores = jnp.concatenate(pieces, axis=0)
            top = jnp.max(scores, axis=0, keepdims=True)
            e = jnp.exp(scores - top)
            probs = (e * (1.0 / jnp.sum(e, axis=0, keepdims=True))).astype(bf16)
            prob[j, :, at] = probs
            halves.append(dot(values[j], probs))
        att[at, :] = jnp.concatenate(halves, axis=0).T.astype(bf16)


def backward_kernel(
    rows, blocks, scal, q_ref, k_ref, v_ref, prob, gatt, gq, gk, gv, diag_ref, fold, ds_all
):
    position = scal[0]
    width = 2 * blocks * rows
    grads = [[], [], []]
    for j in range(2):
        columns = slice(64 * j, 64 * j + 64)
        k, v = k_ref[:, columns], v_ref[:, columns]
        fold[...] = jnp.zeros_like(fold)
        for t in range(blocks):
            at = slice(t * rows, (t + 1) * rows)
            gp = dot(v, gatt[at, columns], 1, 1)
            p = prob[j, :, at].astype(f32)
            pg = p * gp
            delta = jnp.sum(pg, axis=0, keepdims=True)
            ds = (pg - p * delta).astype(bf16)
            ds_all[:, at] = ds
            ds = ds.astype(f32)
            for s in range(blocks):
                fold[:, lanes_of(position, blocks, rows, t, s)] += ds[s * rows : (s + 1) * rows]
        grads[0].append(dot(k.astype(f32).T.astype(bf16), ds_all[...]))
        grads[1].append(dot(ds_all[...], q_ref[:, columns]))
        grads[2].append(dot(prob[j], gatt[:, columns]))
        a = fold[...]
        half = rows // 2
        while half >= 8:
            a = a[:half] + pltpu.roll(a[half:], width - half, 1)
            half //= 2
        row = lax.broadcasted_iota(i32, a.shape, 0)
        for bit in (1, 2, 4):
            a = jnp.where((row & bit) != 0, pltpu.roll(a, width - bit, 1), a)
        diag_ref[0, j : j + 1, :] = jnp.sum(a, axis=0, keepdims=True)
    gq[...] = jnp.concatenate(grads[0], axis=0).T.astype(bf16)
    gk[...] = jnp.concatenate(grads[1], axis=1).astype(bf16)
    gv[...] = jnp.concatenate(grads[2], axis=1).astype(bf16)


def attention_forward(scal, qkv, bias, rows, blocks):
    tokens = rows * blocks
    pairs = bias.shape[0]
    return call(
        functools.partial(forward_kernel, rows, blocks),
        (pairs,),
        [smem]
        + [pl.BlockSpec((tokens, 128), lambda p, n=n: (0, n * pairs + p)) for n in range(3)]
        + [pl.BlockSpec((1, 2, 2 * tokens), lambda p: (p, 0, 0))],
        [
            pl.BlockSpec((tokens, 128), lambda p: (0, p)),
            pl.BlockSpec((2, tokens, tokens), lambda p: (p, 0, 0)),
        ],
        [struct((tokens, 128 * pairs), bf16), struct((2 * pairs, tokens, tokens), bf16)],
        (scal, qkv, qkv, qkv, bias),
        [pltpu.VMEM((2, rows, 2 * tokens), f32)],
        flops=8 * pairs * tokens * tokens * 64,
        exps=2 * pairs * tokens * tokens,
    )


def attention_backward(scal, qkv, probs, grad_att, rows, blocks):
    tokens = rows * blocks
    pairs = probs.shape[0] // 2
    block = pl.BlockSpec((tokens, 128), lambda p: (0, p))
    return call(
        functools.partial(backward_kernel, rows, blocks),
        (pairs,),
        [smem]
        + [pl.BlockSpec((tokens, 128), lambda p, n=n: (0, n * pairs + p)) for n in range(3)]
        + [pl.BlockSpec((2, tokens, tokens), lambda p: (p, 0, 0)), block],
        [block, block, block, pl.BlockSpec((1, 2, 2 * tokens), lambda p: (p, 0, 0))],
        [struct((tokens, 128 * pairs), bf16)] * 3 + [struct((pairs, 2, 2 * tokens), f32)],
        (scal, qkv, qkv, qkv, probs, grad_att),
        [pltpu.VMEM((rows, 2 * tokens), f32), pltpu.VMEM((tokens, tokens), bf16)],
        flops=16 * pairs * tokens * tokens * 64,
    )


def out_copies(shards, scal, weights, joined, sems):
    blocks, depth, _ = joined.shape
    size = depth // shards
    stride = sum(w.shape[0] for w in weights) // shards
    first = stride - extra - blocks * size
    copies = []
    for b in range(blocks):
        for l, (ref, at) in enumerate(shard_places(weights, stride)):
            start = pl.multiple_of(scal[2 + l] * size, size)
            copies.append(
                pltpu.make_async_copy(
                    ref.at[pl.ds(at + first + b * size, size), :],
                    joined.at[b, pl.ds(start, size), :],
                    sems.at[b, l],
                )
            )
    return copies


def out_kernel(blocks, parts, shards, scal, att, *refs):
    weights, outs, joined, sems = refs[:parts], refs[parts:-2], refs[-2], refs[-1]
    copies = out_copies(shards, scal, weights, joined, sems)
    for c in copies:
        c.start()
    rows = outs[0].shape[0]
    wide = joined.shape[2]
    for b in range(joined.shape[0]):
        for c in copies[b * shards : (b + 1) * shards]:
            c.wait()
        total = dot(att[...], joined[b]).astype(bf16)
        for t in range(blocks):
            outs[t][:, b * wide : (b + 1) * wide] = total[t * rows : (t + 1) * rows]


def multiply_out(scal, att, weights, shards, blocks):
    tokens, wide = att.shape
    rows, width = tokens // blocks, wide * blocks
    return call(
        functools.partial(out_kernel, blocks, len(weights), shards),
        (1,),
        [smem, whole(att)] + [pl.BlockSpec(memory_space=ANY)] * len(weights),
        [pl.BlockSpec((rows, width), lambda i: (0, 0))] * blocks,
        [struct((rows, width), bf16)] * blocks,
        (scal, att, *weights),
        [pltpu.VMEM((blocks, wide, wide), bf16), pltpu.SemaphoreType.DMA((blocks, shards))],
        flops=2 * tokens * wide * width,
    )


def grad_attended_kernel(blocks, parts, shards, scal, *refs):
    low, weights = refs[:blocks], refs[blocks : blocks + parts]
    out, joined, sems = refs[blocks + parts :]
    copies = out_copies(shards, scal, weights, joined, sems)
    for c in copies:
        c.start()
    wide = joined.shape[2]
    total = None
    for b in range(joined.shape[0]):
        for c in copies[b * shards : (b + 1) * shards]:
            c.wait()
        part = jnp.concatenate([ref[:, b * wide : (b + 1) * wide] for ref in low], axis=0)
        term = dot(part, joined[b], 1, 1)
        total = term if total is None else total + term
    out[...] = total.astype(bf16)


def make_grad_attended(scal, low_all, weights, shards):
    blocks = len(low_all)
    rows, width = low_all[0].shape
    tokens, wide = rows * blocks, width // blocks
    return call(
        functools.partial(grad_attended_kernel, blocks, len(weights), shards),
        (1,),
        [smem] + [whole(a) for a in low_all] + [pl.BlockSpec(memory_space=ANY)] * len(weights),
        [pl.BlockSpec((tokens, wide), lambda i: (0, 0))],
        [struct((tokens, wide), bf16)],
        (scal, *low_all, *weights),
        [pltpu.VMEM((blocks, wide, wide), bf16), pltpu.SemaphoreType.DMA((blocks, shards))],
        flops=2 * tokens * wide * width,
    )[0]


def hidden_kernel(blocks, shards, scal, x, gains, *refs):
    parts, hidden, nffn = refs[:blocks], refs[blocks], refs[blocks + 1]
    total = x[...].astype(f32)
    for part in parts:
        total = total + part[...].astype(f32)
    hidden[...] = total
    scale = lax.rsqrt(jnp.mean(total * total, axis=1, keepdims=True) + epsilon)
    size = total.shape[1] // shards
    for l in range(shards):
        at = slice(l * size, (l + 1) * size)
        start = pl.multiple_of(scal[2 + l] * size, size)
        nffn[:, at] = (hidden[:, pl.ds(start, size)] * scale * gains[1:2, at]).astype(bf16)


def make_hidden(scal, x, gains, parts, shards):
    rows, width = x.shape
    args = (scal, x, gains, *parts)
    return call(
        functools.partial(hidden_kernel, len(parts), shards),
        (1,),
        [smem] + [whole(a) for a in args[1:]],
        [pl.BlockSpec((rows, width), lambda i: (0, 0))] * 2,
        [struct((rows, width), f32), struct((rows, width), bf16)],
        args,
    )


def gelu_tanh(g):
    return jnp.tanh(0.7978845608028654 * (g + 0.044715 * (g * g * g)))


def units_kernel(blocks, parts, tile, *refs):
    tokens_refs, weights = refs[:blocks], refs[blocks : blocks + parts]
    normed, gate, up, mixed, joined, sems = refs[blocks + parts :]
    rows = tokens_refs[0].shape[0]
    units = weights[0].shape[1] // 2
    step = pl.program_id(0)

    def copies(i):
        result, at = [], 0
        for w, ref in enumerate(weights):
            for n in range(2):
                result.append(
                    pltpu.make_async_copy(
                        ref.at[:, pl.ds(n * units + i * tile, tile)],
                        joined.at[i, pl.ds(at, ref.shape[0]), pl.ds(n * tile, tile)],
                        sems.at[i, 2 * w + n],
                    )
                )
            at += ref.shape[0]
        return result

    @at_step(0)
    def _():
        for i in range(units // tile):
            for c in copies(i):
                c.start()
        for t in range(blocks):
            normed[t * rows : (t + 1) * rows, :] = tokens_refs[t][...]

    for i in range(units // tile):

        @at_step(i)
        def _():
            for c in copies(i):
                c.wait()

    both = dot(normed[...], joined[step])
    g, u = both[:, :tile], both[:, tile:]
    gate[...] = g
    up[...] = u
    mixed[...] = (0.5 * g * (1.0 + gelu_tanh(g)) * u).astype(bf16)


def make_units(tokens_all, weights):
    rows, width = tokens_all[0].shape
    blocks = len(tokens_all)
    tokens = rows * blocks
    units = weights[0].shape[1] // 2
    tile = tile_of(units, 256)
    steps = units // tile
    out = pl.BlockSpec((tokens, tile), lambda i: (0, i))
    return call(
        functools.partial(units_kernel, blocks, len(weights), tile),
        (steps,),
        [whole(a) for a in tokens_all] + [pl.BlockSpec(memory_space=ANY)] * len(weights),
        [pl.BlockSpec((tokens, width), lambda i: (0, 0)), out, out, out],
        [
            struct((tokens, width), bf16),
            struct((tokens, units), f32),
            struct((tokens, units), f32),
            struct((tokens, units), bf16),
        ],
        (*tokens_all, *weights),
        [
            pltpu.VMEM((steps, width, 2 * tile), bf16),
            pltpu.SemaphoreType.DMA((steps, 2 * len(weights))),
        ],
        flops=4 * tokens * width * units,
    )


def grad_down_kernel(blocks, shards, scal, mixed, *refs):
    dy, outs, turned, low = refs[:blocks], refs[blocks:-2], refs[-2], refs[-1]

    @at_step(0)
    def _():
        turned[...] = mixed[...].T

    low[...] = dot(turned[...], jnp.concatenate([r[...] for r in dy], axis=0)).astype(bf16)
    size = low.shape[0] // shards
    each = shards // len(outs)
    for l in range(shards):
        start = pl.multiple_of(scal[2 + l] * size, size)
        outs[side_of(shards)[l][0]][pl.ds(side_of(shards)[l][1] * size, size), :] = low[
            pl.ds(start, size), :
        ]


def side_of(shards):
    chips = shards // 2
    sides, counts = [], [0, 0]
    for slots in (near_slots(chips), far_slots(chips)):
        for p in range(2):
            for _ in slots:
                sides.append((p, counts[p]))
                counts[p] += 1
    return sides


def make_grad_down(scal, mixed, tokens_all, shards):
    blocks = len(tokens_all)
    tokens, units = mixed.shape
    rows, width = tokens // blocks, tokens_all[0].shape[1]
    tile = tile_of(width, 512)
    return call(
        functools.partial(grad_down_kernel, blocks, shards),
        (width // tile,),
        [smem, whole(mixed)] + [pl.BlockSpec((rows, tile), lambda i: (1, i))] * blocks,
        [pl.BlockSpec((units // 2, tile), lambda i: (0, i))] * 2,
        [struct((units // 2, width), bf16)] * 2,
        (scal, mixed, *tokens_all),
        [pltpu.VMEM((units, tokens), bf16), pltpu.VMEM((units, tile), bf16)],
        flops=2 * tokens * units * width,
    )


def down_copies(shards, scal, weights, joined, sems):
    size = joined.shape[0] // shards
    copies = []
    for l, (ref, at) in enumerate(shard_places(weights, size)):
        start = pl.multiple_of(scal[2 + l] * size, size) if shards > 1 else 0
        copies.append(
            pltpu.make_async_copy(
                ref.at[pl.ds(at, size), :], joined.at[pl.ds(start, size), :], sems.at[l]
            )
        )
    return copies


def units_back_kernel(blocks, parts, shards, tile, scal, gate, up, *refs):
    dy, weights = refs[:blocks], refs[blocks : blocks + parts]
    out, joined, grads, sems = refs[blocks + parts :]
    step = pl.program_id(0)
    rows = dy[0].shape[0]
    units = joined.shape[0]

    @at_step(0)
    def _():
        copies = down_copies(shards, scal, weights, joined, sems)
        for c in copies:
            c.start()
        for t in range(blocks):
            grads[t * rows : (t + 1) * rows, :] = dy[t][...]
        for c in copies:
            c.wait()

    weight = joined[pl.ds(pl.multiple_of(step * tile, tile), tile), :]
    grad = dot(grads[...], weight, 1, 1)
    g, u = gate[...], up[...]
    t = gelu_tanh(g)
    slope = 0.5 * (1.0 + t) + 0.5 * g * (1.0 - t * t) * (
        0.7978845608028654 * (1.0 + 3 * 0.044715 * (g * g))
    )
    out[:, pl.ds(pl.multiple_of(step * tile, tile), tile)] = (grad * u * slope).astype(bf16)
    out[:, pl.ds(pl.multiple_of(units + step * tile, tile), tile)] = (
        grad * (0.5 * g * (1.0 + t))
    ).astype(bf16)


def units_back(scal, gate, up, tokens_all, weights, shards):
    blocks = len(tokens_all)
    tokens, units = gate.shape
    rows, width = tokens // blocks, tokens_all[0].shape[1]
    tile = tile_of(units, 256)
    block = pl.BlockSpec((tokens, tile), lambda i: (0, i))
    return call(
        functools.partial(units_back_kernel, blocks, len(weights), shards, tile),
        (units // tile,),
        [smem, block, block]
        + [pl.BlockSpec((rows, width), lambda i: (1, 0))] * blocks
        + [pl.BlockSpec(memory_space=ANY)] * len(weights),
        [pl.BlockSpec((tokens, 2 * units), lambda i: (0, 0))],
        [struct((tokens, 2 * units), bf16)],
        (scal, gate, up, *tokens_all, *weights),
        [
            pltpu.VMEM((units, width), bf16),
            pltpu.VMEM((tokens, width), bf16),
            pltpu.SemaphoreType.DMA((shards,)),
        ],
        flops=2 * tokens * units * width,
    )[0]


def result_kernel(blocks, parts, shards, tile, scal, mixed, *refs):
    weights, outs, joined, sems = refs[:parts], refs[parts:-2], refs[-2], refs[-1]
    start_and_wait(down_copies(shards, scal, weights, joined, sems))
    rows, width = outs[0].shape
    for i in range(width // tile):
        at = slice(i * tile, (i + 1) * tile)
        total = dot(mixed[...], joined[:, at]).astype(bf16)
        for t in range(blocks):
            outs[t][:, at] = total[t * rows : (t + 1) * rows]


def multiply_down(scal, mixed, weights, shards, blocks):
    tokens, units = mixed.shape
    width = weights[0].shape[1]
    rows = tokens // blocks
    return call(
        functools.partial(result_kernel, blocks, len(weights), shards, tile_of(width, 512)),
        (1,),
        [smem, whole(mixed)] + [pl.BlockSpec(memory_space=ANY)] * len(weights),
        [pl.BlockSpec((rows, width), lambda i: (0, 0))] * blocks,
        [struct((rows, width), bf16)] * blocks,
        (scal, mixed, *weights),
        [pltpu.VMEM((units, width), bf16), pltpu.SemaphoreType.DMA((shards,))],
        flops=2 * tokens * units * width,
    )


def ffn_transposed_kernel(parts, blocks, g, *refs):
    weights, outs = refs[:parts], refs[parts : parts + blocks]
    held, sems = refs[parts + blocks : -1], refs[-1]
    rows = outs[0].shape[0]
    copies = [pltpu.make_async_copy(w, h, sems.at[i]) for i, (w, h) in enumerate(zip(weights, held))]
    order = sorted(range(parts), key=lambda i: held[i].shape[0])
    first = [sum(h.shape[0] for h in held[:i]) for i in range(parts)]
    for i in order:
        copies[i].start()
    for i in order:
        copies[i].wait()
        tile = held[i].shape[0] if held[i].shape[0] <= 768 else tile_of(held[i].shape[0], 512)
        for n in range(0, held[i].shape[0], tile):
            total = dot(g[...], held[i][n : n + tile, :], 1, 1).astype(bf16)
            at = first[i] + n
            for t, out in enumerate(outs):
                out[:, at : at + tile] = total[t * rows : (t + 1) * rows]


def ffn_transposed(g, weights, blocks):
    tokens, depth = g.shape
    rows, width = tokens // blocks, sum(w.shape[0] for w in weights)
    return call(
        functools.partial(ffn_transposed_kernel, len(weights), blocks),
        (1,),
        [whole(g)] + [pl.BlockSpec(memory_space=ANY)] * len(weights),
        [pl.BlockSpec((rows, width), lambda i: (0, 0))] * blocks,
        [struct((rows, width), bf16)] * blocks,
        (g, *weights),
        [pltpu.VMEM(w.shape, bf16) for w in weights]
        + [pltpu.SemaphoreType.DMA((len(weights),))],
        flops=2 * tokens * depth * width,
    )


def units_grad_kernel(shards, scal, normed, g, *refs):
    outs, turned = refs[:-1], refs[-1]

    @at_step(0)
    def _():
        turned[...] = normed[...].T

    total = dot(turned[...], g[...]).astype(bf16)
    at = 0
    for out in outs[:2]:
        n = out.shape[0]
        out[...] = total[at : at + n]
        at += n
    if len(outs) == 3:
        size = outs[2].shape[0] // 2
        core = scal[2] & 1
        for n, place in enumerate((core, 1 - core)):
            start = pl.multiple_of(place * size, size)
            outs[2][pl.ds(start, size), :] = total[at + n * size : at + (n + 1) * size]


def units_grad(scal, normed, g, shards):
    tokens, depth = normed.shape
    width = g.shape[1]
    tile = tile_of(width, 512)
    size = depth // shards
    sizes = [len(near_slots(shards // 2)) * size] * 2
    if far_slots(shards // 2):
        sizes.append(2 * size)
    return call(
        functools.partial(units_grad_kernel, shards),
        (width // tile,),
        [smem, whole(normed), pl.BlockSpec((tokens, tile), lambda i: (0, i))],
        [pl.BlockSpec((n, tile), lambda i: (0, i)) for n in sizes],
        [struct((n, width), bf16) for n in sizes],
        (scal, normed, g),
        [pltpu.VMEM((depth, tokens), bf16)],
        flops=2 * tokens * depth * width,
    )


def attn_transposed_kernel(blocks, parts, shards, scales, gq, gk, gv, *refs):
    tokens_refs, weights = refs[:blocks], refs[blocks : blocks + parts]
    outs = refs[blocks + parts : 2 * blocks + parts]
    gain, held, sems = refs[2 * blocks + parts :]
    rows, size = outs[0].shape
    stride = sum(w.shape[0] for w in weights) // shards
    step = pl.program_id(0)

    def copy(l):
        ref, at = shard_places(weights, stride)[l]
        return pltpu.make_async_copy(ref.at[pl.ds(at, 3 * size), :], held.at[l], sems.at[l])

    @at_step(0)
    def _():
        for l in range(shards):
            copy(l).start()

    for l in range(shards):

        @at_step(l)
        def _():
            copy(l).wait()

    total = None
    for n, g in enumerate((gq, gk, gv)):
        term = dot(g[...], held[step, n * size : (n + 1) * size, :], 1, 1)
        total = term if total is None else total + term
    summed = jnp.zeros((1, size), f32)
    for t, out in enumerate(outs):
        at = slice(t * rows, (t + 1) * rows)
        out[...] = total[at].astype(bf16)
        unit = tokens_refs[t][...].astype(f32) * scales[at, 0:1]
        summed = summed + jnp.sum(total[at] * unit, axis=0, keepdims=True)
    gain[...] = summed


def attn_transposed(scales, grads, tokens_all, weights, size, shards, blocks):
    tokens, wide = grads[0].shape
    rows, width = tokens // blocks, size * shards
    tile = pl.BlockSpec((rows, size), lambda l: (0, l))
    results = call(
        functools.partial(attn_transposed_kernel, blocks, len(weights), shards),
        (shards,),
        [whole(scales)]
        + [whole(g) for g in grads]
        + [tile] * blocks
        + [pl.BlockSpec(memory_space=ANY)] * len(weights),
        [tile] * blocks + [pl.BlockSpec((1, size), lambda l: (0, l))],
        [struct((rows, width), bf16)] * blocks + [struct((1, width), f32)],
        (scales, *grads, *tokens_all, *weights),
        [
            pltpu.VMEM((shards, 3 * size, wide), bf16),
            pltpu.SemaphoreType.DMA((shards,)),
        ],
        flops=6 * tokens * wide * width,
    )
    return results[:-1], results[-1]


def split_low(a):
    high = a.astype(bf16)
    return high, (a - high.astype(f32)).astype(bf16)


def owner_counts(shards):
    counts = []
    for slots in (near_slots(shards // 2), far_slots(shards // 2)):
        if slots:
            counts += [len(slots)] * 2
    return counts


def shard_owners(outs, shards):
    return [out for out, n in zip(outs, owner_counts(shards)) for _ in range(n)]


def attn_grad_kernel(
    blocks, shards, each, with_out, scal, normed, att, gq, gk, gv, diag, gain_attn, gain_ffn, *refs
):
    low = refs[:blocks]
    outs, (joined, turned, table) = refs[blocks:-3], refs[-3:]
    tokens, width = normed.shape
    wide = att.shape[1]
    size = width // shards
    head_rows = wide // shards
    rows = tokens // blocks
    my_heads = 2 * diag.shape[0]
    heads = my_heads * blocks

    @at_step(0)
    def _():
        for n, g in enumerate((gq, gk, gv)):
            joined[:, n * wide : (n + 1) * wide] = g[...]
        if with_out:
            turned[...] = dot(
                att[...].T, jnp.concatenate([r[...] for r in low], axis=0)
            ).astype(bf16)
        lane = lax.broadcasted_iota(i32, (1, 2 * tokens), 1)
        lane = jnp.where(lane < 2 * tokens - rows, lane, lane - 2 * tokens)
        of_offset = bucket_rows(scal, shards, (blocks - 1) * rows - lane)
        sums = jnp.concatenate([diag[p] for p in range(diag.shape[0])], axis=0)
        total = None
        for part in split_low(sums):
            term = dot(of_offset, part, 1, 1)
            total = term if total is None else total + term
        chosen = head_choice(each, shards, scal[0], my_heads, heads)
        value = None
        for part in split_low(total):
            term = dot(part, chosen)
            value = term if value is None else value + term
        table[...] = value

    buckets = bucket_total // shards
    for l, out in enumerate(shard_owners(outs, shards)):

        @at_step(l)
        def _():
            total = dot(normed[:, l * size : (l + 1) * size], joined[...], 0, 0).astype(bf16)
            for n in range(3):
                out[n * size : (n + 1) * size, :] = total[:, n * wide : (n + 1) * wide]
            if with_out:
                start = pl.multiple_of(scal[2 + l] * head_rows, head_rows)
                for b in range(blocks):
                    out[3 * size + b * head_rows : 3 * size + (b + 1) * head_rows, :] = turned[
                        pl.ds(start, head_rows), b * wide : (b + 1) * wide
                    ]
            part = jnp.concatenate(
                [
                    jnp.zeros((2, heads), f32),
                    table[l * buckets : (l + 1) * buckets, :],
                    jnp.zeros((extra - 2 - buckets, heads), f32),
                ],
                axis=0,
            )
            part = jnp.concatenate([part, jnp.zeros((extra, size - heads), f32)], axis=1)
            row = lax.broadcasted_iota(i32, (extra, size), 0)
            columns = slice(l * size, (l + 1) * size)
            part = part + jnp.where(
                row == 0,
                gain_attn[:, columns],
                jnp.where(row == 1, gain_ffn[:, columns], 0.0),
            )
            last = out.shape[0] - extra
            out[last:, :] = jnp.zeros((extra, wide), bf16)
            out[last:, :size] = part.astype(bf16)


def attn_grad(scal, normed, att, grads, diag, gain_attn, gain_ffn, low_all, shards, each, stride):
    tokens, width = normed.shape
    wide = att.shape[1]
    blocks = len(low_all)
    counts = owner_counts(shards)
    specs, first = [], 0
    for n in counts:
        specs.append(
            pl.BlockSpec((stride, wide), lambda l, f=first, n=n: (jnp.clip(l - f, 0, n - 1), 0))
        )
        first += n
    args = (scal, normed, att, *grads, diag, gain_attn, gain_ffn, *low_all)
    return call(
        functools.partial(attn_grad_kernel, blocks, shards, each, bool(each)),
        (shards,),
        [smem] + [whole(a) for a in args[1:]],
        specs,
        [struct((n * stride, wide), bf16) for n in counts],
        args,
        [
            pltpu.VMEM((tokens, 3 * wide), bf16),
            pltpu.VMEM((wide, width), bf16),
            pltpu.VMEM((bucket_total, 2 * diag.shape[0] * blocks), f32),
        ],
        flops=8 * tokens * wide * width,
    )


def ffn_norm_back_kernel(blocks, shards, scal, hidden, gains, own, *refs):
    parts = refs[:blocks]
    grad_hidden, low, grad_gain, g, gain = refs[blocks:]
    size = hidden.shape[1] // shards
    for l in range(shards):
        at = slice(l * size, (l + 1) * size)
        start = pl.multiple_of(scal[2 + l] * size, size)
        total = parts[0][:, at].astype(f32)
        for part in parts[1:]:
            total = total + part[:, at].astype(f32)
        g[:, pl.ds(start, size)] = total
        gain[:, pl.ds(start, size)] = gains[1:2, at]
    h = hidden[...]
    scale = lax.rsqrt(jnp.mean(h * h, axis=1, keepdims=True) + epsilon)
    weighted = g[...] * gain[...]
    inner = jnp.mean(weighted * h, axis=1, keepdims=True)
    value = own[...].astype(f32) + scale * weighted - h * (scale * scale * scale) * inner
    grad_hidden[...] = value
    low[...] = value.astype(bf16)
    g[...] = g[...] * h * scale
    for l in range(shards):
        start = pl.multiple_of(scal[2 + l] * size, size)
        grad_gain[:, l * size : (l + 1) * size] = jnp.sum(
            g[:, pl.ds(start, size)], axis=0, keepdims=True
        )


def ffn_norm_back(scal, hidden, gains, own, parts, shards):
    rows, width = hidden.shape
    block = pl.BlockSpec((rows, width), lambda i: (0, 0))
    return call(
        functools.partial(ffn_norm_back_kernel, len(parts), shards),
        (1,),
        [smem, block, whole(gains), pl.BlockSpec((rows, width), lambda i: (1, 0))]
        + [block] * len(parts),
        [block, block, pl.BlockSpec((1, width), lambda i: (0, 0))],
        [struct((rows, width), f32), struct((rows, width), bf16), struct((1, width), f32)],
        (scal, hidden, gains, own, *parts),
        [pltpu.VMEM((rows, width), f32), pltpu.VMEM((1, width), f32)],
    )


def attn_norm_back_kernel(blocks, shards, scal, grad_hidden, gains, own, *refs):
    parts = refs[:blocks]
    grad, value = refs[blocks:]
    x = own[...].astype(f32)
    g = parts[0][...].astype(f32)
    for part in parts[1:]:
        g = g + part[...].astype(f32)
    scale = lax.rsqrt(jnp.mean(x * x, axis=1, keepdims=True) + epsilon)
    weighted = g * gains[0:1, :]
    inner = jnp.mean(weighted * x, axis=1, keepdims=True)
    value[...] = scale * weighted - x * (scale * scale * scale) * inner
    size = x.shape[1] // shards
    for l in range(shards):
        at = slice(l * size, (l + 1) * size)
        where = pl.ds(pl.multiple_of(scal[2 + l] * size, size), size)
        grad[:, where] = (grad_hidden[:, where] + value[:, at]).astype(bf16)


def attn_norm_back(scal, grad_hidden, gains, own, parts, shards):
    rows, width = grad_hidden.shape
    block = pl.BlockSpec((rows, width), lambda i: (0, 0))
    return call(
        functools.partial(attn_norm_back_kernel, len(parts), shards),
        (1,),
        [smem, block, whole(gains), block] + [block] * len(parts),
        [block],
        [struct((rows, width), bf16)],
        (scal, grad_hidden, gains, own, *parts),
        [pltpu.VMEM((rows, width), f32)],
    )[0]


def by_position(scal, blocks, body):
    for p in range(blocks):

        @pl.when(scal[0] == p)
        def _():
            body([p ^ c for c in range(blocks)])


def columns_kernel(groups, scal, *refs):
    pieces, outs = refs[:-2], refs[-2:]
    blocks = len(pieces)
    units = pieces[0].shape[1] // 2
    size = units // groups
    wide = blocks * size

    def body(order):
        for n, out in enumerate(outs):
            for g in range(groups):
                at = n * units + g * size
                out[:, g * wide : (g + 1) * wide] = jnp.concatenate(
                    [pieces[t][:, at : at + size] for t in order], axis=1
                ).astype(f32)

    by_position(scal, blocks, body)


def assemble_units(scal, pieces, groups):
    rows, columns = pieces[0].shape
    tile = min(rows, 32)
    wide = len(pieces) * columns // 2
    return call(
        functools.partial(columns_kernel, groups),
        (rows // tile,),
        [smem] + [pl.BlockSpec((tile, columns), lambda i: (i, 0))] * len(pieces),
        [pl.BlockSpec((tile, wide), lambda i: (i, 0))] * 2,
        [struct((rows, wide), f32)] * 2,
        (scal, *pieces),
    )


def rows_kernel(size, scal, *refs):
    position = scal[0]
    for t, piece in enumerate(refs[:-1]):
        start = pl.multiple_of((position ^ t) * size, 8)
        refs[-1][pl.ds(start, size), :] = piece[...].astype(f32)


def assemble_rows(scal, pieces):
    rows, columns = pieces[0].shape
    tile = tile_of(columns, 512)
    return call(
        functools.partial(rows_kernel, rows),
        (columns // tile,),
        [smem] + [pl.BlockSpec((rows, tile), lambda i: (0, i))] * len(pieces),
        [pl.BlockSpec((rows * len(pieces), tile), lambda i: (0, i))],
        [struct((rows * len(pieces), columns), f32)],
        (scal, *pieces),
    )[0]


def attention_outputs_kernel(each, blocks, head_width, count, last, scal, *refs):
    columns, rest = refs[: count * blocks], refs[count * blocks :]
    with_out = last and bool(each)
    out_blocks = rest[:blocks] if with_out else ()
    rest = rest[blocks:] if with_out else rest
    small, outs = (rest[:blocks], rest[blocks:]) if last else ((), rest)
    wide = columns[0].shape[1]
    step = pl.program_id(0)

    def body(order):
        for n in range(count):
            pieces = [columns[count * t + n] for t in order]
            if each:
                size = each * head_width
                for g in range(wide // size):
                    outs[n][:, g * blocks * size : (g + 1) * blocks * size] = jnp.concatenate(
                        [ref[:, g * size : (g + 1) * size] for ref in pieces], axis=1
                    ).astype(f32)
            else:
                for c, ref in enumerate(pieces):
                    outs[n][:, c * wide : (c + 1) * wide] = ref[...].astype(f32)

        if last:

            @at_step(0)
            def _():
                total = small[order[0]][...].astype(f32)
                for t in order[1:]:
                    total = total + small[t][...].astype(f32)
                outs[-1][...] = total

    by_position(scal, blocks, body)
    if with_out:
        for t in range(blocks):

            @pl.when((step ^ scal[0]) == t)
            def _():
                size = outs[count].shape[0]
                for b in range(blocks):
                    outs[count][:, b * wide : (b + 1) * wide] = out_blocks[t][
                        b * size : (b + 1) * size, :
                    ].astype(f32)


def attention_outputs(scal, pieces, count, rows, each, head_width, last):
    blocks = len(pieces)
    total, wide = pieces[0].shape
    tile = rows // blocks
    per = rows // tile
    specs, args = [], []
    for a in pieces:
        for n in range(count):
            specs.append(pl.BlockSpec((tile, wide), lambda i, n=n: (n * per + i, 0)))
            args.append(a)
    outputs = count
    if last and each:
        specs += [pl.BlockSpec((rows, wide), lambda i: (count, 0))] * blocks
        args += pieces
        outputs += 1
    if last:
        specs += [pl.BlockSpec((extra, wide), lambda i: (total // extra - 1, 0))] * blocks
        args += pieces
    block = pl.BlockSpec((tile, wide * blocks), lambda i: (i, 0))
    out_specs, out_shape = [block] * outputs, [struct((rows, wide * blocks), f32)] * outputs
    if last:
        out_specs.append(pl.BlockSpec((extra, wide), lambda i: (0, 0)))
        out_shape.append(struct((extra, wide), f32))
    return call(
        functools.partial(attention_outputs_kernel, each, blocks, head_width, count, last),
        (blocks,),
        [smem] + specs,
        out_specs,
        out_shape,
        (scal, *args),
    )


def take_blocks(a, starts, size):
    return jnp.concatenate([lax.dynamic_slice_in_dim(a, s, size, 0) for s in starts], 0)


def on_device(
    inputs,
    lengths,
    w_query,
    w_key,
    w_value,
    w_out,
    w_gate,
    w_up,
    w_down,
    norm_attn,
    norm_ffn,
    relative_bias_table,
    cotangent,
):
    blocks = lax.axis_size("ctx")
    shards = lax.axis_size("fsdp")
    chips = shards // 2
    position = lax.axis_index("ctx")
    shard = lax.axis_index("fsdp")
    chip, core = shard // 2, shard % 2
    rows, width = inputs.shape[1], inputs.shape[2]
    tokens = rows * blocks
    heads = relative_bias_table.shape[1]
    head_width = width // heads
    my_heads = heads // blocks
    pairs = my_heads // 2
    each = heads // shards // blocks if (heads // shards) % blocks == 0 else 0
    strided = each in (1, 2)
    each = each if strided else 0
    units = w_gate.shape[1] // blocks
    shard_rows = width // shards
    unit_rows = w_down.shape[0] // blocks

    slot_of, parity_of = [], []
    for slots in (near_slots(chips), far_slots(chips)):
        for p in range(2):
            slot_of += slots
            parity_of += [p] * len(slots)
    pad = [0, 0]
    order = 2 * ((chip + jnp.array(pad + slot_of, i32)) % chips) + (
        core ^ jnp.array(pad + parity_of, i32)
    )
    index = jnp.arange(shards + 2, dtype=i32)
    scal = jnp.where(index == 0, position, jnp.where(index == 1, lengths[0], order)).astype(i32)

    def heads_of(c):
        if strided:
            return [
                (h // each) * (heads // shards) + c * each + h % each for h in range(my_heads)
            ]
        return [c * my_heads + h for h in range(my_heads)]

    args = (
        scal,
        w_query,
        w_key,
        w_value,
        w_out,
        norm_attn.reshape(1, -1),
        norm_ffn.reshape(1, -1),
        relative_bias_table,
    )
    stride = (4 if strided else 3) * shard_rows + extra
    own_attn = call(
        functools.partial(
            choose_attention_kernel, [heads_of(c) for c in range(blocks)], head_width, strided
        ),
        (1,),
        [smem] + [whole(a) for a in args[1:]],
        [pl.BlockSpec((stride, 128 * pairs), lambda i: (0, 0))],
        [struct((stride, 128 * pairs), bf16)],
        args,
    )[0]
    near_attn = gather_near(own_attn)
    own_tokens = call(
        functools.partial(tokens_kernel, shards),
        (1,),
        [smem] + [pl.BlockSpec((rows, width), lambda i: (0, 0))] * 2,
        [pl.BlockSpec((2 * rows, width), lambda i: (0, 0))],
        [struct((2 * rows, width), bf16)],
        (after(scal, own_attn), inputs[0], cotangent[0]),
    )[0]
    all_tokens = ctx_gather(own_tokens)
    tile = tile_of(shard_rows, 64)
    own_gate_up = call(
        functools.partial(choose_units_kernel, shards),
        (shard_rows // tile,),
        [smem] + [pl.BlockSpec((tile, w_gate.shape[1]), lambda i: (i, 0))] * 2,
        [pl.BlockSpec((tile, 2 * units), lambda i: (i, 0))],
        [struct((shard_rows, 2 * units), bf16)],
        (after(scal, own_tokens), w_gate, w_up),
    )[0]
    joint = together([*near_attn, *all_tokens], own_gate_up)
    near_attn, all_tokens = joint[: len(near_attn)], joint[len(near_attn) :]
    far_attn = gather_far(near_attn, chip)
    n = len(near_attn)
    joint = together([core_swap(a) for a in near_attn] + far_attn)
    weights_attn, far_attn = [*near_attn, *joint[:n]], joint[n:]
    near_gate_up = gather_near(after(own_gate_up, *far_attn))
    weights_attn += with_other_core(far_attn)
    if not strided:
        gathered = lax.all_gather(w_out, "fsdp", axis=0, tiled=True)
        size = my_heads * head_width
        full_out = lax.dynamic_slice_in_dim(gathered, position * size, size, 0)

    normed, qkv, bias, gains, scales = project(
        scal, all_tokens, weights_attn, shards, each, pairs
    )
    attended, probs = attention_forward(scal, qkv, bias, rows, blocks)
    if strided:
        parts = multiply_out(scal, attended, weights_attn, shards, blocks)
    else:
        whole_part = dot(attended, full_out).astype(bf16)
        parts = [whole_part[t * rows : (t + 1) * rows] for t in range(blocks)]
    parts = ctx_exchange(parts)
    hidden, own_nffn = make_hidden(scal, inputs[0], gains, parts, shards)

    near_gate_up = together(near_gate_up, own_nffn)
    far_gate_up = gather_far(near_gate_up, chip)
    joint = together(with_other_core(near_gate_up) + ctx_gather(own_nffn) + far_gate_up)
    weights_gate_up = list(joint[:2])
    all_nffn, far_gate_up = joint[2 : 2 + blocks], joint[2 + blocks :]
    own_down = lax.dynamic_slice_in_dim(w_down, position * unit_rows, unit_rows, 0)
    near_down = gather_near(after(own_down, all_nffn[0]))
    weights_gate_up += with_other_core(far_gate_up)
    normed_ffn, gate, up, mixed_units = make_units(all_nffn, weights_gate_up)

    aligned = unit_rows % 16 == 0
    if aligned:
        grads_down = make_grad_down(scal, mixed_units, all_tokens, shards)
    else:
        all_dy = jnp.concatenate([a[rows:] for a in all_tokens], axis=0)
        grad_down = dot(mixed_units, all_dy, 0, 0).astype(bf16)
        grads_down = [
            take_blocks(
                grad_down,
                [order[2 + l] * unit_rows for l in range(shards) if parity_of[l] == side],
                unit_rows,
            )
            for side in range(2)
        ]
    joint = together([*near_down, *grads_down])
    near_down, grads_down = joint[:-2], joint[-2:]
    far_down = gather_far(near_down, chip)
    sums_down = core_sum(*grads_down)
    joint = together(with_other_core(near_down) + far_down, *sums_down)
    down_parts, far_down = list(joint[:2]), joint[2:]
    down_parts, down_shards = down_parts + with_other_core(far_down), shards
    if not aligned:
        joined = jnp.concatenate(down_parts, axis=0)
        place = jnp.argsort(order[2:])
        down_parts = [take_blocks(joined, [place[r] * unit_rows for r in range(shards)], unit_rows)]
        down_shards = 1

    far_sum = None
    if len(sums_down) == 2:
        far_sum = reduce_far(after(sums_down[0], *far_down))
    grad_units = units_back(scal, gate, up, all_tokens, down_parts, down_shards)
    if far_sum is not None:
        far_sum, grad_units = together([far_sum, grad_units])
    sends, kept = near_sends(sums_down[-1], far_sum, chip)
    sends = together(sends, grad_units)
    received = near_receive(sends)
    parts = ffn_transposed(after(grad_units, *sends), weights_gate_up, blocks)
    grads_gate_up = units_grad(scal, normed_ffn, after(grad_units, *parts), shards)
    parts = ctx_exchange(parts)
    n = len(received)
    joint = together([*received, *grads_gate_up])
    received, grads_gate_up = joint[:n], joint[n:]
    far_sum, far_add = [], grads_gate_up[0]
    if len(grads_gate_up) == 3:
        both = core_exchange(grads_gate_up[2])
        far_add = add_low(both[:shard_rows], both[shard_rows:])
        far_sum = [reduce_far(far_add)]
    share_down = near_total(received, kept, chip)
    parts = together(parts, far_add)
    grad_hidden, low, grad_gain_ffn = ffn_norm_back(
        scal, hidden, gains, own_tokens, parts, shards
    )

    all_low = ctx_gather(low)
    near_sum = add_low(grads_gate_up[0], core_swap(after(grads_gate_up[1], low)))
    result_parts = multiply_down(
        scal, after(mixed_units, near_sum), down_parts, down_shards, blocks
    )
    sends, kept = near_sends(near_sum, far_sum[0] if far_sum else None, chip)
    received = near_receive(sends)
    result_parts = ctx_exchange(together(result_parts, *all_low))
    if strided:
        grad_att = make_grad_attended(after(scal, *sends), all_low, weights_attn, shards)
    else:
        grad_att = dot(jnp.concatenate(all_low, axis=0), full_out, 1, 1).astype(bf16)
    *grads, diagonals = attention_backward(scal, qkv, probs, grad_att, rows, blocks)
    joint = together([*grads, *result_parts])
    grads, result_parts = joint[:3], joint[3:]
    result = hidden
    for part in result_parts:
        result = result + part.astype(f32)
    result = result.astype(bf16)
    parts, grad_gain_attn = attn_transposed(
        scales, grads, all_tokens, weights_attn, shard_rows, shards, blocks
    )
    near_down_share = ctx_gather_near(after(share_down, *result_parts))
    joint = together([*parts, *near_down_share])
    parts, near_down_share = list(joint[:blocks]), joint[blocks:]
    parts = ctx_exchange(parts)
    grads_attn = attn_grad(
        scal,
        normed,
        attended,
        [after(grads[0], *parts[:1]), *grads[1:]],
        diagonals,
        grad_gain_attn,
        grad_gain_ffn,
        all_low,
        shards,
        each,
        stride,
    )
    n = len(received)
    joint = together([*parts, *received, *grads_attn])
    parts, received, grads_attn = joint[:blocks], joint[blocks : blocks + n], joint[blocks + n :]
    input_grad = attn_norm_back(scal, grad_hidden, gains, own_tokens, parts, shards)
    far_sum, far_add = [], grads_attn[0]
    if len(grads_attn) == 4:
        far_add = add_low(grads_attn[2], core_swap(grads_attn[3]))
        far_sum = [reduce_far(far_add)]
    near_sum = add_low(grads_attn[0], core_swap(after(grads_attn[1], far_add)))
    share_gate_up = near_total(received, kept, chip)
    near_units = ctx_gather_near(after(share_gate_up, far_add))
    near_sum, *far_sum = together([near_sum, *far_sum])
    far_sum = far_sum[0] if far_sum else None
    cut = 2 * shard_rows
    sends, kept = near_sends(near_sum, far_sum, chip, (0, cut))
    first = near_receive(sends)
    far_units = ctx_gather_far(near_units)
    sends, later = near_sends(
        after(near_sum, *far_units),
        None if far_sum is None else after(far_sum, *far_units),
        chip,
        (cut, stride),
    )
    far_down_share = ctx_gather_far(together(near_down_share, *far_units))
    n = len(first)
    joint = together([*first, *far_down_share, *sends])
    first, far_down_share, sends = joint[:n], joint[n:-n], joint[-n:]
    first = near_total(first, kept, chip)
    second = near_receive(sends)
    joint = together([*ctx_gather(first), *second])
    pieces_first, second = joint[:blocks], near_total(joint[blocks:], later, chip)
    pieces_second = ctx_gather(second)
    pieces_gate_up = ctx_pieces(share_gate_up, near_units, far_units)
    pieces_down = ctx_pieces(share_down, near_down_share, far_down_share)

    g_down = assemble_rows(scal, pieces_down)
    if blocks * unit_rows % 128 == 0:
        g_gate, g_up = assemble_units(scal, pieces_gate_up, shards)
    else:
        stacked = jnp.stack(pieces_gate_up)
        stacked = [
            lax.dynamic_slice_in_dim(stacked, position ^ c, 1, 0)[0] for c in range(blocks)
        ]
        g_gate, g_up = [
            jnp.concatenate(
                [
                    stacked[c][:, n * units + r * unit_rows : n * units + (r + 1) * unit_rows]
                    for r in range(shards)
                    for c in range(blocks)
                ],
                axis=1,
            ).astype(f32)
            for n in range(2)
        ]
    outs_attn = attention_outputs(
        scal, list(pieces_first), 2, shard_rows, each, head_width, False
    )
    *rest, small = attention_outputs(
        scal, list(pieces_second), 1, shard_rows, each, head_width, True
    )
    outs_attn = [*outs_attn, *rest]
    if not strided:
        spot = jnp.zeros((width, width), bf16)
        spot = lax.dynamic_update_slice_in_dim(
            spot,
            dot(attended, jnp.concatenate(all_low, axis=0), 0, 0).astype(bf16),
            position * my_heads * head_width,
            0,
        )
        g_out = lax.psum_scatter(spot, "fsdp", scatter_dimension=0, tiled=True)
        outs_attn.append(lax.psum(g_out, "ctx").astype(f32))
    buckets = relative_bias_table.shape[0]
    return (
        result[None],
        input_grad[None],
        *outs_attn,
        g_gate,
        g_up,
        g_down,
        small[0, :shard_rows],
        small[1, :shard_rows],
        small[2 : 2 + buckets, :heads],
    )


def solution(mesh):
    rows = P("fsdp", None)
    tokens = P("fsdp", "ctx", None)
    in_specs = (tokens, P("fsdp")) + (rows,) * 7 + (P("fsdp"), P("fsdp"), rows, tokens)
    out_specs = (tokens, tokens) + (rows,) * 7 + (P("fsdp"), P("fsdp"), rows)
    return jax.shard_map(
        on_device, mesh=mesh, in_specs=in_specs, out_specs=out_specs, check_vma=False
    )
```

```python
import functools

import jax
import jax.numpy as jnp
import numpy as np
from jax import lax
from jax.experimental import pallas as pl
from jax.experimental.pallas import tpu as pltpu
from jax.sharding import PartitionSpec as P

bucket_total = 32
bucket_total = 32
bucket_edges = (12, 16, 23, 32, 46, 64, 91)
epsilon = 1e-06
masked_score = -1e30
f32 = jnp.float32
bf16 = jnp.bfloat16
i32 = jnp.int32
vmem_limit = 52 * 1024 * 1024
extra = 16
ANY = pl.ANY


def dot(a, b, ca=1, cb=0):
    return lax.dot_general(a, b, (((ca,), (cb,)), ((), ())), preferred_element_type=f32)


def buckets_of(offset):
    distance = jnp.abs(offset)
    bucket = jnp.minimum(distance, 8)
    for edge_value in bucket_edges:
        bucket = bucket + (distance >= edge_value).astype(i32)
    return bucket + 16 * (offset > 0).astype(i32)


def after(value, *earlier):
    return lax.optimization_barrier((value, *earlier))[0]


def together(values, *earlier):
    return lax.optimization_barrier((*values, *earlier))[: len(values)]


def core_swap(a):
    size = lax.axis_size("fsdp")
    return lax.ppermute(a, "fsdp", [(r, r ^ 1) for r in range(size)])


def core_exchange(a):
    groups = [[r, r + 1] for r in range(0, lax.axis_size("fsdp"), 2)]
    return lax.all_to_all(a, "fsdp", 0, 0, axis_index_groups=groups, tiled=True)


def chip_send(a, pairs):
    return lax.ppermute(a, "fsdp", [(2 * s + k, 2 * d + k) for s, d in pairs for k in range(2)])


def ctx_send(a, distance):
    size = lax.axis_size("ctx")
    return lax.ppermute(a, "ctx", [(i, i ^ distance) for i in range(size)])


def near_slots(chips):
    return [0, 1, 3] if chips == 4 else list(range(chips))


def far_slots(chips):
    return [2] if chips == 4 else []


def gather_near(own):
    chips = lax.axis_size("fsdp") // 2
    if chips == 4:
        above = chip_send(own, [(1, 0), (2, 1), (3, 2), (0, 3)])
        below = chip_send(own, [(0, 1), (1, 2), (2, 3), (3, 0)])
        return [own, above, below]
    return [own] + [
        chip_send(own, [((z + t) % chips, z) for z in range(chips)]) for t in range(1, chips)
    ]


def gather_far(near, chip):
    if lax.axis_size("fsdp") // 2 != 4:
        return []
    own, above, below = near
    middle = jnp.where(chip == 1, above, jnp.where(chip == 2, below, own))
    return [chip_send(middle, [(3, 1), (0, 2), (1, 0), (2, 3)])]


def with_other_core(slots):
    if not slots:
        return []
    half = jnp.concatenate(slots, axis=0) if len(slots) > 1 else slots[0]
    return [half, core_swap(half)]


def add_low(a, b):
    return (a.astype(f32) + b.astype(f32)).astype(bf16)


def core_sum(mine, other):
    chips = lax.axis_size("fsdp") // 2
    swapped = core_swap(other)
    if chips != 4:
        return [add_low(mine, swapped)]
    near = mine.shape[0] // 4 * 3
    return [add_low(mine[near:], swapped[near:]), add_low(mine[:near], swapped[:near])]


def reduce_far(far):
    return chip_send(far, [(0, 1), (3, 2), (1, 3), (2, 0)])


def near_sends(near, far, chip, rows=None):
    chips = lax.axis_size("fsdp") // 2
    size = near.shape[0] // len(near_slots(chips))
    first, last = rows or (0, size)
    parts = [near[s * size + first : s * size + last] for s in range(len(near_slots(chips)))]
    if chips != 4:
        return parts[1:], (parts[0], None)
    far = far[first:last]
    wide = far.astype(f32)
    zero = jnp.zeros((), f32)
    up = parts[1].astype(f32) + jnp.where(chip == 1, wide, zero)
    down = parts[2].astype(f32) + jnp.where(chip == 2, wide, zero)
    return [up.astype(bf16), down.astype(bf16)], (parts[0], far)


def near_receive(sends):
    chips = lax.axis_size("fsdp") // 2
    if chips == 4:
        from_below = chip_send(sends[0], [(0, 1), (1, 2), (2, 3), (3, 0)])
        from_above = chip_send(sends[1], [(1, 0), (2, 1), (3, 2), (0, 3)])
        return [from_below, from_above]
    return [
        chip_send(sends[t - 1], [(z, (z + t) % chips) for z in range(chips)])
        for t in range(1, chips)
    ]


def near_total(received, kept, chip):
    own, far = kept
    total = own.astype(f32)
    if far is not None:
        total = total + jnp.where((chip == 0) | (chip == 3), far.astype(f32), jnp.zeros((), f32))
    for part in received:
        total = total + part.astype(f32)
    return total.astype(bf16)


def ctx_gather(a):
    return [a] + [ctx_send(a, t) for t in range(1, lax.axis_size("ctx"))]


def ctx_gather_near(a):
    if lax.axis_size("ctx") == 4:
        return [ctx_send(a, 1), ctx_send(a, 2)]
    return ctx_gather(a)[1:]


def ctx_gather_far(near):
    if lax.axis_size("ctx") == 4:
        half = near[0].shape[0] // 2
        return [ctx_send(near[1][:half], 1), ctx_send(near[0][half:], 2)]
    return []


def ctx_pieces(own, near, far):
    return [own, *near] + ([jnp.concatenate(far, axis=0)] if far else [])


def ctx_exchange(parts):
    return [parts[0]] + [ctx_send(parts[t], t) for t in range(1, len(parts))]


smem = pl.BlockSpec(memory_space=pltpu.SMEM)


def whole(a):
    return pl.BlockSpec(a.shape, lambda *_: (0,) * len(a.shape))


def struct(shape, dtype):
    return jax.ShapeDtypeStruct(shape, dtype)


def call(kernel, grid, in_specs, out_specs, out_shape, args, scratch=(), flops=0, moved=None, exps=0):
    if moved is None:
        moved = sum(a.size * a.dtype.itemsize for a in args) + sum(
            int(np.prod(o.shape)) * jnp.dtype(o.dtype).itemsize for o in out_shape
        )
    return pl.pallas_call(
        kernel,
        grid=grid,
        in_specs=in_specs,
        out_specs=out_specs,
        out_shape=out_shape,
        scratch_shapes=scratch,
        compiler_params=pltpu.CompilerParams(vmem_limit_bytes=vmem_limit),
        cost_estimate=pl.CostEstimate(flops=1, bytes_accessed=1, transcendentals=0),
    )(*args)


def shard_places(refs, stride):
    return [(ref, s * stride) for ref in refs for s in range(ref.shape[0] // stride)]


def tile_of(size, most):
    tile = most
    while size % tile:
        tile //= 2
    return tile


def start_and_wait(copies):
    for c in copies:
        c.start()
    for c in copies:
        c.wait()


def at_step(n):
    return pl.when(pl.program_id(0) == n)


def choose_attention_kernel(head_ids, head_width, with_out, scal, q, k, v, wo, na, nf, table, out):
    position = scal[0]
    rows = q.shape[0]
    wide = out.shape[1]
    for c, ids in enumerate(head_ids):

        @pl.when(position == c)
        def _():
            for n, ref in enumerate((q, k, v)):
                for pair in range(len(ids) // 2):
                    halves = [
                        ref[:, h * head_width : (h + 1) * head_width]
                        for h in ids[2 * pair : 2 * pair + 2]
                    ]
                    out[n * rows : (n + 1) * rows, pair * 128 : pair * 128 + 128] = (
                        jnp.concatenate(halves, axis=1)
                    )
            if with_out:
                blocks = len(head_ids)
                size = rows // blocks
                for b in range(blocks):
                    out[3 * rows + b * size : 3 * rows + (b + 1) * size, :] = wo[
                        c * size : (c + 1) * size, b * wide : (b + 1) * wide
                    ]

    row = lax.broadcasted_iota(i32, (extra, rows), 0)
    gains = jnp.where(row == 0, na[...].astype(f32), jnp.where(row == 1, nf[...].astype(f32), 0.0))
    buckets, heads = table.shape
    low = jnp.concatenate(
        [
            jnp.zeros((2, heads), f32),
            table[...].astype(f32),
            jnp.zeros((extra - 2 - buckets, heads), f32),
        ],
        axis=0,
    )
    low = jnp.concatenate([low, jnp.zeros((extra, rows - heads), f32)], axis=1)
    last = out.shape[0] - extra
    out[last:, :] = jnp.zeros((extra, wide), bf16)
    out[last:, :rows] = (gains + low).astype(bf16)


def choose_units_kernel(shards, scal, gate, up, out):
    position = scal[0]
    units = out.shape[1] // 2
    size = units // shards
    group = gate.shape[1] // shards
    for c in range(gate.shape[1] // units):

        @pl.when(position == c)
        def _():
            for n, ref in enumerate((gate, up)):
                out[:, n * units : (n + 1) * units] = jnp.concatenate(
                    [
                        ref[:, r * group + c * size : r * group + (c + 1) * size]
                        for r in range(shards)
                    ],
                    axis=1,
                )


def tokens_kernel(shards, scal, x, cotangent, out):
    rows, width = x.shape
    size = width // shards
    for l in range(shards):
        start = pl.multiple_of(scal[2 + l] * size, size)
        out[:rows, l * size : (l + 1) * size] = x[:, pl.ds(start, size)]
    row = lax.broadcasted_iota(i32, (rows, width), 0) + scal[0] * rows
    out[rows:, :] = jnp.where(row < scal[1], cotangent[...].astype(f32), 0.0).astype(bf16)


def head_choice(each, shards, position, my_heads, heads):
    h = lax.broadcasted_iota(i32, (my_heads, heads), 0)
    if each:
        shift = each.bit_length() - 1
        head_id = (h >> shift) * (heads // shards) + position * each + (h & (each - 1))
    else:
        head_id = position * my_heads + h
    return (lax.broadcasted_iota(i32, (my_heads, heads), 1) == head_id).astype(f32).astype(bf16)


def bucket_rows(scal, shards, offset):
    row = lax.broadcasted_iota(i32, (bucket_total, offset.shape[1]), 0)
    buckets = bucket_total // shards
    shift = buckets.bit_length() - 1
    bucket_id = jnp.zeros_like(row)
    for l in range(shards):
        bucket_id = jnp.where(
            (row >> shift) == l, scal[2 + l] * buckets + (row & (buckets - 1)), bucket_id
        )
    return (buckets_of(offset) == bucket_id).astype(f32).astype(bf16)


def qkv_kernel(blocks, parts, shards, each, scal, *refs):
    tokens_refs, weights = refs[:blocks], refs[blocks : blocks + parts]
    normed, qkv, bias, gains, scales, joined, small, sems, small_sems = refs[blocks + parts :]
    rows = tokens_refs[0].shape[0]
    tokens, width = normed.shape
    size = width // shards
    stride = sum(w.shape[0] for w in weights) // shards
    places = shard_places(weights, stride)
    step = pl.program_id(0)

    def copy(n, l):
        ref, at = places[l]
        return pltpu.make_async_copy(
            ref.at[pl.ds(at + n * size, size), :],
            joined.at[n, pl.ds(l * size, size), :],
            sems.at[n, l],
        )

    def small_copy(l):
        ref, at = places[l]
        return pltpu.make_async_copy(
            ref.at[pl.ds(at + stride - extra, extra), :], small.at[l], small_sems.at[l]
        )

    @at_step(0)
    def _():
        for l in range(shards):
            small_copy(l).start()
        for n in range(3):
            for l in range(shards):
                copy(n, l).start()
        for l in range(shards):
            small_copy(l).wait()
        my_heads = 2 * bias.shape[0]
        heads = my_heads * blocks
        buckets = bucket_total // shards
        tables = []
        for l in range(shards):
            value = small[l, :, :size].astype(f32)
            gains[:, l * size : (l + 1) * size] = value[:2]
            tables.append(value[2 : 2 + buckets, :heads])
        table = jnp.concatenate(tables, axis=0).astype(bf16)
        chosen = head_choice(each, shards, scal[0], my_heads, heads)
        mine = dot(chosen, table, 1, 1).astype(bf16)
        offset = tokens - lax.broadcasted_iota(i32, (1, 2 * tokens), 1)
        value = dot(mine, bucket_rows(scal, shards, offset))
        for pair in range(bias.shape[0]):
            bias[pair] = value[2 * pair : 2 * pair + 2]
        for t in range(blocks):
            at = slice(t * rows, (t + 1) * rows)
            x = tokens_refs[t][...].astype(f32)
            scale = lax.rsqrt(jnp.mean(x * x, axis=1, keepdims=True) + epsilon)
            normed[at, :] = (x * scale * gains[0:1, :]).astype(bf16)
            scales[at, :] = jnp.broadcast_to(scale, (rows, 128))

    for n in range(3):

        @at_step(n)
        def _():
            for l in range(shards):
                copy(n, l).wait()

    qkv[...] = dot(normed[...], joined[step]).astype(bf16)


def project(scal, tokens_all, weights, shards, each, pairs):
    rows, width = tokens_all[0].shape[0] // 2, tokens_all[0].shape[1]
    blocks = len(tokens_all)
    tokens = rows * blocks
    wide = 128 * pairs
    return call(
        functools.partial(qkv_kernel, blocks, len(weights), shards, each),
        (3,),
        [smem]
        + [pl.BlockSpec((rows, width), lambda n: (0, 0))] * blocks
        + [pl.BlockSpec(memory_space=ANY)] * len(weights),
        [
            pl.BlockSpec((tokens, width), lambda n: (0, 0)),
            pl.BlockSpec((tokens, wide), lambda n: (0, n)),
            pl.BlockSpec((pairs, 2, 2 * tokens), lambda n: (0, 0, 0)),
            pl.BlockSpec((2, width), lambda n: (0, 0)),
            pl.BlockSpec((tokens, 128), lambda n: (0, 0)),
        ],
        [
            struct((tokens, width), bf16),
            struct((tokens, 3 * wide), bf16),
            struct((pairs, 2, 2 * tokens), f32),
            struct((2, width), f32),
            struct((tokens, 128), f32),
        ],
        (scal, *tokens_all, *weights),
        [
            pltpu.VMEM((3, width, wide), bf16),
            pltpu.VMEM((shards, extra, wide), bf16),
            pltpu.SemaphoreType.DMA((3, shards)),
            pltpu.SemaphoreType.DMA((shards,)),
        ],
        flops=6 * tokens * width * wide,
    )


def lanes_of(position, blocks, rows, query, key):
    start = (blocks - 1 + (position ^ query) - (position ^ key)) * rows
    return pl.ds(pl.multiple_of(start, rows), rows)


def forward_kernel(rows, blocks, scal, q_ref, k_ref, v_ref, bias_ref, att, prob, toeplitz):
    position, length = scal[0], scal[1]
    width = 2 * blocks * rows
    slot = lax.broadcasted_iota(i32, (rows, rows), 0)
    for j in range(2):
        row = jnp.broadcast_to(bias_ref[0, j : j + 1, :], (rows, width))
        toeplitz[j] = pltpu.roll(row, width - rows, 1, stride=1, stride_axis=0)
    values = [v_ref[:, 64 * j : 64 * j + 64].astype(f32).T.astype(bf16) for j in range(2)]
    for t in range(blocks):
        at = slice(t * rows, (t + 1) * rows)
        halves = []
        for j in range(2):
            q = q_ref[at, 64 * j : 64 * j + 64]
            k = k_ref[:, 64 * j : 64 * j + 64]
            scores = dot(k, q, 1, 1)
            pieces = []
            for s in range(blocks):
                piece = (
                    scores[s * rows : (s + 1) * rows]
                    + toeplitz[j, :, lanes_of(position, blocks, rows, t, s)]
                )
                live = slot + (position ^ s) * rows < length
                pieces.append(jnp.where(live, piece, masked_score))
            scores = jnp.concatenate(pieces, axis=0)
            top = jnp.max(scores, axis=0, keepdims=True)
            e = jnp.exp(scores - top)
            probs = (e * (1.0 / jnp.sum(e, axis=0, keepdims=True))).astype(bf16)
            prob[j, :, at] = probs
            halves.append(dot(values[j], probs))
        att[at, :] = jnp.concatenate(halves, axis=0).T.astype(bf16)


def backward_kernel(
    rows, blocks, scal, q_ref, k_ref, v_ref, prob, gatt, gq, gk, gv, diag_ref, fold, ds_all
):
    position = scal[0]
    width = 2 * blocks * rows
    grads = [[], [], []]
    for j in range(2):
        columns = slice(64 * j, 64 * j + 64)
        k, v = k_ref[:, columns], v_ref[:, columns]
        fold[...] = jnp.zeros_like(fold)
        for t in range(blocks):
            at = slice(t * rows, (t + 1) * rows)
            gp = dot(v, gatt[at, columns], 1, 1)
            p = prob[j, :, at].astype(f32)
            pg = p * gp
            delta = jnp.sum(pg, axis=0, keepdims=True)
            ds = (pg - p * delta).astype(bf16)
            ds_all[:, at] = ds
            ds = ds.astype(f32)
            for s in range(blocks):
                fold[:, lanes_of(position, blocks, rows, t, s)] += ds[s * rows : (s + 1) * rows]
        grads[0].append(dot(k.astype(f32).T.astype(bf16), ds_all[...]))
        grads[1].append(dot(ds_all[...], q_ref[:, columns]))
        grads[2].append(dot(prob[j], gatt[:, columns]))
        a = fold[...]
        half = rows // 2
        while half >= 8:
            a = a[:half] + pltpu.roll(a[half:], width - half, 1)
            half //= 2
        row = lax.broadcasted_iota(i32, a.shape, 0)
        for bit in (1, 2, 4):
            a = jnp.where((row & bit) != 0, pltpu.roll(a, width - bit, 1), a)
        diag_ref[0, j : j + 1, :] = jnp.sum(a, axis=0, keepdims=True)
    gq[...] = jnp.concatenate(grads[0], axis=0).T.astype(bf16)
    gk[...] = jnp.concatenate(grads[1], axis=1).astype(bf16)
    gv[...] = jnp.concatenate(grads[2], axis=1).astype(bf16)


def attention_forward(scal, qkv, bias, rows, blocks):
    tokens = rows * blocks
    pairs = bias.shape[0]
    return call(
        functools.partial(forward_kernel, rows, blocks),
        (pairs,),
        [smem]
        + [pl.BlockSpec((tokens, 128), lambda p, n=n: (0, n * pairs + p)) for n in range(3)]
        + [pl.BlockSpec((1, 2, 2 * tokens), lambda p: (p, 0, 0))],
        [
            pl.BlockSpec((tokens, 128), lambda p: (0, p)),
            pl.BlockSpec((2, tokens, tokens), lambda p: (p, 0, 0)),
        ],
        [struct((tokens, 128 * pairs), bf16), struct((2 * pairs, tokens, tokens), bf16)],
        (scal, qkv, qkv, qkv, bias),
        [pltpu.VMEM((2, rows, 2 * tokens), f32)],
        flops=8 * pairs * tokens * tokens * 64,
        exps=2 * pairs * tokens * tokens,
    )


def attention_backward(scal, qkv, probs, grad_att, rows, blocks):
    tokens = rows * blocks
    pairs = probs.shape[0] // 2
    block = pl.BlockSpec((tokens, 128), lambda p: (0, p))
    return call(
        functools.partial(backward_kernel, rows, blocks),
        (pairs,),
        [smem]
        + [pl.BlockSpec((tokens, 128), lambda p, n=n: (0, n * pairs + p)) for n in range(3)]
        + [pl.BlockSpec((2, tokens, tokens), lambda p: (p, 0, 0)), block],
        [block, block, block, pl.BlockSpec((1, 2, 2 * tokens), lambda p: (p, 0, 0))],
        [struct((tokens, 128 * pairs), bf16)] * 3 + [struct((pairs, 2, 2 * tokens), f32)],
        (scal, qkv, qkv, qkv, probs, grad_att),
        [pltpu.VMEM((rows, 2 * tokens), f32), pltpu.VMEM((tokens, tokens), bf16)],
        flops=16 * pairs * tokens * tokens * 64,
    )


def out_copies(shards, scal, weights, joined, sems):
    blocks, depth, _ = joined.shape
    size = depth // shards
    stride = sum(w.shape[0] for w in weights) // shards
    first = stride - extra - blocks * size
    copies = []
    for b in range(blocks):
        for l, (ref, at) in enumerate(shard_places(weights, stride)):
            start = pl.multiple_of(scal[2 + l] * size, size)
            copies.append(
                pltpu.make_async_copy(
                    ref.at[pl.ds(at + first + b * size, size), :],
                    joined.at[b, pl.ds(start, size), :],
                    sems.at[b, l],
                )
            )
    return copies


def out_kernel(blocks, parts, shards, scal, att, *refs):
    weights, outs, joined, sems = refs[:parts], refs[parts:-2], refs[-2], refs[-1]
    copies = out_copies(shards, scal, weights, joined, sems)
    for c in copies:
        c.start()
    rows = outs[0].shape[0]
    wide = joined.shape[2]
    for b in range(joined.shape[0]):
        for c in copies[b * shards : (b + 1) * shards]:
            c.wait()
        total = dot(att[...], joined[b]).astype(bf16)
        for t in range(blocks):
            outs[t][:, b * wide : (b + 1) * wide] = total[t * rows : (t + 1) * rows]


def multiply_out(scal, att, weights, shards, blocks):
    tokens, wide = att.shape
    rows, width = tokens // blocks, wide * blocks
    return call(
        functools.partial(out_kernel, blocks, len(weights), shards),
        (1,),
        [smem, whole(att)] + [pl.BlockSpec(memory_space=ANY)] * len(weights),
        [pl.BlockSpec((rows, width), lambda i: (0, 0))] * blocks,
        [struct((rows, width), bf16)] * blocks,
        (scal, att, *weights),
        [pltpu.VMEM((blocks, wide, wide), bf16), pltpu.SemaphoreType.DMA((blocks, shards))],
        flops=2 * tokens * wide * width,
    )


def grad_attended_kernel(blocks, parts, shards, scal, *refs):
    low, weights = refs[:blocks], refs[blocks : blocks + parts]
    out, joined, sems = refs[blocks + parts :]
    copies = out_copies(shards, scal, weights, joined, sems)
    for c in copies:
        c.start()
    wide = joined.shape[2]
    total = None
    for b in range(joined.shape[0]):
        for c in copies[b * shards : (b + 1) * shards]:
            c.wait()
        part = jnp.concatenate([ref[:, b * wide : (b + 1) * wide] for ref in low], axis=0)
        term = dot(part, joined[b], 1, 1)
        total = term if total is None else total + term
    out[...] = total.astype(bf16)


def make_grad_attended(scal, low_all, weights, shards):
    blocks = len(low_all)
    rows, width = low_all[0].shape
    tokens, wide = rows * blocks, width // blocks
    return call(
        functools.partial(grad_attended_kernel, blocks, len(weights), shards),
        (1,),
        [smem] + [whole(a) for a in low_all] + [pl.BlockSpec(memory_space=ANY)] * len(weights),
        [pl.BlockSpec((tokens, wide), lambda i: (0, 0))],
        [struct((tokens, wide), bf16)],
        (scal, *low_all, *weights),
        [pltpu.VMEM((blocks, wide, wide), bf16), pltpu.SemaphoreType.DMA((blocks, shards))],
        flops=2 * tokens * wide * width,
    )[0]


def hidden_kernel(blocks, shards, scal, x, gains, *refs):
    parts, hidden, nffn = refs[:blocks], refs[blocks], refs[blocks + 1]
    total = x[...].astype(f32)
    for part in parts:
        total = total + part[...].astype(f32)
    hidden[...] = total
    scale = lax.rsqrt(jnp.mean(total * total, axis=1, keepdims=True) + epsilon)
    size = total.shape[1] // shards
    for l in range(shards):
        at = slice(l * size, (l + 1) * size)
        start = pl.multiple_of(scal[2 + l] * size, size)
        nffn[:, at] = (hidden[:, pl.ds(start, size)] * scale * gains[1:2, at]).astype(bf16)


def make_hidden(scal, x, gains, parts, shards):
    rows, width = x.shape
    args = (scal, x, gains, *parts)
    return call(
        functools.partial(hidden_kernel, len(parts), shards),
        (1,),
        [smem] + [whole(a) for a in args[1:]],
        [pl.BlockSpec((rows, width), lambda i: (0, 0))] * 2,
        [struct((rows, width), f32), struct((rows, width), bf16)],
        args,
    )


def gelu_tanh(g):
    return jnp.tanh(0.7978845608028654 * (g + 0.044715 * (g * g * g)))


def units_kernel(blocks, parts, tile, *refs):
    tokens_refs, weights = refs[:blocks], refs[blocks : blocks + parts]
    normed, gate, up, mixed, joined, sems = refs[blocks + parts :]
    rows = tokens_refs[0].shape[0]
    units = weights[0].shape[1] // 2
    step = pl.program_id(0)

    def copies(i):
        result, at = [], 0
        for w, ref in enumerate(weights):
            for n in range(2):
                result.append(
                    pltpu.make_async_copy(
                        ref.at[:, pl.ds(n * units + i * tile, tile)],
                        joined.at[i, pl.ds(at, ref.shape[0]), pl.ds(n * tile, tile)],
                        sems.at[i, 2 * w + n],
                    )
                )
            at += ref.shape[0]
        return result

    @at_step(0)
    def _():
        for i in range(units // tile):
            for c in copies(i):
                c.start()
        for t in range(blocks):
            normed[t * rows : (t + 1) * rows, :] = tokens_refs[t][...]

    for i in range(units // tile):

        @at_step(i)
        def _():
            for c in copies(i):
                c.wait()

    both = dot(normed[...], joined[step])
    g, u = both[:, :tile], both[:, tile:]
    gate[...] = g
    up[...] = u
    mixed[...] = (0.5 * g * (1.0 + gelu_tanh(g)) * u).astype(bf16)


def make_units(tokens_all, weights):
    rows, width = tokens_all[0].shape
    blocks = len(tokens_all)
    tokens = rows * blocks
    units = weights[0].shape[1] // 2
    tile = tile_of(units, 256)
    steps = units // tile
    out = pl.BlockSpec((tokens, tile), lambda i: (0, i))
    return call(
        functools.partial(units_kernel, blocks, len(weights), tile),
        (steps,),
        [whole(a) for a in tokens_all] + [pl.BlockSpec(memory_space=ANY)] * len(weights),
        [pl.BlockSpec((tokens, width), lambda i: (0, 0)), out, out, out],
        [
            struct((tokens, width), bf16),
            struct((tokens, units), f32),
            struct((tokens, units), f32),
            struct((tokens, units), bf16),
        ],
        (*tokens_all, *weights),
        [
            pltpu.VMEM((steps, width, 2 * tile), bf16),
            pltpu.SemaphoreType.DMA((steps, 2 * len(weights))),
        ],
        flops=4 * tokens * width * units,
    )


def grad_down_kernel(blocks, shards, scal, mixed, *refs):
    dy, outs, turned, low = refs[:blocks], refs[blocks:-2], refs[-2], refs[-1]

    @at_step(0)
    def _():
        turned[...] = mixed[...].T

    low[...] = dot(turned[...], jnp.concatenate([r[...] for r in dy], axis=0)).astype(bf16)
    size = low.shape[0] // shards
    each = shards // len(outs)
    for l in range(shards):
        start = pl.multiple_of(scal[2 + l] * size, size)
        outs[side_of(shards)[l][0]][pl.ds(side_of(shards)[l][1] * size, size), :] = low[
            pl.ds(start, size), :
        ]


def side_of(shards):
    chips = shards // 2
    sides, counts = [], [0, 0]
    for slots in (near_slots(chips), far_slots(chips)):
        for p in range(2):
            for _ in slots:
                sides.append((p, counts[p]))
                counts[p] += 1
    return sides


def make_grad_down(scal, mixed, tokens_all, shards):
    blocks = len(tokens_all)
    tokens, units = mixed.shape
    rows, width = tokens // blocks, tokens_all[0].shape[1]
    tile = tile_of(width, 512)
    return call(
        functools.partial(grad_down_kernel, blocks, shards),
        (width // tile,),
        [smem, whole(mixed)] + [pl.BlockSpec((rows, tile), lambda i: (1, i))] * blocks,
        [pl.BlockSpec((units // 2, tile), lambda i: (0, i))] * 2,
        [struct((units // 2, width), bf16)] * 2,
        (scal, mixed, *tokens_all),
        [pltpu.VMEM((units, tokens), bf16), pltpu.VMEM((units, tile), bf16)],
        flops=2 * tokens * units * width,
    )


def down_copies(shards, scal, weights, joined, sems):
    size = joined.shape[0] // shards
    copies = []
    for l, (ref, at) in enumerate(shard_places(weights, size)):
        start = pl.multiple_of(scal[2 + l] * size, size) if shards > 1 else 0
        copies.append(
            pltpu.make_async_copy(
                ref.at[pl.ds(at, size), :], joined.at[pl.ds(start, size), :], sems.at[l]
            )
        )
    return copies


def units_back_kernel(blocks, parts, shards, tile, scal, gate, up, *refs):
    dy, weights = refs[:blocks], refs[blocks : blocks + parts]
    out, joined, grads, sems = refs[blocks + parts :]
    step = pl.program_id(0)
    rows = dy[0].shape[0]
    units = joined.shape[0]

    @at_step(0)
    def _():
        copies = down_copies(shards, scal, weights, joined, sems)
        for c in copies:
            c.start()
        for t in range(blocks):
            grads[t * rows : (t + 1) * rows, :] = dy[t][...]
        for c in copies:
            c.wait()

    weight = joined[pl.ds(pl.multiple_of(step * tile, tile), tile), :]
    grad = dot(grads[...], weight, 1, 1)
    g, u = gate[...], up[...]
    t = gelu_tanh(g)
    slope = 0.5 * (1.0 + t) + 0.5 * g * (1.0 - t * t) * (
        0.7978845608028654 * (1.0 + 3 * 0.044715 * (g * g))
    )
    out[:, pl.ds(pl.multiple_of(step * tile, tile), tile)] = (grad * u * slope).astype(bf16)
    out[:, pl.ds(pl.multiple_of(units + step * tile, tile), tile)] = (
        grad * (0.5 * g * (1.0 + t))
    ).astype(bf16)


def units_back(scal, gate, up, tokens_all, weights, shards):
    blocks = len(tokens_all)
    tokens, units = gate.shape
    rows, width = tokens // blocks, tokens_all[0].shape[1]
    tile = tile_of(units, 256)
    block = pl.BlockSpec((tokens, tile), lambda i: (0, i))
    return call(
        functools.partial(units_back_kernel, blocks, len(weights), shards, tile),
        (units // tile,),
        [smem, block, block]
        + [pl.BlockSpec((rows, width), lambda i: (1, 0))] * blocks
        + [pl.BlockSpec(memory_space=ANY)] * len(weights),
        [pl.BlockSpec((tokens, 2 * units), lambda i: (0, 0))],
        [struct((tokens, 2 * units), bf16)],
        (scal, gate, up, *tokens_all, *weights),
        [
            pltpu.VMEM((units, width), bf16),
            pltpu.VMEM((tokens, width), bf16),
            pltpu.SemaphoreType.DMA((shards,)),
        ],
        flops=2 * tokens * units * width,
    )[0]


def result_kernel(blocks, parts, shards, tile, scal, mixed, *refs):
    weights, outs, joined, sems = refs[:parts], refs[parts:-2], refs[-2], refs[-1]
    start_and_wait(down_copies(shards, scal, weights, joined, sems))
    rows, width = outs[0].shape
    for i in range(width // tile):
        at = slice(i * tile, (i + 1) * tile)
        total = dot(mixed[...], joined[:, at]).astype(bf16)
        for t in range(blocks):
            outs[t][:, at] = total[t * rows : (t + 1) * rows]


def multiply_down(scal, mixed, weights, shards, blocks):
    tokens, units = mixed.shape
    width = weights[0].shape[1]
    rows = tokens // blocks
    return call(
        functools.partial(result_kernel, blocks, len(weights), shards, tile_of(width, 512)),
        (1,),
        [smem, whole(mixed)] + [pl.BlockSpec(memory_space=ANY)] * len(weights),
        [pl.BlockSpec((rows, width), lambda i: (0, 0))] * blocks,
        [struct((rows, width), bf16)] * blocks,
        (scal, mixed, *weights),
        [pltpu.VMEM((units, width), bf16), pltpu.SemaphoreType.DMA((shards,))],
        flops=2 * tokens * units * width,
    )


def ffn_transposed_kernel(parts, blocks, g, *refs):
    weights, outs = refs[:parts], refs[parts : parts + blocks]
    held, sems = refs[parts + blocks : -1], refs[-1]
    rows = outs[0].shape[0]
    copies = [pltpu.make_async_copy(w, h, sems.at[i]) for i, (w, h) in enumerate(zip(weights, held))]
    order = sorted(range(parts), key=lambda i: held[i].shape[0])
    first = [sum(h.shape[0] for h in held[:i]) for i in range(parts)]
    for i in order:
        copies[i].start()
    for i in order:
        copies[i].wait()
        tile = held[i].shape[0] if held[i].shape[0] <= 768 else tile_of(held[i].shape[0], 512)
        for n in range(0, held[i].shape[0], tile):
            total = dot(g[...], held[i][n : n + tile, :], 1, 1).astype(bf16)
            at = first[i] + n
            for t, out in enumerate(outs):
                out[:, at : at + tile] = total[t * rows : (t + 1) * rows]


def ffn_transposed(g, weights, blocks):
    tokens, depth = g.shape
    rows, width = tokens // blocks, sum(w.shape[0] for w in weights)
    return call(
        functools.partial(ffn_transposed_kernel, len(weights), blocks),
        (1,),
        [whole(g)] + [pl.BlockSpec(memory_space=ANY)] * len(weights),
        [pl.BlockSpec((rows, width), lambda i: (0, 0))] * blocks,
        [struct((rows, width), bf16)] * blocks,
        (g, *weights),
        [pltpu.VMEM(w.shape, bf16) for w in weights]
        + [pltpu.SemaphoreType.DMA((len(weights),))],
        flops=2 * tokens * depth * width,
    )


def units_grad_kernel(shards, scal, normed, g, *refs):
    outs, turned = refs[:-1], refs[-1]

    @at_step(0)
    def _():
        turned[...] = normed[...].T

    total = dot(turned[...], g[...]).astype(bf16)
    at = 0
    for out in outs[:2]:
        n = out.shape[0]
        out[...] = total[at : at + n]
        at += n
    if len(outs) == 3:
        size = outs[2].shape[0] // 2
        core = scal[2] & 1
        for n, place in enumerate((core, 1 - core)):
            start = pl.multiple_of(place * size, size)
            outs[2][pl.ds(start, size), :] = total[at + n * size : at + (n + 1) * size]


def units_grad(scal, normed, g, shards):
    tokens, depth = normed.shape
    width = g.shape[1]
    tile = tile_of(width, 512)
    size = depth // shards
    sizes = [len(near_slots(shards // 2)) * size] * 2
    if far_slots(shards // 2):
        sizes.append(2 * size)
    return call(
        functools.partial(units_grad_kernel, shards),
        (width // tile,),
        [smem, whole(normed), pl.BlockSpec((tokens, tile), lambda i: (0, i))],
        [pl.BlockSpec((n, tile), lambda i: (0, i)) for n in sizes],
        [struct((n, width), bf16) for n in sizes],
        (scal, normed, g),
        [pltpu.VMEM((depth, tokens), bf16)],
        flops=2 * tokens * depth * width,
    )


def attn_transposed_kernel(blocks, parts, shards, scales, gq, gk, gv, *refs):
    tokens_refs, weights = refs[:blocks], refs[blocks : blocks + parts]
    outs = refs[blocks + parts : 2 * blocks + parts]
    gain, held, sems = refs[2 * blocks + parts :]
    rows, size = outs[0].shape
    stride = sum(w.shape[0] for w in weights) // shards
    step = pl.program_id(0)

    def copy(l):
        ref, at = shard_places(weights, stride)[l]
        return pltpu.make_async_copy(ref.at[pl.ds(at, 3 * size), :], held.at[l], sems.at[l])

    @at_step(0)
    def _():
        for l in range(shards):
            copy(l).start()

    for l in range(shards):

        @at_step(l)
        def _():
            copy(l).wait()

    total = None
    for n, g in enumerate((gq, gk, gv)):
        term = dot(g[...], held[step, n * size : (n + 1) * size, :], 1, 1)
        total = term if total is None else total + term
    summed = jnp.zeros((1, size), f32)
    for t, out in enumerate(outs):
        at = slice(t * rows, (t + 1) * rows)
        out[...] = total[at].astype(bf16)
        unit = tokens_refs[t][...].astype(f32) * scales[at, 0:1]
        summed = summed + jnp.sum(total[at] * unit, axis=0, keepdims=True)
    gain[...] = summed


def attn_transposed(scales, grads, tokens_all, weights, size, shards, blocks):
    tokens, wide = grads[0].shape
    rows, width = tokens // blocks, size * shards
    tile = pl.BlockSpec((rows, size), lambda l: (0, l))
    results = call(
        functools.partial(attn_transposed_kernel, blocks, len(weights), shards),
        (shards,),
        [whole(scales)]
        + [whole(g) for g in grads]
        + [tile] * blocks
        + [pl.BlockSpec(memory_space=ANY)] * len(weights),
        [tile] * blocks + [pl.BlockSpec((1, size), lambda l: (0, l))],
        [struct((rows, width), bf16)] * blocks + [struct((1, width), f32)],
        (scales, *grads, *tokens_all, *weights),
        [
            pltpu.VMEM((shards, 3 * size, wide), bf16),
            pltpu.SemaphoreType.DMA((shards,)),
        ],
        flops=6 * tokens * wide * width,
    )
    return results[:-1], results[-1]


def split_low(a):
    high = a.astype(bf16)
    return high, (a - high.astype(f32)).astype(bf16)


def owner_counts(shards):
    counts = []
    for slots in (near_slots(shards // 2), far_slots(shards // 2)):
        if slots:
            counts += [len(slots)] * 2
    return counts


def shard_owners(outs, shards):
    return [out for out, n in zip(outs, owner_counts(shards)) for _ in range(n)]


def attn_grad_kernel(
    blocks, shards, each, with_out, scal, normed, att, gq, gk, gv, diag, gain_attn, gain_ffn, *refs
):
    low = refs[:blocks]
    outs, (joined, turned, table) = refs[blocks:-3], refs[-3:]
    tokens, width = normed.shape
    wide = att.shape[1]
    size = width // shards
    head_rows = wide // shards
    rows = tokens // blocks
    my_heads = 2 * diag.shape[0]
    heads = my_heads * blocks

    @at_step(0)
    def _():
        for n, g in enumerate((gq, gk, gv)):
            joined[:, n * wide : (n + 1) * wide] = g[...]
        if with_out:
            turned[...] = dot(
                att[...].T, jnp.concatenate([r[...] for r in low], axis=0)
            ).astype(bf16)
        lane = lax.broadcasted_iota(i32, (1, 2 * tokens), 1)
        lane = jnp.where(lane < 2 * tokens - rows, lane, lane - 2 * tokens)
        of_offset = bucket_rows(scal, shards, (blocks - 1) * rows - lane)
        sums = jnp.concatenate([diag[p] for p in range(diag.shape[0])], axis=0)
        total = None
        for part in split_low(sums):
            term = dot(of_offset, part, 1, 1)
            total = term if total is None else total + term
        chosen = head_choice(each, shards, scal[0], my_heads, heads)
        value = None
        for part in split_low(total):
            term = dot(part, chosen)
            value = term if value is None else value + term
        table[...] = value

    buckets = bucket_total // shards
    for l, out in enumerate(shard_owners(outs, shards)):

        @at_step(l)
        def _():
            total = dot(normed[:, l * size : (l + 1) * size], joined[...], 0, 0).astype(bf16)
            for n in range(3):
                out[n * size : (n + 1) * size, :] = total[:, n * wide : (n + 1) * wide]
            if with_out:
                start = pl.multiple_of(scal[2 + l] * head_rows, head_rows)
                for b in range(blocks):
                    out[3 * size + b * head_rows : 3 * size + (b + 1) * head_rows, :] = turned[
                        pl.ds(start, head_rows), b * wide : (b + 1) * wide
                    ]
            part = jnp.concatenate(
                [
                    jnp.zeros((2, heads), f32),
                    table[l * buckets : (l + 1) * buckets, :],
                    jnp.zeros((extra - 2 - buckets, heads), f32),
                ],
                axis=0,
            )
            part = jnp.concatenate([part, jnp.zeros((extra, size - heads), f32)], axis=1)
            row = lax.broadcasted_iota(i32, (extra, size), 0)
            columns = slice(l * size, (l + 1) * size)
            part = part + jnp.where(
                row == 0,
                gain_attn[:, columns],
                jnp.where(row == 1, gain_ffn[:, columns], 0.0),
            )
            last = out.shape[0] - extra
            out[last:, :] = jnp.zeros((extra, wide), bf16)
            out[last:, :size] = part.astype(bf16)


def attn_grad(scal, normed, att, grads, diag, gain_attn, gain_ffn, low_all, shards, each, stride):
    tokens, width = normed.shape
    wide = att.shape[1]
    blocks = len(low_all)
    counts = owner_counts(shards)
    specs, first = [], 0
    for n in counts:
        specs.append(
            pl.BlockSpec((stride, wide), lambda l, f=first, n=n: (jnp.clip(l - f, 0, n - 1), 0))
        )
        first += n
    args = (scal, normed, att, *grads, diag, gain_attn, gain_ffn, *low_all)
    return call(
        functools.partial(attn_grad_kernel, blocks, shards, each, bool(each)),
        (shards,),
        [smem] + [whole(a) for a in args[1:]],
        specs,
        [struct((n * stride, wide), bf16) for n in counts],
        args,
        [
            pltpu.VMEM((tokens, 3 * wide), bf16),
            pltpu.VMEM((wide, width), bf16),
            pltpu.VMEM((bucket_total, 2 * diag.shape[0] * blocks), f32),
        ],
        flops=8 * tokens * wide * width,
    )


def ffn_norm_back_kernel(blocks, shards, scal, hidden, gains, own, *refs):
    parts = refs[:blocks]
    grad_hidden, low, grad_gain, g, gain = refs[blocks:]
    size = hidden.shape[1] // shards
    for l in range(shards):
        at = slice(l * size, (l + 1) * size)
        start = pl.multiple_of(scal[2 + l] * size, size)
        total = parts[0][:, at].astype(f32)
        for part in parts[1:]:
            total = total + part[:, at].astype(f32)
        g[:, pl.ds(start, size)] = total
        gain[:, pl.ds(start, size)] = gains[1:2, at]
    h = hidden[...]
    scale = lax.rsqrt(jnp.mean(h * h, axis=1, keepdims=True) + epsilon)
    weighted = g[...] * gain[...]
    inner = jnp.mean(weighted * h, axis=1, keepdims=True)
    value = own[...].astype(f32) + scale * weighted - h * (scale * scale * scale) * inner
    grad_hidden[...] = value
    low[...] = value.astype(bf16)
    g[...] = g[...] * h * scale
    for l in range(shards):
        start = pl.multiple_of(scal[2 + l] * size, size)
        grad_gain[:, l * size : (l + 1) * size] = jnp.sum(
            g[:, pl.ds(start, size)], axis=0, keepdims=True
        )


def ffn_norm_back(scal, hidden, gains, own, parts, shards):
    rows, width = hidden.shape
    block = pl.BlockSpec((rows, width), lambda i: (0, 0))
    return call(
        functools.partial(ffn_norm_back_kernel, len(parts), shards),
        (1,),
        [smem, block, whole(gains), pl.BlockSpec((rows, width), lambda i: (1, 0))]
        + [block] * len(parts),
        [block, block, pl.BlockSpec((1, width), lambda i: (0, 0))],
        [struct((rows, width), f32), struct((rows, width), bf16), struct((1, width), f32)],
        (scal, hidden, gains, own, *parts),
        [pltpu.VMEM((rows, width), f32), pltpu.VMEM((1, width), f32)],
    )


def attn_norm_back_kernel(blocks, shards, scal, grad_hidden, gains, own, *refs):
    parts = refs[:blocks]
    grad, value = refs[blocks:]
    x = own[...].astype(f32)
    g = parts[0][...].astype(f32)
    for part in parts[1:]:
        g = g + part[...].astype(f32)
    scale = lax.rsqrt(jnp.mean(x * x, axis=1, keepdims=True) + epsilon)
    weighted = g * gains[0:1, :]
    inner = jnp.mean(weighted * x, axis=1, keepdims=True)
    value[...] = scale * weighted - x * (scale * scale * scale) * inner
    size = x.shape[1] // shards
    for l in range(shards):
        at = slice(l * size, (l + 1) * size)
        where = pl.ds(pl.multiple_of(scal[2 + l] * size, size), size)
        grad[:, where] = (grad_hidden[:, where] + value[:, at]).astype(bf16)


def attn_norm_back(scal, grad_hidden, gains, own, parts, shards):
    rows, width = grad_hidden.shape
    block = pl.BlockSpec((rows, width), lambda i: (0, 0))
    return call(
        functools.partial(attn_norm_back_kernel, len(parts), shards),
        (1,),
        [smem, block, whole(gains), block] + [block] * len(parts),
        [block],
        [struct((rows, width), bf16)],
        (scal, grad_hidden, gains, own, *parts),
        [pltpu.VMEM((rows, width), f32)],
    )[0]


def by_position(scal, blocks, body):
    for p in range(blocks):

        @pl.when(scal[0] == p)
        def _():
            body([p ^ c for c in range(blocks)])


def columns_kernel(groups, scal, *refs):
    pieces, outs = refs[:-2], refs[-2:]
    blocks = len(pieces)
    units = pieces[0].shape[1] // 2
    size = units // groups
    wide = blocks * size

    def body(order):
        for n, out in enumerate(outs):
            for g in range(groups):
                at = n * units + g * size
                out[:, g * wide : (g + 1) * wide] = jnp.concatenate(
                    [pieces[t][:, at : at + size] for t in order], axis=1
                ).astype(f32)

    by_position(scal, blocks, body)


def assemble_units(scal, pieces, groups):
    rows, columns = pieces[0].shape
    tile = min(rows, 32)
    wide = len(pieces) * columns // 2
    return call(
        functools.partial(columns_kernel, groups),
        (rows // tile,),
        [smem] + [pl.BlockSpec((tile, columns), lambda i: (i, 0))] * len(pieces),
        [pl.BlockSpec((tile, wide), lambda i: (i, 0))] * 2,
        [struct((rows, wide), f32)] * 2,
        (scal, *pieces),
    )


def rows_kernel(size, scal, *refs):
    position = scal[0]
    for t, piece in enumerate(refs[:-1]):
        start = pl.multiple_of((position ^ t) * size, 8)
        refs[-1][pl.ds(start, size), :] = piece[...].astype(f32)


def assemble_rows(scal, pieces):
    rows, columns = pieces[0].shape
    tile = tile_of(columns, 512)
    return call(
        functools.partial(rows_kernel, rows),
        (columns // tile,),
        [smem] + [pl.BlockSpec((rows, tile), lambda i: (0, i))] * len(pieces),
        [pl.BlockSpec((rows * len(pieces), tile), lambda i: (0, i))],
        [struct((rows * len(pieces), columns), f32)],
        (scal, *pieces),
    )[0]


def attention_outputs_kernel(each, blocks, head_width, count, last, scal, *refs):
    columns, rest = refs[: count * blocks], refs[count * blocks :]
    with_out = last and bool(each)
    out_blocks = rest[:blocks] if with_out else ()
    rest = rest[blocks:] if with_out else rest
    small, outs = (rest[:blocks], rest[blocks:]) if last else ((), rest)
    wide = columns[0].shape[1]
    step = pl.program_id(0)

    def body(order):
        for n in range(count):
            pieces = [columns[count * t + n] for t in order]
            if each:
                size = each * head_width
                for g in range(wide // size):
                    outs[n][:, g * blocks * size : (g + 1) * blocks * size] = jnp.concatenate(
                        [ref[:, g * size : (g + 1) * size] for ref in pieces], axis=1
                    ).astype(f32)
            else:
                for c, ref in enumerate(pieces):
                    outs[n][:, c * wide : (c + 1) * wide] = ref[...].astype(f32)

        if last:

            @at_step(0)
            def _():
                total = small[order[0]][...].astype(f32)
                for t in order[1:]:
                    total = total + small[t][...].astype(f32)
                outs[-1][...] = total

    by_position(scal, blocks, body)
    if with_out:
        for t in range(blocks):

            @pl.when((step ^ scal[0]) == t)
            def _():
                size = outs[count].shape[0]
                for b in range(blocks):
                    outs[count][:, b * wide : (b + 1) * wide] = out_blocks[t][
                        b * size : (b + 1) * size, :
                    ].astype(f32)


def attention_outputs(scal, pieces, count, rows, each, head_width, last):
    blocks = len(pieces)
    total, wide = pieces[0].shape
    tile = rows // blocks
    per = rows // tile
    specs, args = [], []
    for a in pieces:
        for n in range(count):
            specs.append(pl.BlockSpec((tile, wide), lambda i, n=n: (n * per + i, 0)))
            args.append(a)
    outputs = count
    if last and each:
        specs += [pl.BlockSpec((rows, wide), lambda i: (count, 0))] * blocks
        args += pieces
        outputs += 1
    if last:
        specs += [pl.BlockSpec((extra, wide), lambda i: (total // extra - 1, 0))] * blocks
        args += pieces
    block = pl.BlockSpec((tile, wide * blocks), lambda i: (i, 0))
    out_specs, out_shape = [block] * outputs, [struct((rows, wide * blocks), f32)] * outputs
    if last:
        out_specs.append(pl.BlockSpec((extra, wide), lambda i: (0, 0)))
        out_shape.append(struct((extra, wide), f32))
    return call(
        functools.partial(attention_outputs_kernel, each, blocks, head_width, count, last),
        (blocks,),
        [smem] + specs,
        out_specs,
        out_shape,
        (scal, *args),
    )


def take_blocks(a, starts, size):
    return jnp.concatenate([lax.dynamic_slice_in_dim(a, s, size, 0) for s in starts], 0)


def on_device(
    inputs,
    lengths,
    w_query,
    w_key,
    w_value,
    w_out,
    w_gate,
    w_up,
    w_down,
    norm_attn,
    norm_ffn,
    relative_bias_table,
    cotangent,
):
    blocks = lax.axis_size("ctx")
    shards = lax.axis_size("fsdp")
    chips = shards // 2
    position = lax.axis_index("ctx")
    shard = lax.axis_index("fsdp")
    chip, core = shard // 2, shard % 2
    rows, width = inputs.shape[1], inputs.shape[2]
    tokens = rows * blocks
    heads = relative_bias_table.shape[1]
    head_width = width // heads
    my_heads = heads // blocks
    pairs = my_heads // 2
    each = heads // shards // blocks if (heads // shards) % blocks == 0 else 0
    strided = each in (1, 2)
    each = each if strided else 0
    units = w_gate.shape[1] // blocks
    shard_rows = width // shards
    unit_rows = w_down.shape[0] // blocks

    slot_of, parity_of = [], []
    for slots in (near_slots(chips), far_slots(chips)):
        for p in range(2):
            slot_of += slots
            parity_of += [p] * len(slots)
    pad = [0, 0]
    order = 2 * ((chip + jnp.array(pad + slot_of, i32)) % chips) + (
        core ^ jnp.array(pad + parity_of, i32)
    )
    index = jnp.arange(shards + 2, dtype=i32)
    scal = jnp.where(index == 0, position, jnp.where(index == 1, lengths[0], order)).astype(i32)

    def heads_of(c):
        if strided:
            return [
                (h // each) * (heads // shards) + c * each + h % each for h in range(my_heads)
            ]
        return [c * my_heads + h for h in range(my_heads)]

    args = (
        scal,
        w_query,
        w_key,
        w_value,
        w_out,
        norm_attn.reshape(1, -1),
        norm_ffn.reshape(1, -1),
        relative_bias_table,
    )
    stride = (4 if strided else 3) * shard_rows + extra
    own_attn = call(
        functools.partial(
            choose_attention_kernel, [heads_of(c) for c in range(blocks)], head_width, strided
        ),
        (1,),
        [smem] + [whole(a) for a in args[1:]],
        [pl.BlockSpec((stride, 128 * pairs), lambda i: (0, 0))],
        [struct((stride, 128 * pairs), bf16)],
        args,
    )[0]
    near_attn = gather_near(own_attn)
    own_tokens = call(
        functools.partial(tokens_kernel, shards),
        (1,),
        [smem] + [pl.BlockSpec((rows, width), lambda i: (0, 0))] * 2,
        [pl.BlockSpec((2 * rows, width), lambda i: (0, 0))],
        [struct((2 * rows, width), bf16)],
        (after(scal, own_attn), inputs[0], cotangent[0]),
    )[0]
    all_tokens = ctx_gather(own_tokens)
    tile = tile_of(shard_rows, 64)
    own_gate_up = call(
        functools.partial(choose_units_kernel, shards),
        (shard_rows // tile,),
        [smem] + [pl.BlockSpec((tile, w_gate.shape[1]), lambda i: (i, 0))] * 2,
        [pl.BlockSpec((tile, 2 * units), lambda i: (i, 0))],
        [struct((shard_rows, 2 * units), bf16)],
        (after(scal, own_tokens), w_gate, w_up),
    )[0]
    joint = together([*near_attn, *all_tokens], own_gate_up)
    near_attn, all_tokens = joint[: len(near_attn)], joint[len(near_attn) :]
    far_attn = gather_far(near_attn, chip)
    n = len(near_attn)
    joint = together([core_swap(a) for a in near_attn] + far_attn)
    weights_attn, far_attn = [*near_attn, *joint[:n]], joint[n:]
    near_gate_up = gather_near(after(own_gate_up, *far_attn))
    weights_attn += with_other_core(far_attn)
    if not strided:
        gathered = lax.all_gather(w_out, "fsdp", axis=0, tiled=True)
        size = my_heads * head_width
        full_out = lax.dynamic_slice_in_dim(gathered, position * size, size, 0)

    normed, qkv, bias, gains, scales = project(
        scal, all_tokens, weights_attn, shards, each, pairs
    )
    attended, probs = attention_forward(scal, qkv, bias, rows, blocks)
    if strided:
        parts = multiply_out(scal, attended, weights_attn, shards, blocks)
    else:
        whole_part = dot(attended, full_out).astype(bf16)
        parts = [whole_part[t * rows : (t + 1) * rows] for t in range(blocks)]
    parts = ctx_exchange(parts)
    hidden, own_nffn = make_hidden(scal, inputs[0], gains, parts, shards)

    near_gate_up = together(near_gate_up, own_nffn)
    far_gate_up = gather_far(near_gate_up, chip)
    joint = together(with_other_core(near_gate_up) + ctx_gather(own_nffn) + far_gate_up)
    weights_gate_up = list(joint[:2])
    all_nffn, far_gate_up = joint[2 : 2 + blocks], joint[2 + blocks :]
    own_down = lax.dynamic_slice_in_dim(w_down, position * unit_rows, unit_rows, 0)
    near_down = gather_near(after(own_down, all_nffn[0]))
    weights_gate_up += with_other_core(far_gate_up)
    normed_ffn, gate, up, mixed_units = make_units(all_nffn, weights_gate_up)

    aligned = unit_rows % 16 == 0
    if aligned:
        grads_down = make_grad_down(scal, mixed_units, all_tokens, shards)
    else:
        all_dy = jnp.concatenate([a[rows:] for a in all_tokens], axis=0)
        grad_down = dot(mixed_units, all_dy, 0, 0).astype(bf16)
        grads_down = [
            take_blocks(
                grad_down,
                [order[2 + l] * unit_rows for l in range(shards) if parity_of[l] == side],
                unit_rows,
            )
            for side in range(2)
        ]
    joint = together([*near_down, *grads_down])
    near_down, grads_down = joint[:-2], joint[-2:]
    far_down = gather_far(near_down, chip)
    sums_down = core_sum(*grads_down)
    joint = together(with_other_core(near_down) + far_down, *sums_down)
    down_parts, far_down = list(joint[:2]), joint[2:]
    down_parts, down_shards = down_parts + with_other_core(far_down), shards
    if not aligned:
        joined = jnp.concatenate(down_parts, axis=0)
        place = jnp.argsort(order[2:])
        down_parts = [take_blocks(joined, [place[r] * unit_rows for r in range(shards)], unit_rows)]
        down_shards = 1

    far_sum = None
    if len(sums_down) == 2:
        far_sum = reduce_far(after(sums_down[0], *far_down))
    grad_units = units_back(scal, gate, up, all_tokens, down_parts, down_shards)
    if far_sum is not None:
        far_sum, grad_units = together([far_sum, grad_units])
    sends, kept = near_sends(sums_down[-1], far_sum, chip)
    sends = together(sends, grad_units)
    received = near_receive(sends)
    parts = ffn_transposed(after(grad_units, *sends), weights_gate_up, blocks)
    grads_gate_up = units_grad(scal, normed_ffn, after(grad_units, *parts), shards)
    parts = ctx_exchange(parts)
    n = len(received)
    joint = together([*received, *grads_gate_up])
    received, grads_gate_up = joint[:n], joint[n:]
    far_sum, far_add = [], grads_gate_up[0]
    if len(grads_gate_up) == 3:
        both = core_exchange(grads_gate_up[2])
        far_add = add_low(both[:shard_rows], both[shard_rows:])
        far_sum = [reduce_far(far_add)]
    share_down = near_total(received, kept, chip)
    parts = together(parts, far_add)
    grad_hidden, low, grad_gain_ffn = ffn_norm_back(
        scal, hidden, gains, own_tokens, parts, shards
    )

    all_low = ctx_gather(low)
    near_sum = add_low(grads_gate_up[0], core_swap(after(grads_gate_up[1], low)))
    result_parts = multiply_down(
        scal, after(mixed_units, near_sum, share_down), down_parts, down_shards, blocks
    )
    near_sum, *result_parts = together([near_sum, *result_parts])
    sends, kept = near_sends(near_sum, far_sum[0] if far_sum else None, chip)
    received = near_receive(sends)
    result_parts = ctx_exchange(together(result_parts, *all_low))
    if strided:
        grad_att = make_grad_attended(after(scal, *sends), all_low, weights_attn, shards)
    else:
        grad_att = dot(jnp.concatenate(all_low, axis=0), full_out, 1, 1).astype(bf16)
    *grads, diagonals = attention_backward(scal, qkv, probs, grad_att, rows, blocks)
    joint = together([*grads, *result_parts])
    grads, result_parts = joint[:3], joint[3:]
    result = hidden
    for part in result_parts:
        result = result + part.astype(f32)
    result = result.astype(bf16)
    parts, grad_gain_attn = attn_transposed(
        scales, grads, all_tokens, weights_attn, shard_rows, shards, blocks
    )
    near_down_share = ctx_gather_near(after(share_down, *result_parts))
    joint = together([*parts, *near_down_share])
    parts, near_down_share = list(joint[:blocks]), joint[blocks:]
    parts = ctx_exchange(parts)
    grads_attn = attn_grad(
        scal,
        normed,
        attended,
        [after(grads[0], *parts[:1]), *grads[1:]],
        diagonals,
        grad_gain_attn,
        grad_gain_ffn,
        all_low,
        shards,
        each,
        stride,
    )
    n = len(received)
    joint = together([*received, *grads_attn])
    received, grads_attn = joint[:n], joint[n:]
    share_gate_up = near_total(received, kept, chip)
    joint = together([*parts, share_gate_up, *grads_attn])
    parts, share_gate_up, grads_attn = joint[:blocks], joint[blocks], joint[blocks + 1 :]
    input_grad = attn_norm_back(scal, grad_hidden, gains, own_tokens, parts, shards)
    far_sum, far_add = [], grads_attn[0]
    if len(grads_attn) == 4:
        far_add = add_low(grads_attn[2], core_swap(grads_attn[3]))
        far_sum = [reduce_far(far_add)]
    near_sum = add_low(grads_attn[0], core_swap(after(grads_attn[1], far_add)))
    near_units = ctx_gather_near(after(share_gate_up, far_add))
    near_sum, *far_sum = together([near_sum, *far_sum])
    far_sum = far_sum[0] if far_sum else None
    cut = 2 * shard_rows
    sends, kept = near_sends(near_sum, far_sum, chip, (0, cut))
    first = near_receive(sends)
    far_units = ctx_gather_far(near_units)
    sends, later = near_sends(
        after(near_sum, *far_units),
        None if far_sum is None else after(far_sum, *far_units),
        chip,
        (cut, stride),
    )
    far_down_share = ctx_gather_far(together(near_down_share, *far_units))
    n = len(first)
    joint = together([*first, *far_down_share, *sends])
    first, far_down_share, sends = joint[:n], joint[n:-n], joint[-n:]
    first = near_total(first, kept, chip)
    second = near_receive(sends)
    joint = together([*ctx_gather(first), *second])
    pieces_first, second = joint[:blocks], near_total(joint[blocks:], later, chip)
    pieces_second = ctx_gather(second)
    pieces_gate_up = ctx_pieces(share_gate_up, near_units, far_units)
    pieces_down = ctx_pieces(share_down, near_down_share, far_down_share)

    g_down = assemble_rows(scal, pieces_down)
    if blocks * unit_rows % 128 == 0:
        g_gate, g_up = assemble_units(scal, pieces_gate_up, shards)
    else:
        stacked = jnp.stack(pieces_gate_up)
        stacked = [
            lax.dynamic_slice_in_dim(stacked, position ^ c, 1, 0)[0] for c in range(blocks)
        ]
        g_gate, g_up = [
            jnp.concatenate(
                [
                    stacked[c][:, n * units + r * unit_rows : n * units + (r + 1) * unit_rows]
                    for r in range(shards)
                    for c in range(blocks)
                ],
                axis=1,
            ).astype(f32)
            for n in range(2)
        ]
    outs_attn = attention_outputs(
        scal, list(pieces_first), 2, shard_rows, each, head_width, False
    )
    *rest, small = attention_outputs(
        scal, list(pieces_second), 1, shard_rows, each, head_width, True
    )
    outs_attn = [*outs_attn, *rest]
    if not strided:
        spot = jnp.zeros((width, width), bf16)
        spot = lax.dynamic_update_slice_in_dim(
            spot,
            dot(attended, jnp.concatenate(all_low, axis=0), 0, 0).astype(bf16),
            position * my_heads * head_width,
            0,
        )
        g_out = lax.psum_scatter(spot, "fsdp", scatter_dimension=0, tiled=True)
        outs_attn.append(lax.psum(g_out, "ctx").astype(f32))
    buckets = relative_bias_table.shape[0]
    return (
        result[None],
        input_grad[None],
        *outs_attn,
        g_gate,
        g_up,
        g_down,
        small[0, :shard_rows],
        small[1, :shard_rows],
        small[2 : 2 + buckets, :heads],
    )


def solution(mesh):
    rows = P("fsdp", None)
    tokens = P("fsdp", "ctx", None)
    in_specs = (tokens, P("fsdp")) + (rows,) * 7 + (P("fsdp"), P("fsdp"), rows, tokens)
    out_specs = (tokens, tokens) + (rows,) * 7 + (P("fsdp"), P("fsdp"), rows)
    return jax.shard_map(
        on_device, mesh=mesh, in_specs=in_specs, out_specs=out_specs, check_vma=False
    )
```

```python
import functools

import jax
import jax.numpy as jnp
import numpy as np
from jax import lax
from jax.experimental import pallas as pl
from jax.experimental.pallas import tpu as pltpu
from jax.sharding import PartitionSpec as P

bucket_total = 32
bucket_total = 32
bucket_edges = (12, 16, 23, 32, 46, 64, 91)
epsilon = 1e-06
masked_score = -1e30
f32 = jnp.float32
bf16 = jnp.bfloat16
i32 = jnp.int32
vmem_limit = 52 * 1024 * 1024
extra = 16
ANY = pl.ANY


def dot(a, b, ca=1, cb=0):
    return lax.dot_general(a, b, (((ca,), (cb,)), ((), ())), preferred_element_type=f32)


def buckets_of(offset):
    distance = jnp.abs(offset)
    bucket = jnp.minimum(distance, 8)
    for edge_value in bucket_edges:
        bucket = bucket + (distance >= edge_value).astype(i32)
    return bucket + 16 * (offset > 0).astype(i32)


def after(value, *earlier):
    return lax.optimization_barrier((value, *earlier))[0]


def together(values, *earlier):
    return lax.optimization_barrier((*values, *earlier))[: len(values)]


def core_swap(a):
    size = lax.axis_size("fsdp")
    return lax.ppermute(a, "fsdp", [(r, r ^ 1) for r in range(size)])


def core_exchange(a):
    groups = [[r, r + 1] for r in range(0, lax.axis_size("fsdp"), 2)]
    return lax.all_to_all(a, "fsdp", 0, 0, axis_index_groups=groups, tiled=True)


def chip_send(a, pairs):
    return lax.ppermute(a, "fsdp", [(2 * s + k, 2 * d + k) for s, d in pairs for k in range(2)])


def ctx_send(a, distance):
    size = lax.axis_size("ctx")
    return lax.ppermute(a, "ctx", [(i, i ^ distance) for i in range(size)])


def near_slots(chips):
    return [0, 1, 3] if chips == 4 else list(range(chips))


def far_slots(chips):
    return [2] if chips == 4 else []


def gather_near(own):
    chips = lax.axis_size("fsdp") // 2
    if chips == 4:
        above = chip_send(own, [(1, 0), (2, 1), (3, 2), (0, 3)])
        below = chip_send(own, [(0, 1), (1, 2), (2, 3), (3, 0)])
        return [own, above, below]
    return [own] + [
        chip_send(own, [((z + t) % chips, z) for z in range(chips)]) for t in range(1, chips)
    ]


def gather_far(near, chip):
    if lax.axis_size("fsdp") // 2 != 4:
        return []
    own, above, below = near
    middle = jnp.where(chip == 1, above, jnp.where(chip == 2, below, own))
    return [chip_send(middle, [(3, 1), (0, 2), (1, 0), (2, 3)])]


def with_other_core(slots):
    if not slots:
        return []
    half = jnp.concatenate(slots, axis=0) if len(slots) > 1 else slots[0]
    return [half, core_swap(half)]


def add_low(a, b):
    return (a.astype(f32) + b.astype(f32)).astype(bf16)


def core_sum(mine, other):
    chips = lax.axis_size("fsdp") // 2
    swapped = core_swap(other)
    if chips != 4:
        return [add_low(mine, swapped)]
    near = mine.shape[0] // 4 * 3
    return [add_low(mine[near:], swapped[near:]), add_low(mine[:near], swapped[:near])]


def reduce_far(far):
    return chip_send(far, [(0, 1), (3, 2), (1, 3), (2, 0)])


def near_sends(near, far, chip, rows=None):
    chips = lax.axis_size("fsdp") // 2
    size = near.shape[0] // len(near_slots(chips))
    first, last = rows or (0, size)
    parts = [near[s * size + first : s * size + last] for s in range(len(near_slots(chips)))]
    if chips != 4:
        return parts[1:], (parts[0], None)
    far = far[first:last]
    wide = far.astype(f32)
    zero = jnp.zeros((), f32)
    up = parts[1].astype(f32) + jnp.where(chip == 1, wide, zero)
    down = parts[2].astype(f32) + jnp.where(chip == 2, wide, zero)
    return [up.astype(bf16), down.astype(bf16)], (parts[0], far)


def near_receive(sends):
    chips = lax.axis_size("fsdp") // 2
    if chips == 4:
        from_below = chip_send(sends[0], [(0, 1), (1, 2), (2, 3), (3, 0)])
        from_above = chip_send(sends[1], [(1, 0), (2, 1), (3, 2), (0, 3)])
        return [from_below, from_above]
    return [
        chip_send(sends[t - 1], [(z, (z + t) % chips) for z in range(chips)])
        for t in range(1, chips)
    ]


def near_total(received, kept, chip):
    own, far = kept
    total = own.astype(f32)
    if far is not None:
        total = total + jnp.where((chip == 0) | (chip == 3), far.astype(f32), jnp.zeros((), f32))
    for part in received:
        total = total + part.astype(f32)
    return total.astype(bf16)


def ctx_gather(a):
    return [a] + [ctx_send(a, t) for t in range(1, lax.axis_size("ctx"))]


def ctx_gather_near(a):
    if lax.axis_size("ctx") == 4:
        return [ctx_send(a, 1), ctx_send(a, 2)]
    return ctx_gather(a)[1:]


def ctx_gather_far(near):
    if lax.axis_size("ctx") == 4:
        half = near[0].shape[0] // 2
        return [ctx_send(near[1][:half], 1), ctx_send(near[0][half:], 2)]
    return []


def ctx_pieces(own, near, far):
    return [own, *near] + ([jnp.concatenate(far, axis=0)] if far else [])


def ctx_exchange(parts):
    return [parts[0]] + [ctx_send(parts[t], t) for t in range(1, len(parts))]


smem = pl.BlockSpec(memory_space=pltpu.SMEM)


def whole(a):
    return pl.BlockSpec(a.shape, lambda *_: (0,) * len(a.shape))


def struct(shape, dtype):
    return jax.ShapeDtypeStruct(shape, dtype)


def call(kernel, grid, in_specs, out_specs, out_shape, args, scratch=(), flops=0, moved=None, exps=0):
    if moved is None:
        moved = sum(a.size * a.dtype.itemsize for a in args) + sum(
            int(np.prod(o.shape)) * jnp.dtype(o.dtype).itemsize for o in out_shape
        )
    return pl.pallas_call(
        kernel,
        grid=grid,
        in_specs=in_specs,
        out_specs=out_specs,
        out_shape=out_shape,
        scratch_shapes=scratch,
        compiler_params=pltpu.CompilerParams(vmem_limit_bytes=vmem_limit),
        cost_estimate=pl.CostEstimate(flops=1, bytes_accessed=1, transcendentals=0),
    )(*args)


def shard_places(refs, stride):
    return [(ref, s * stride) for ref in refs for s in range(ref.shape[0] // stride)]


def tile_of(size, most):
    tile = most
    while size % tile:
        tile //= 2
    return tile


def start_and_wait(copies):
    for c in copies:
        c.start()
    for c in copies:
        c.wait()


def at_step(n):
    return pl.when(pl.program_id(0) == n)


def choose_attention_kernel(head_ids, head_width, with_out, scal, q, k, v, wo, na, nf, table, out):
    position = scal[0]
    rows = q.shape[0]
    wide = out.shape[1]
    for c, ids in enumerate(head_ids):

        @pl.when(position == c)
        def _():
            for n, ref in enumerate((q, k, v)):
                for pair in range(len(ids) // 2):
                    halves = [
                        ref[:, h * head_width : (h + 1) * head_width]
                        for h in ids[2 * pair : 2 * pair + 2]
                    ]
                    out[n * rows : (n + 1) * rows, pair * 128 : pair * 128 + 128] = (
                        jnp.concatenate(halves, axis=1)
                    )
            if with_out:
                blocks = len(head_ids)
                size = rows // blocks
                for b in range(blocks):
                    out[3 * rows + b * size : 3 * rows + (b + 1) * size, :] = wo[
                        c * size : (c + 1) * size, b * wide : (b + 1) * wide
                    ]

    row = lax.broadcasted_iota(i32, (extra, rows), 0)
    gains = jnp.where(row == 0, na[...].astype(f32), jnp.where(row == 1, nf[...].astype(f32), 0.0))
    buckets, heads = table.shape
    low = jnp.concatenate(
        [
            jnp.zeros((2, heads), f32),
            table[...].astype(f32),
            jnp.zeros((extra - 2 - buckets, heads), f32),
        ],
        axis=0,
    )
    low = jnp.concatenate([low, jnp.zeros((extra, rows - heads), f32)], axis=1)
    last = out.shape[0] - extra
    out[last:, :] = jnp.zeros((extra, wide), bf16)
    out[last:, :rows] = (gains + low).astype(bf16)


def choose_units_kernel(shards, scal, gate, up, out):
    position = scal[0]
    units = out.shape[1] // 2
    size = units // shards
    group = gate.shape[1] // shards
    for c in range(gate.shape[1] // units):

        @pl.when(position == c)
        def _():
            for n, ref in enumerate((gate, up)):
                out[:, n * units : (n + 1) * units] = jnp.concatenate(
                    [
                        ref[:, r * group + c * size : r * group + (c + 1) * size]
                        for r in range(shards)
                    ],
                    axis=1,
                )


def tokens_kernel(shards, scal, x, cotangent, out):
    rows, width = x.shape
    size = width // shards
    for l in range(shards):
        start = pl.multiple_of(scal[2 + l] * size, size)
        out[:rows, l * size : (l + 1) * size] = x[:, pl.ds(start, size)]
    row = lax.broadcasted_iota(i32, (rows, width), 0) + scal[0] * rows
    out[rows:, :] = jnp.where(row < scal[1], cotangent[...].astype(f32), 0.0).astype(bf16)


def head_choice(each, shards, position, my_heads, heads):
    h = lax.broadcasted_iota(i32, (my_heads, heads), 0)
    if each:
        shift = each.bit_length() - 1
        head_id = (h >> shift) * (heads // shards) + position * each + (h & (each - 1))
    else:
        head_id = position * my_heads + h
    return (lax.broadcasted_iota(i32, (my_heads, heads), 1) == head_id).astype(f32).astype(bf16)


def bucket_rows(scal, shards, offset):
    row = lax.broadcasted_iota(i32, (bucket_total, offset.shape[1]), 0)
    buckets = bucket_total // shards
    shift = buckets.bit_length() - 1
    bucket_id = jnp.zeros_like(row)
    for l in range(shards):
        bucket_id = jnp.where(
            (row >> shift) == l, scal[2 + l] * buckets + (row & (buckets - 1)), bucket_id
        )
    return (buckets_of(offset) == bucket_id).astype(f32).astype(bf16)


def qkv_kernel(blocks, parts, shards, each, scal, *refs):
    tokens_refs, weights = refs[:blocks], refs[blocks : blocks + parts]
    normed, qkv, bias, gains, scales, joined, small, sems, small_sems = refs[blocks + parts :]
    rows = tokens_refs[0].shape[0]
    tokens, width = normed.shape
    size = width // shards
    stride = sum(w.shape[0] for w in weights) // shards
    places = shard_places(weights, stride)
    step = pl.program_id(0)

    def copy(n, l):
        ref, at = places[l]
        return pltpu.make_async_copy(
            ref.at[pl.ds(at + n * size, size), :],
            joined.at[n, pl.ds(l * size, size), :],
            sems.at[n, l],
        )

    def small_copy(l):
        ref, at = places[l]
        return pltpu.make_async_copy(
            ref.at[pl.ds(at + stride - extra, extra), :], small.at[l], small_sems.at[l]
        )

    @at_step(0)
    def _():
        for l in range(shards):
            small_copy(l).start()
        for n in range(3):
            for l in range(shards):
                copy(n, l).start()
        for l in range(shards):
            small_copy(l).wait()
        my_heads = 2 * bias.shape[0]
        heads = my_heads * blocks
        buckets = bucket_total // shards
        tables = []
        for l in range(shards):
            value = small[l, :, :size].astype(f32)
            gains[:, l * size : (l + 1) * size] = value[:2]
            tables.append(value[2 : 2 + buckets, :heads])
        table = jnp.concatenate(tables, axis=0).astype(bf16)
        chosen = head_choice(each, shards, scal[0], my_heads, heads)
        mine = dot(chosen, table, 1, 1).astype(bf16)
        offset = tokens - lax.broadcasted_iota(i32, (1, 2 * tokens), 1)
        value = dot(mine, bucket_rows(scal, shards, offset))
        for pair in range(bias.shape[0]):
            bias[pair] = value[2 * pair : 2 * pair + 2]
        for t in range(blocks):
            at = slice(t * rows, (t + 1) * rows)
            x = tokens_refs[t][...].astype(f32)
            scale = lax.rsqrt(jnp.mean(x * x, axis=1, keepdims=True) + epsilon)
            normed[at, :] = (x * scale * gains[0:1, :]).astype(bf16)
            scales[at, :] = jnp.broadcast_to(scale, (rows, 128))

    for n in range(3):

        @at_step(n)
        def _():
            for l in range(shards):
                copy(n, l).wait()

    qkv[...] = dot(normed[...], joined[step]).astype(bf16)


def project(scal, tokens_all, weights, shards, each, pairs):
    rows, width = tokens_all[0].shape[0] // 2, tokens_all[0].shape[1]
    blocks = len(tokens_all)
    tokens = rows * blocks
    wide = 128 * pairs
    return call(
        functools.partial(qkv_kernel, blocks, len(weights), shards, each),
        (3,),
        [smem]
        + [pl.BlockSpec((rows, width), lambda n: (0, 0))] * blocks
        + [pl.BlockSpec(memory_space=ANY)] * len(weights),
        [
            pl.BlockSpec((tokens, width), lambda n: (0, 0)),
            pl.BlockSpec((tokens, wide), lambda n: (0, n)),
            pl.BlockSpec((pairs, 2, 2 * tokens), lambda n: (0, 0, 0)),
            pl.BlockSpec((2, width), lambda n: (0, 0)),
            pl.BlockSpec((tokens, 128), lambda n: (0, 0)),
        ],
        [
            struct((tokens, width), bf16),
            struct((tokens, 3 * wide), bf16),
            struct((pairs, 2, 2 * tokens), f32),
            struct((2, width), f32),
            struct((tokens, 128), f32),
        ],
        (scal, *tokens_all, *weights),
        [
            pltpu.VMEM((3, width, wide), bf16),
            pltpu.VMEM((shards, extra, wide), bf16),
            pltpu.SemaphoreType.DMA((3, shards)),
            pltpu.SemaphoreType.DMA((shards,)),
        ],
        flops=6 * tokens * width * wide,
    )


def lanes_of(position, blocks, rows, query, key):
    start = (blocks - 1 + (position ^ query) - (position ^ key)) * rows
    return pl.ds(pl.multiple_of(start, rows), rows)


def forward_kernel(rows, blocks, scal, q_ref, k_ref, v_ref, bias_ref, att, prob, toeplitz):
    position, length = scal[0], scal[1]
    width = 2 * blocks * rows
    slot = lax.broadcasted_iota(i32, (rows, rows), 0)
    for j in range(2):
        row = jnp.broadcast_to(bias_ref[0, j : j + 1, :], (rows, width))
        toeplitz[j] = pltpu.roll(row, width - rows, 1, stride=1, stride_axis=0)
    values = [v_ref[:, 64 * j : 64 * j + 64].astype(f32).T.astype(bf16) for j in range(2)]
    for t in range(blocks):
        at = slice(t * rows, (t + 1) * rows)
        halves = []
        for j in range(2):
            q = q_ref[at, 64 * j : 64 * j + 64]
            k = k_ref[:, 64 * j : 64 * j + 64]
            scores = dot(k, q, 1, 1)
            pieces = []
            for s in range(blocks):
                piece = (
                    scores[s * rows : (s + 1) * rows]
                    + toeplitz[j, :, lanes_of(position, blocks, rows, t, s)]
                )
                live = slot + (position ^ s) * rows < length
                pieces.append(jnp.where(live, piece, masked_score))
            scores = jnp.concatenate(pieces, axis=0)
            top = jnp.max(scores, axis=0, keepdims=True)
            e = jnp.exp(scores - top)
            probs = (e * (1.0 / jnp.sum(e, axis=0, keepdims=True))).astype(bf16)
            prob[j, :, at] = probs
            halves.append(dot(values[j], probs))
        att[at, :] = jnp.concatenate(halves, axis=0).T.astype(bf16)


def backward_kernel(
    rows, blocks, scal, q_ref, k_ref, v_ref, prob, gatt, gq, gk, gv, diag_ref, fold, ds_all
):
    position = scal[0]
    width = 2 * blocks * rows
    grads = [[], [], []]
    for j in range(2):
        columns = slice(64 * j, 64 * j + 64)
        k, v = k_ref[:, columns], v_ref[:, columns]
        fold[...] = jnp.zeros_like(fold)
        for t in range(blocks):
            at = slice(t * rows, (t + 1) * rows)
            gp = dot(v, gatt[at, columns], 1, 1)
            p = prob[j, :, at].astype(f32)
            pg = p * gp
            delta = jnp.sum(pg, axis=0, keepdims=True)
            ds = (pg - p * delta).astype(bf16)
            ds_all[:, at] = ds
            ds = ds.astype(f32)
            for s in range(blocks):
                fold[:, lanes_of(position, blocks, rows, t, s)] += ds[s * rows : (s + 1) * rows]
        grads[0].append(dot(k.astype(f32).T.astype(bf16), ds_all[...]))
        grads[1].append(dot(ds_all[...], q_ref[:, columns]))
        grads[2].append(dot(prob[j], gatt[:, columns]))
        a = fold[...]
        half = rows // 2
        while half >= 8:
            a = a[:half] + pltpu.roll(a[half:], width - half, 1)
            half //= 2
        row = lax.broadcasted_iota(i32, a.shape, 0)
        for bit in (1, 2, 4):
            a = jnp.where((row & bit) != 0, pltpu.roll(a, width - bit, 1), a)
        diag_ref[0, j : j + 1, :] = jnp.sum(a, axis=0, keepdims=True)
    gq[...] = jnp.concatenate(grads[0], axis=0).T.astype(bf16)
    gk[...] = jnp.concatenate(grads[1], axis=1).astype(bf16)
    gv[...] = jnp.concatenate(grads[2], axis=1).astype(bf16)


def attention_forward(scal, qkv, bias, rows, blocks):
    tokens = rows * blocks
    pairs = bias.shape[0]
    return call(
        functools.partial(forward_kernel, rows, blocks),
        (pairs,),
        [smem]
        + [pl.BlockSpec((tokens, 128), lambda p, n=n: (0, n * pairs + p)) for n in range(3)]
        + [pl.BlockSpec((1, 2, 2 * tokens), lambda p: (p, 0, 0))],
        [
            pl.BlockSpec((tokens, 128), lambda p: (0, p)),
            pl.BlockSpec((2, tokens, tokens), lambda p: (p, 0, 0)),
        ],
        [struct((tokens, 128 * pairs), bf16), struct((2 * pairs, tokens, tokens), bf16)],
        (scal, qkv, qkv, qkv, bias),
        [pltpu.VMEM((2, rows, 2 * tokens), f32)],
        flops=8 * pairs * tokens * tokens * 64,
        exps=2 * pairs * tokens * tokens,
    )


def attention_backward(scal, qkv, probs, grad_att, rows, blocks):
    tokens = rows * blocks
    pairs = probs.shape[0] // 2
    block = pl.BlockSpec((tokens, 128), lambda p: (0, p))
    return call(
        functools.partial(backward_kernel, rows, blocks),
        (pairs,),
        [smem]
        + [pl.BlockSpec((tokens, 128), lambda p, n=n: (0, n * pairs + p)) for n in range(3)]
        + [pl.BlockSpec((2, tokens, tokens), lambda p: (p, 0, 0)), block],
        [block, block, block, pl.BlockSpec((1, 2, 2 * tokens), lambda p: (p, 0, 0))],
        [struct((tokens, 128 * pairs), bf16)] * 3 + [struct((pairs, 2, 2 * tokens), f32)],
        (scal, qkv, qkv, qkv, probs, grad_att),
        [pltpu.VMEM((rows, 2 * tokens), f32), pltpu.VMEM((tokens, tokens), bf16)],
        flops=16 * pairs * tokens * tokens * 64,
    )


def out_copies(shards, scal, weights, joined, sems):
    blocks, depth, _ = joined.shape
    size = depth // shards
    stride = sum(w.shape[0] for w in weights) // shards
    first = stride - extra - blocks * size
    copies = []
    for b in range(blocks):
        for l, (ref, at) in enumerate(shard_places(weights, stride)):
            start = pl.multiple_of(scal[2 + l] * size, size)
            copies.append(
                pltpu.make_async_copy(
                    ref.at[pl.ds(at + first + b * size, size), :],
                    joined.at[b, pl.ds(start, size), :],
                    sems.at[b, l],
                )
            )
    return copies


def out_kernel(blocks, parts, shards, scal, att, *refs):
    weights, outs, joined, sems = refs[:parts], refs[parts:-2], refs[-2], refs[-1]
    copies = out_copies(shards, scal, weights, joined, sems)
    for c in copies:
        c.start()
    rows = outs[0].shape[0]
    wide = joined.shape[2]
    for b in range(joined.shape[0]):
        for c in copies[b * shards : (b + 1) * shards]:
            c.wait()
        total = dot(att[...], joined[b]).astype(bf16)
        for t in range(blocks):
            outs[t][:, b * wide : (b + 1) * wide] = total[t * rows : (t + 1) * rows]


def multiply_out(scal, att, weights, shards, blocks):
    tokens, wide = att.shape
    rows, width = tokens // blocks, wide * blocks
    return call(
        functools.partial(out_kernel, blocks, len(weights), shards),
        (1,),
        [smem, whole(att)] + [pl.BlockSpec(memory_space=ANY)] * len(weights),
        [pl.BlockSpec((rows, width), lambda i: (0, 0))] * blocks,
        [struct((rows, width), bf16)] * blocks,
        (scal, att, *weights),
        [pltpu.VMEM((blocks, wide, wide), bf16), pltpu.SemaphoreType.DMA((blocks, shards))],
        flops=2 * tokens * wide * width,
    )


def grad_attended_kernel(blocks, parts, shards, scal, *refs):
    low, weights = refs[:blocks], refs[blocks : blocks + parts]
    out, joined, sems = refs[blocks + parts :]
    copies = out_copies(shards, scal, weights, joined, sems)
    for c in copies:
        c.start()
    wide = joined.shape[2]
    total = None
    for b in range(joined.shape[0]):
        for c in copies[b * shards : (b + 1) * shards]:
            c.wait()
        part = jnp.concatenate([ref[:, b * wide : (b + 1) * wide] for ref in low], axis=0)
        term = dot(part, joined[b], 1, 1)
        total = term if total is None else total + term
    out[...] = total.astype(bf16)


def make_grad_attended(scal, low_all, weights, shards):
    blocks = len(low_all)
    rows, width = low_all[0].shape
    tokens, wide = rows * blocks, width // blocks
    return call(
        functools.partial(grad_attended_kernel, blocks, len(weights), shards),
        (1,),
        [smem] + [whole(a) for a in low_all] + [pl.BlockSpec(memory_space=ANY)] * len(weights),
        [pl.BlockSpec((tokens, wide), lambda i: (0, 0))],
        [struct((tokens, wide), bf16)],
        (scal, *low_all, *weights),
        [pltpu.VMEM((blocks, wide, wide), bf16), pltpu.SemaphoreType.DMA((blocks, shards))],
        flops=2 * tokens * wide * width,
    )[0]


def hidden_kernel(blocks, shards, scal, x, gains, *refs):
    parts, hidden, nffn = refs[:blocks], refs[blocks], refs[blocks + 1]
    total = x[...].astype(f32)
    for part in parts:
        total = total + part[...].astype(f32)
    hidden[...] = total
    scale = lax.rsqrt(jnp.mean(total * total, axis=1, keepdims=True) + epsilon)
    size = total.shape[1] // shards
    for l in range(shards):
        at = slice(l * size, (l + 1) * size)
        start = pl.multiple_of(scal[2 + l] * size, size)
        nffn[:, at] = (hidden[:, pl.ds(start, size)] * scale * gains[1:2, at]).astype(bf16)


def make_hidden(scal, x, gains, parts, shards):
    rows, width = x.shape
    args = (scal, x, gains, *parts)
    return call(
        functools.partial(hidden_kernel, len(parts), shards),
        (1,),
        [smem] + [whole(a) for a in args[1:]],
        [pl.BlockSpec((rows, width), lambda i: (0, 0))] * 2,
        [struct((rows, width), f32), struct((rows, width), bf16)],
        args,
    )


def gelu_tanh(g):
    return jnp.tanh(0.7978845608028654 * (g + 0.044715 * (g * g * g)))


def units_kernel(blocks, parts, tile, *refs):
    tokens_refs, weights = refs[:blocks], refs[blocks : blocks + parts]
    normed, gate, up, mixed, joined, sems = refs[blocks + parts :]
    rows = tokens_refs[0].shape[0]
    units = weights[0].shape[1] // 2
    step = pl.program_id(0)

    def copies(i):
        result, at = [], 0
        for w, ref in enumerate(weights):
            for n in range(2):
                result.append(
                    pltpu.make_async_copy(
                        ref.at[:, pl.ds(n * units + i * tile, tile)],
                        joined.at[i, pl.ds(at, ref.shape[0]), pl.ds(n * tile, tile)],
                        sems.at[i, 2 * w + n],
                    )
                )
            at += ref.shape[0]
        return result

    @at_step(0)
    def _():
        for i in range(units // tile):
            for c in copies(i):
                c.start()
        for t in range(blocks):
            normed[t * rows : (t + 1) * rows, :] = tokens_refs[t][...]

    for i in range(units // tile):

        @at_step(i)
        def _():
            for c in copies(i):
                c.wait()

    both = dot(normed[...], joined[step])
    g, u = both[:, :tile], both[:, tile:]
    gate[...] = g
    up[...] = u
    mixed[...] = (0.5 * g * (1.0 + gelu_tanh(g)) * u).astype(bf16)


def make_units(tokens_all, weights):
    rows, width = tokens_all[0].shape
    blocks = len(tokens_all)
    tokens = rows * blocks
    units = weights[0].shape[1] // 2
    tile = tile_of(units, 256)
    steps = units // tile
    out = pl.BlockSpec((tokens, tile), lambda i: (0, i))
    return call(
        functools.partial(units_kernel, blocks, len(weights), tile),
        (steps,),
        [whole(a) for a in tokens_all] + [pl.BlockSpec(memory_space=ANY)] * len(weights),
        [pl.BlockSpec((tokens, width), lambda i: (0, 0)), out, out, out],
        [
            struct((tokens, width), bf16),
            struct((tokens, units), f32),
            struct((tokens, units), f32),
            struct((tokens, units), bf16),
        ],
        (*tokens_all, *weights),
        [
            pltpu.VMEM((steps, width, 2 * tile), bf16),
            pltpu.SemaphoreType.DMA((steps, 2 * len(weights))),
        ],
        flops=4 * tokens * width * units,
    )


def grad_down_kernel(blocks, shards, scal, mixed, *refs):
    dy, outs, turned, low = refs[:blocks], refs[blocks:-2], refs[-2], refs[-1]

    @at_step(0)
    def _():
        turned[...] = mixed[...].T

    low[...] = dot(turned[...], jnp.concatenate([r[...] for r in dy], axis=0)).astype(bf16)
    size = low.shape[0] // shards
    each = shards // len(outs)
    for l in range(shards):
        start = pl.multiple_of(scal[2 + l] * size, size)
        outs[side_of(shards)[l][0]][pl.ds(side_of(shards)[l][1] * size, size), :] = low[
            pl.ds(start, size), :
        ]


def side_of(shards):
    chips = shards // 2
    sides, counts = [], [0, 0]
    for slots in (near_slots(chips), far_slots(chips)):
        for p in range(2):
            for _ in slots:
                sides.append((p, counts[p]))
                counts[p] += 1
    return sides


def make_grad_down(scal, mixed, tokens_all, shards):
    blocks = len(tokens_all)
    tokens, units = mixed.shape
    rows, width = tokens // blocks, tokens_all[0].shape[1]
    tile = tile_of(width, 512)
    return call(
        functools.partial(grad_down_kernel, blocks, shards),
        (width // tile,),
        [smem, whole(mixed)] + [pl.BlockSpec((rows, tile), lambda i: (1, i))] * blocks,
        [pl.BlockSpec((units // 2, tile), lambda i: (0, i))] * 2,
        [struct((units // 2, width), bf16)] * 2,
        (scal, mixed, *tokens_all),
        [pltpu.VMEM((units, tokens), bf16), pltpu.VMEM((units, tile), bf16)],
        flops=2 * tokens * units * width,
    )


def down_copies(shards, scal, weights, joined, sems):
    size = joined.shape[0] // shards
    copies = []
    for l, (ref, at) in enumerate(shard_places(weights, size)):
        start = pl.multiple_of(scal[2 + l] * size, size) if shards > 1 else 0
        copies.append(
            pltpu.make_async_copy(
                ref.at[pl.ds(at, size), :], joined.at[pl.ds(start, size), :], sems.at[l]
            )
        )
    return copies


def units_back_kernel(blocks, parts, shards, tile, scal, gate, up, *refs):
    dy, weights = refs[:blocks], refs[blocks : blocks + parts]
    out, joined, grads, sems = refs[blocks + parts :]
    step = pl.program_id(0)
    rows = dy[0].shape[0]
    units = joined.shape[0]

    @at_step(0)
    def _():
        copies = down_copies(shards, scal, weights, joined, sems)
        for c in copies:
            c.start()
        for t in range(blocks):
            grads[t * rows : (t + 1) * rows, :] = dy[t][...]
        for c in copies:
            c.wait()

    weight = joined[pl.ds(pl.multiple_of(step * tile, tile), tile), :]
    grad = dot(grads[...], weight, 1, 1)
    g, u = gate[...], up[...]
    t = gelu_tanh(g)
    slope = 0.5 * (1.0 + t) + 0.5 * g * (1.0 - t * t) * (
        0.7978845608028654 * (1.0 + 3 * 0.044715 * (g * g))
    )
    out[:, pl.ds(pl.multiple_of(step * tile, tile), tile)] = (grad * u * slope).astype(bf16)
    out[:, pl.ds(pl.multiple_of(units + step * tile, tile), tile)] = (
        grad * (0.5 * g * (1.0 + t))
    ).astype(bf16)


def units_back(scal, gate, up, tokens_all, weights, shards):
    blocks = len(tokens_all)
    tokens, units = gate.shape
    rows, width = tokens // blocks, tokens_all[0].shape[1]
    tile = tile_of(units, 256)
    block = pl.BlockSpec((tokens, tile), lambda i: (0, i))
    return call(
        functools.partial(units_back_kernel, blocks, len(weights), shards, tile),
        (units // tile,),
        [smem, block, block]
        + [pl.BlockSpec((rows, width), lambda i: (1, 0))] * blocks
        + [pl.BlockSpec(memory_space=ANY)] * len(weights),
        [pl.BlockSpec((tokens, 2 * units), lambda i: (0, 0))],
        [struct((tokens, 2 * units), bf16)],
        (scal, gate, up, *tokens_all, *weights),
        [
            pltpu.VMEM((units, width), bf16),
            pltpu.VMEM((tokens, width), bf16),
            pltpu.SemaphoreType.DMA((shards,)),
        ],
        flops=2 * tokens * units * width,
    )[0]


def result_kernel(blocks, parts, shards, tile, scal, mixed, *refs):
    weights, outs, joined, sems = refs[:parts], refs[parts:-2], refs[-2], refs[-1]
    start_and_wait(down_copies(shards, scal, weights, joined, sems))
    rows, width = outs[0].shape
    for i in range(width // tile):
        at = slice(i * tile, (i + 1) * tile)
        total = dot(mixed[...], joined[:, at]).astype(bf16)
        for t in range(blocks):
            outs[t][:, at] = total[t * rows : (t + 1) * rows]


def multiply_down(scal, mixed, weights, shards, blocks):
    tokens, units = mixed.shape
    width = weights[0].shape[1]
    rows = tokens // blocks
    return call(
        functools.partial(result_kernel, blocks, len(weights), shards, tile_of(width, 512)),
        (1,),
        [smem, whole(mixed)] + [pl.BlockSpec(memory_space=ANY)] * len(weights),
        [pl.BlockSpec((rows, width), lambda i: (0, 0))] * blocks,
        [struct((rows, width), bf16)] * blocks,
        (scal, mixed, *weights),
        [pltpu.VMEM((units, width), bf16), pltpu.SemaphoreType.DMA((shards,))],
        flops=2 * tokens * units * width,
    )


def ffn_transposed_kernel(parts, blocks, g, *refs):
    weights, outs = refs[:parts], refs[parts : parts + blocks]
    held, sems = refs[parts + blocks : -1], refs[-1]
    rows = outs[0].shape[0]
    copies = [pltpu.make_async_copy(w, h, sems.at[i]) for i, (w, h) in enumerate(zip(weights, held))]
    order = sorted(range(parts), key=lambda i: held[i].shape[0])
    first = [sum(h.shape[0] for h in held[:i]) for i in range(parts)]
    for i in order[:2]:
        copies[i].start()
    for n, i in enumerate(order):
        copies[i].wait()
        if n + 2 < parts:
            copies[order[n + 2]].start()
        tile = held[i].shape[0] if held[i].shape[0] <= 768 else tile_of(held[i].shape[0], 512)
        for row in range(0, held[i].shape[0], tile):
            total = dot(g[...], held[i][row : row + tile, :], 1, 1).astype(bf16)
            at = first[i] + row
            for t, out in enumerate(outs):
                out[:, at : at + tile] = total[t * rows : (t + 1) * rows]


def ffn_transposed(g, weights, blocks):
    tokens, depth = g.shape
    rows, width = tokens // blocks, sum(w.shape[0] for w in weights)
    return call(
        functools.partial(ffn_transposed_kernel, len(weights), blocks),
        (1,),
        [whole(g)] + [pl.BlockSpec(memory_space=ANY)] * len(weights),
        [pl.BlockSpec((rows, width), lambda i: (0, 0))] * blocks,
        [struct((rows, width), bf16)] * blocks,
        (g, *weights),
        [pltpu.VMEM(w.shape, bf16) for w in weights]
        + [pltpu.SemaphoreType.DMA((len(weights),))],
        flops=2 * tokens * depth * width,
    )


def units_grad_kernel(shards, scal, normed, g, *refs):
    outs, turned = refs[:-1], refs[-1]

    @at_step(0)
    def _():
        turned[...] = normed[...].T

    total = dot(turned[...], g[...]).astype(bf16)
    at = 0
    for out in outs[:2]:
        n = out.shape[0]
        out[...] = total[at : at + n]
        at += n
    if len(outs) == 3:
        size = outs[2].shape[0] // 2
        core = scal[2] & 1
        for n, place in enumerate((core, 1 - core)):
            start = pl.multiple_of(place * size, size)
            outs[2][pl.ds(start, size), :] = total[at + n * size : at + (n + 1) * size]


def units_grad(scal, normed, g, shards):
    tokens, depth = normed.shape
    width = g.shape[1]
    tile = tile_of(width, 512)
    size = depth // shards
    sizes = [len(near_slots(shards // 2)) * size] * 2
    if far_slots(shards // 2):
        sizes.append(2 * size)
    return call(
        functools.partial(units_grad_kernel, shards),
        (width // tile,),
        [smem, whole(normed), pl.BlockSpec((tokens, tile), lambda i: (0, i))],
        [pl.BlockSpec((n, tile), lambda i: (0, i)) for n in sizes],
        [struct((n, width), bf16) for n in sizes],
        (scal, normed, g),
        [pltpu.VMEM((depth, tokens), bf16)],
        flops=2 * tokens * depth * width,
    )


def attn_transposed_kernel(blocks, parts, shards, scales, gq, gk, gv, *refs):
    tokens_refs, weights = refs[:blocks], refs[blocks : blocks + parts]
    outs = refs[blocks + parts : 2 * blocks + parts]
    gain, held, sems = refs[2 * blocks + parts :]
    rows, size = outs[0].shape
    stride = sum(w.shape[0] for w in weights) // shards
    step = pl.program_id(0)

    def copy(l):
        ref, at = shard_places(weights, stride)[l]
        return pltpu.make_async_copy(ref.at[pl.ds(at, 3 * size), :], held.at[l], sems.at[l])

    @at_step(0)
    def _():
        for l in range(shards):
            copy(l).start()

    for l in range(shards):

        @at_step(l)
        def _():
            copy(l).wait()

    total = None
    for n, g in enumerate((gq, gk, gv)):
        term = dot(g[...], held[step, n * size : (n + 1) * size, :], 1, 1)
        total = term if total is None else total + term
    summed = jnp.zeros((1, size), f32)
    for t, out in enumerate(outs):
        at = slice(t * rows, (t + 1) * rows)
        out[...] = total[at].astype(bf16)
        unit = tokens_refs[t][...].astype(f32) * scales[at, 0:1]
        summed = summed + jnp.sum(total[at] * unit, axis=0, keepdims=True)
    gain[...] = summed


def attn_transposed(scales, grads, tokens_all, weights, size, shards, blocks):
    tokens, wide = grads[0].shape
    rows, width = tokens // blocks, size * shards
    tile = pl.BlockSpec((rows, size), lambda l: (0, l))
    results = call(
        functools.partial(attn_transposed_kernel, blocks, len(weights), shards),
        (shards,),
        [whole(scales)]
        + [whole(g) for g in grads]
        + [tile] * blocks
        + [pl.BlockSpec(memory_space=ANY)] * len(weights),
        [tile] * blocks + [pl.BlockSpec((1, size), lambda l: (0, l))],
        [struct((rows, width), bf16)] * blocks + [struct((1, width), f32)],
        (scales, *grads, *tokens_all, *weights),
        [
            pltpu.VMEM((shards, 3 * size, wide), bf16),
            pltpu.SemaphoreType.DMA((shards,)),
        ],
        flops=6 * tokens * wide * width,
    )
    return results[:-1], results[-1]


def split_low(a):
    high = a.astype(bf16)
    return high, (a - high.astype(f32)).astype(bf16)


def owner_counts(shards):
    counts = []
    for slots in (near_slots(shards // 2), far_slots(shards // 2)):
        if slots:
            counts += [len(slots)] * 2
    return counts


def shard_owners(outs, shards):
    return [out for out, n in zip(outs, owner_counts(shards)) for _ in range(n)]


def attn_grad_kernel(
    blocks, shards, each, with_out, scal, normed, att, gq, gk, gv, diag, gain_attn, gain_ffn, *refs
):
    low = refs[:blocks]
    outs, (joined, turned, table) = refs[blocks:-3], refs[-3:]
    tokens, width = normed.shape
    wide = att.shape[1]
    size = width // shards
    head_rows = wide // shards
    rows = tokens // blocks
    my_heads = 2 * diag.shape[0]
    heads = my_heads * blocks

    @at_step(0)
    def _():
        for n, g in enumerate((gq, gk, gv)):
            joined[:, n * wide : (n + 1) * wide] = g[...]
        if with_out:
            turned[...] = dot(
                att[...].T, jnp.concatenate([r[...] for r in low], axis=0)
            ).astype(bf16)
        lane = lax.broadcasted_iota(i32, (1, 2 * tokens), 1)
        lane = jnp.where(lane < 2 * tokens - rows, lane, lane - 2 * tokens)
        of_offset = bucket_rows(scal, shards, (blocks - 1) * rows - lane)
        sums = jnp.concatenate([diag[p] for p in range(diag.shape[0])], axis=0)
        total = None
        for part in split_low(sums):
            term = dot(of_offset, part, 1, 1)
            total = term if total is None else total + term
        chosen = head_choice(each, shards, scal[0], my_heads, heads)
        value = None
        for part in split_low(total):
            term = dot(part, chosen)
            value = term if value is None else value + term
        table[...] = value

    buckets = bucket_total // shards
    for l, out in enumerate(shard_owners(outs, shards)):

        @at_step(l)
        def _():
            total = dot(normed[:, l * size : (l + 1) * size], joined[...], 0, 0).astype(bf16)
            for n in range(3):
                out[n * size : (n + 1) * size, :] = total[:, n * wide : (n + 1) * wide]
            if with_out:
                start = pl.multiple_of(scal[2 + l] * head_rows, head_rows)
                for b in range(blocks):
                    out[3 * size + b * head_rows : 3 * size + (b + 1) * head_rows, :] = turned[
                        pl.ds(start, head_rows), b * wide : (b + 1) * wide
                    ]
            part = jnp.concatenate(
                [
                    jnp.zeros((2, heads), f32),
                    table[l * buckets : (l + 1) * buckets, :],
                    jnp.zeros((extra - 2 - buckets, heads), f32),
                ],
                axis=0,
            )
            part = jnp.concatenate([part, jnp.zeros((extra, size - heads), f32)], axis=1)
            row = lax.broadcasted_iota(i32, (extra, size), 0)
            columns = slice(l * size, (l + 1) * size)
            part = part + jnp.where(
                row == 0,
                gain_attn[:, columns],
                jnp.where(row == 1, gain_ffn[:, columns], 0.0),
            )
            last = out.shape[0] - extra
            out[last:, :] = jnp.zeros((extra, wide), bf16)
            out[last:, :size] = part.astype(bf16)


def attn_grad(scal, normed, att, grads, diag, gain_attn, gain_ffn, low_all, shards, each, stride):
    tokens, width = normed.shape
    wide = att.shape[1]
    blocks = len(low_all)
    counts = owner_counts(shards)
    specs, first = [], 0
    for n in counts:
        specs.append(
            pl.BlockSpec((stride, wide), lambda l, f=first, n=n: (jnp.clip(l - f, 0, n - 1), 0))
        )
        first += n
    args = (scal, normed, att, *grads, diag, gain_attn, gain_ffn, *low_all)
    return call(
        functools.partial(attn_grad_kernel, blocks, shards, each, bool(each)),
        (shards,),
        [smem] + [whole(a) for a in args[1:]],
        specs,
        [struct((n * stride, wide), bf16) for n in counts],
        args,
        [
            pltpu.VMEM((tokens, 3 * wide), bf16),
            pltpu.VMEM((wide, width), bf16),
            pltpu.VMEM((bucket_total, 2 * diag.shape[0] * blocks), f32),
        ],
        flops=8 * tokens * wide * width,
    )


def ffn_norm_back_kernel(blocks, shards, scal, hidden, gains, own, *refs):
    parts = refs[:blocks]
    grad_hidden, low, grad_gain, g, gain = refs[blocks:]
    size = hidden.shape[1] // shards
    for l in range(shards):
        at = slice(l * size, (l + 1) * size)
        start = pl.multiple_of(scal[2 + l] * size, size)
        total = parts[0][:, at].astype(f32)
        for part in parts[1:]:
            total = total + part[:, at].astype(f32)
        g[:, pl.ds(start, size)] = total
        gain[:, pl.ds(start, size)] = gains[1:2, at]
    h = hidden[...]
    scale = lax.rsqrt(jnp.mean(h * h, axis=1, keepdims=True) + epsilon)
    weighted = g[...] * gain[...]
    inner = jnp.mean(weighted * h, axis=1, keepdims=True)
    value = own[...].astype(f32) + scale * weighted - h * (scale * scale * scale) * inner
    grad_hidden[...] = value
    low[...] = value.astype(bf16)
    g[...] = g[...] * h * scale
    for l in range(shards):
        start = pl.multiple_of(scal[2 + l] * size, size)
        grad_gain[:, l * size : (l + 1) * size] = jnp.sum(
            g[:, pl.ds(start, size)], axis=0, keepdims=True
        )


def ffn_norm_back(scal, hidden, gains, own, parts, shards):
    rows, width = hidden.shape
    block = pl.BlockSpec((rows, width), lambda i: (0, 0))
    return call(
        functools.partial(ffn_norm_back_kernel, len(parts), shards),
        (1,),
        [smem, block, whole(gains), pl.BlockSpec((rows, width), lambda i: (1, 0))]
        + [block] * len(parts),
        [block, block, pl.BlockSpec((1, width), lambda i: (0, 0))],
        [struct((rows, width), f32), struct((rows, width), bf16), struct((1, width), f32)],
        (scal, hidden, gains, own, *parts),
        [pltpu.VMEM((rows, width), f32), pltpu.VMEM((1, width), f32)],
    )


def attn_norm_back_kernel(blocks, shards, scal, grad_hidden, gains, own, *refs):
    parts = refs[:blocks]
    grad, value = refs[blocks:]
    x = own[...].astype(f32)
    g = parts[0][...].astype(f32)
    for part in parts[1:]:
        g = g + part[...].astype(f32)
    scale = lax.rsqrt(jnp.mean(x * x, axis=1, keepdims=True) + epsilon)
    weighted = g * gains[0:1, :]
    inner = jnp.mean(weighted * x, axis=1, keepdims=True)
    value[...] = scale * weighted - x * (scale * scale * scale) * inner
    size = x.shape[1] // shards
    for l in range(shards):
        at = slice(l * size, (l + 1) * size)
        where = pl.ds(pl.multiple_of(scal[2 + l] * size, size), size)
        grad[:, where] = (grad_hidden[:, where] + value[:, at]).astype(bf16)


def attn_norm_back(scal, grad_hidden, gains, own, parts, shards):
    rows, width = grad_hidden.shape
    block = pl.BlockSpec((rows, width), lambda i: (0, 0))
    return call(
        functools.partial(attn_norm_back_kernel, len(parts), shards),
        (1,),
        [smem, block, whole(gains), block] + [block] * len(parts),
        [block],
        [struct((rows, width), bf16)],
        (scal, grad_hidden, gains, own, *parts),
        [pltpu.VMEM((rows, width), f32)],
    )[0]


def by_position(scal, blocks, body):
    for p in range(blocks):

        @pl.when(scal[0] == p)
        def _():
            body([p ^ c for c in range(blocks)])


def columns_kernel(groups, scal, *refs):
    pieces, outs = refs[:-2], refs[-2:]
    blocks = len(pieces)
    units = pieces[0].shape[1] // 2
    size = units // groups
    wide = blocks * size

    def body(order):
        for n, out in enumerate(outs):
            for g in range(groups):
                at = n * units + g * size
                out[:, g * wide : (g + 1) * wide] = jnp.concatenate(
                    [pieces[t][:, at : at + size] for t in order], axis=1
                ).astype(f32)

    by_position(scal, blocks, body)


def assemble_units(scal, pieces, groups):
    rows, columns = pieces[0].shape
    tile = min(rows, 32)
    wide = len(pieces) * columns // 2
    return call(
        functools.partial(columns_kernel, groups),
        (rows // tile,),
        [smem] + [pl.BlockSpec((tile, columns), lambda i: (i, 0))] * len(pieces),
        [pl.BlockSpec((tile, wide), lambda i: (i, 0))] * 2,
        [struct((rows, wide), f32)] * 2,
        (scal, *pieces),
    )


def rows_kernel(size, scal, *refs):
    position = scal[0]
    for t, piece in enumerate(refs[:-1]):
        start = pl.multiple_of((position ^ t) * size, 8)
        refs[-1][pl.ds(start, size), :] = piece[...].astype(f32)


def assemble_rows(scal, pieces):
    rows, columns = pieces[0].shape
    tile = tile_of(columns, 512)
    return call(
        functools.partial(rows_kernel, rows),
        (columns // tile,),
        [smem] + [pl.BlockSpec((rows, tile), lambda i: (0, i))] * len(pieces),
        [pl.BlockSpec((rows * len(pieces), tile), lambda i: (0, i))],
        [struct((rows * len(pieces), columns), f32)],
        (scal, *pieces),
    )[0]


def attention_outputs_kernel(each, blocks, head_width, count, last, scal, *refs):
    columns, rest = refs[: count * blocks], refs[count * blocks :]
    with_out = last and bool(each)
    out_blocks = rest[:blocks] if with_out else ()
    rest = rest[blocks:] if with_out else rest
    small, outs = (rest[:blocks], rest[blocks:]) if last else ((), rest)
    wide = columns[0].shape[1]
    step = pl.program_id(0)

    def body(order):
        for n in range(count):
            pieces = [columns[count * t + n] for t in order]
            if each:
                size = each * head_width
                for g in range(wide // size):
                    outs[n][:, g * blocks * size : (g + 1) * blocks * size] = jnp.concatenate(
                        [ref[:, g * size : (g + 1) * size] for ref in pieces], axis=1
                    ).astype(f32)
            else:
                for c, ref in enumerate(pieces):
                    outs[n][:, c * wide : (c + 1) * wide] = ref[...].astype(f32)

        if last:

            @at_step(0)
            def _():
                total = small[order[0]][...].astype(f32)
                for t in order[1:]:
                    total = total + small[t][...].astype(f32)
                outs[-1][...] = total

    by_position(scal, blocks, body)
    if with_out:
        for t in range(blocks):

            @pl.when((step ^ scal[0]) == t)
            def _():
                size = outs[count].shape[0]
                for b in range(blocks):
                    outs[count][:, b * wide : (b + 1) * wide] = out_blocks[t][
                        b * size : (b + 1) * size, :
                    ].astype(f32)


def attention_outputs(scal, pieces, count, rows, each, head_width, last):
    blocks = len(pieces)
    total, wide = pieces[0].shape
    tile = rows // blocks
    per = rows // tile
    specs, args = [], []
    for a in pieces:
        for n in range(count):
            specs.append(pl.BlockSpec((tile, wide), lambda i, n=n: (n * per + i, 0)))
            args.append(a)
    outputs = count
    if last and each:
        specs += [pl.BlockSpec((rows, wide), lambda i: (count, 0))] * blocks
        args += pieces
        outputs += 1
    if last:
        specs += [pl.BlockSpec((extra, wide), lambda i: (total // extra - 1, 0))] * blocks
        args += pieces
    block = pl.BlockSpec((tile, wide * blocks), lambda i: (i, 0))
    out_specs, out_shape = [block] * outputs, [struct((rows, wide * blocks), f32)] * outputs
    if last:
        out_specs.append(pl.BlockSpec((extra, wide), lambda i: (0, 0)))
        out_shape.append(struct((extra, wide), f32))
    return call(
        functools.partial(attention_outputs_kernel, each, blocks, head_width, count, last),
        (blocks,),
        [smem] + specs,
        out_specs,
        out_shape,
        (scal, *args),
    )


def take_blocks(a, starts, size):
    return jnp.concatenate([lax.dynamic_slice_in_dim(a, s, size, 0) for s in starts], 0)


def on_device(
    inputs,
    lengths,
    w_query,
    w_key,
    w_value,
    w_out,
    w_gate,
    w_up,
    w_down,
    norm_attn,
    norm_ffn,
    relative_bias_table,
    cotangent,
):
    blocks = lax.axis_size("ctx")
    shards = lax.axis_size("fsdp")
    chips = shards // 2
    position = lax.axis_index("ctx")
    shard = lax.axis_index("fsdp")
    chip, core = shard // 2, shard % 2
    rows, width = inputs.shape[1], inputs.shape[2]
    tokens = rows * blocks
    heads = relative_bias_table.shape[1]
    head_width = width // heads
    my_heads = heads // blocks
    pairs = my_heads // 2
    each = heads // shards // blocks if (heads // shards) % blocks == 0 else 0
    strided = each in (1, 2)
    each = each if strided else 0
    units = w_gate.shape[1] // blocks
    shard_rows = width // shards
    unit_rows = w_down.shape[0] // blocks

    slot_of, parity_of = [], []
    for slots in (near_slots(chips), far_slots(chips)):
        for p in range(2):
            slot_of += slots
            parity_of += [p] * len(slots)
    pad = [0, 0]
    order = 2 * ((chip + jnp.array(pad + slot_of, i32)) % chips) + (
        core ^ jnp.array(pad + parity_of, i32)
    )
    index = jnp.arange(shards + 2, dtype=i32)
    scal = jnp.where(index == 0, position, jnp.where(index == 1, lengths[0], order)).astype(i32)

    def heads_of(c):
        if strided:
            return [
                (h // each) * (heads // shards) + c * each + h % each for h in range(my_heads)
            ]
        return [c * my_heads + h for h in range(my_heads)]

    args = (
        scal,
        w_query,
        w_key,
        w_value,
        w_out,
        norm_attn.reshape(1, -1),
        norm_ffn.reshape(1, -1),
        relative_bias_table,
    )
    stride = (4 if strided else 3) * shard_rows + extra
    own_attn = call(
        functools.partial(
            choose_attention_kernel, [heads_of(c) for c in range(blocks)], head_width, strided
        ),
        (1,),
        [smem] + [whole(a) for a in args[1:]],
        [pl.BlockSpec((stride, 128 * pairs), lambda i: (0, 0))],
        [struct((stride, 128 * pairs), bf16)],
        args,
    )[0]
    near_attn = gather_near(own_attn)
    own_tokens = call(
        functools.partial(tokens_kernel, shards),
        (1,),
        [smem] + [pl.BlockSpec((rows, width), lambda i: (0, 0))] * 2,
        [pl.BlockSpec((2 * rows, width), lambda i: (0, 0))],
        [struct((2 * rows, width), bf16)],
        (after(scal, own_attn), inputs[0], cotangent[0]),
    )[0]
    all_tokens = ctx_gather(own_tokens)
    tile = tile_of(shard_rows, 64)
    own_gate_up = call(
        functools.partial(choose_units_kernel, shards),
        (shard_rows // tile,),
        [smem] + [pl.BlockSpec((tile, w_gate.shape[1]), lambda i: (i, 0))] * 2,
        [pl.BlockSpec((tile, 2 * units), lambda i: (i, 0))],
        [struct((shard_rows, 2 * units), bf16)],
        (after(scal, own_tokens), w_gate, w_up),
    )[0]
    joint = together([*near_attn, *all_tokens], own_gate_up)
    near_attn, all_tokens = joint[: len(near_attn)], joint[len(near_attn) :]
    far_attn = gather_far(near_attn, chip)
    n = len(near_attn)
    joint = together([core_swap(a) for a in near_attn] + far_attn)
    weights_attn, far_attn = [*near_attn, *joint[:n]], joint[n:]
    near_gate_up = gather_near(after(own_gate_up, *far_attn))
    weights_attn += with_other_core(far_attn)
    if not strided:
        gathered = lax.all_gather(w_out, "fsdp", axis=0, tiled=True)
        size = my_heads * head_width
        full_out = lax.dynamic_slice_in_dim(gathered, position * size, size, 0)

    normed, qkv, bias, gains, scales = project(
        scal, all_tokens, weights_attn, shards, each, pairs
    )
    attended, probs = attention_forward(scal, qkv, bias, rows, blocks)
    if strided:
        parts = multiply_out(scal, attended, weights_attn, shards, blocks)
    else:
        whole_part = dot(attended, full_out).astype(bf16)
        parts = [whole_part[t * rows : (t + 1) * rows] for t in range(blocks)]
    parts = ctx_exchange(parts)
    hidden, own_nffn = make_hidden(scal, inputs[0], gains, parts, shards)

    near_gate_up = together(near_gate_up, own_nffn)
    far_gate_up = gather_far(near_gate_up, chip)
    joint = together(with_other_core(near_gate_up) + ctx_gather(own_nffn) + far_gate_up)
    weights_gate_up = list(joint[:2])
    all_nffn, far_gate_up = joint[2 : 2 + blocks], joint[2 + blocks :]
    own_down = lax.dynamic_slice_in_dim(w_down, position * unit_rows, unit_rows, 0)
    near_down = gather_near(after(own_down, all_nffn[0]))
    weights_gate_up += with_other_core(far_gate_up)
    normed_ffn, gate, up, mixed_units = make_units(all_nffn, weights_gate_up)

    aligned = unit_rows % 16 == 0
    if aligned:
        grads_down = make_grad_down(scal, mixed_units, all_tokens, shards)
    else:
        all_dy = jnp.concatenate([a[rows:] for a in all_tokens], axis=0)
        grad_down = dot(mixed_units, all_dy, 0, 0).astype(bf16)
        grads_down = [
            take_blocks(
                grad_down,
                [order[2 + l] * unit_rows for l in range(shards) if parity_of[l] == side],
                unit_rows,
            )
            for side in range(2)
        ]
    joint = together([*near_down, *grads_down])
    near_down, grads_down = joint[:-2], joint[-2:]
    far_down = gather_far(near_down, chip)
    sums_down = core_sum(*grads_down)
    joint = together(with_other_core(near_down) + far_down, *sums_down)
    down_parts, far_down = list(joint[:2]), joint[2:]
    down_parts, down_shards = down_parts + with_other_core(far_down), shards
    if not aligned:
        joined = jnp.concatenate(down_parts, axis=0)
        place = jnp.argsort(order[2:])
        down_parts = [take_blocks(joined, [place[r] * unit_rows for r in range(shards)], unit_rows)]
        down_shards = 1

    far_sum = None
    if len(sums_down) == 2:
        far_sum = reduce_far(after(sums_down[0], *far_down))
    grad_units = units_back(scal, gate, up, all_tokens, down_parts, down_shards)
    if far_sum is not None:
        far_sum, grad_units = together([far_sum, grad_units])
    sends, kept = near_sends(sums_down[-1], far_sum, chip)
    sends = together(sends, grad_units)
    received = near_receive(sends)
    parts = ffn_transposed(after(grad_units, *sends), weights_gate_up, blocks)
    grads_gate_up = units_grad(scal, normed_ffn, after(grad_units, *parts), shards)
    parts = ctx_exchange(parts)
    n = len(received)
    joint = together([*received, *grads_gate_up])
    received, grads_gate_up = joint[:n], joint[n:]
    far_sum, far_add = [], grads_gate_up[0]
    if len(grads_gate_up) == 3:
        both = core_exchange(grads_gate_up[2])
        far_add = add_low(both[:shard_rows], both[shard_rows:])
        far_sum = [reduce_far(far_add)]
    share_down = near_total(received, kept, chip)
    parts = together(parts, far_add)
    grad_hidden, low, grad_gain_ffn = ffn_norm_back(
        scal, hidden, gains, own_tokens, parts, shards
    )

    all_low = ctx_gather(low)
    near_sum = add_low(grads_gate_up[0], core_swap(after(grads_gate_up[1], low)))
    result_parts = multiply_down(
        scal, after(mixed_units, near_sum, share_down), down_parts, down_shards, blocks
    )
    near_sum, *result_parts = together([near_sum, *result_parts])
    sends, kept = near_sends(near_sum, far_sum[0] if far_sum else None, chip)
    received = near_receive(sends)
    result_parts = ctx_exchange(together(result_parts, *all_low))
    if strided:
        grad_att = make_grad_attended(after(scal, *sends), all_low, weights_attn, shards)
    else:
        grad_att = dot(jnp.concatenate(all_low, axis=0), full_out, 1, 1).astype(bf16)
    *grads, diagonals = attention_backward(scal, qkv, probs, grad_att, rows, blocks)
    joint = together([*grads, *result_parts])
    grads, result_parts = joint[:3], joint[3:]
    result = hidden
    for part in result_parts:
        result = result + part.astype(f32)
    result = result.astype(bf16)
    parts, grad_gain_attn = attn_transposed(
        scales, grads, all_tokens, weights_attn, shard_rows, shards, blocks
    )
    near_down_share = ctx_gather_near(after(share_down, *result_parts))
    joint = together([*parts, *near_down_share])
    parts, near_down_share = list(joint[:blocks]), joint[blocks:]
    parts = ctx_exchange(parts)
    grads_attn = attn_grad(
        scal,
        normed,
        attended,
        [after(grads[0], *parts[:1]), *grads[1:]],
        diagonals,
        grad_gain_attn,
        grad_gain_ffn,
        all_low,
        shards,
        each,
        stride,
    )
    n = len(received)
    joint = together([*received, *grads_attn])
    received, grads_attn = joint[:n], joint[n:]
    share_gate_up = near_total(received, kept, chip)
    joint = together([*parts, share_gate_up, *grads_attn])
    parts, share_gate_up, grads_attn = joint[:blocks], joint[blocks], joint[blocks + 1 :]
    input_grad = attn_norm_back(scal, grad_hidden, gains, own_tokens, parts, shards)
    far_sum, far_add = [], grads_attn[0]
    if len(grads_attn) == 4:
        far_add = add_low(grads_attn[2], core_swap(grads_attn[3]))
        far_sum = [reduce_far(far_add)]
    near_sum = add_low(grads_attn[0], core_swap(after(grads_attn[1], far_add)))
    near_units = ctx_gather_near(after(share_gate_up, far_add))
    near_sum, *far_sum = together([near_sum, *far_sum])
    far_sum = far_sum[0] if far_sum else None
    cut = 2 * shard_rows
    sends, kept = near_sends(near_sum, far_sum, chip, (0, cut))
    first = near_receive(sends)
    far_units = ctx_gather_far(near_units)
    sends, later = near_sends(
        after(near_sum, *far_units),
        None if far_sum is None else after(far_sum, *far_units),
        chip,
        (cut, stride),
    )
    far_down_share = ctx_gather_far(together(near_down_share, *far_units))
    n = len(first)
    joint = together([*first, *far_down_share, *sends])
    first, far_down_share, sends = joint[:n], joint[n:-n], joint[-n:]
    first = near_total(first, kept, chip)
    second = near_receive(sends)
    joint = together([*ctx_gather(first), *second])
    pieces_first, second = joint[:blocks], near_total(joint[blocks:], later, chip)
    pieces_second = ctx_gather(second)
    pieces_gate_up = ctx_pieces(share_gate_up, near_units, far_units)
    pieces_down = ctx_pieces(share_down, near_down_share, far_down_share)

    g_down = assemble_rows(scal, pieces_down)
    if blocks * unit_rows % 128 == 0:
        g_gate, g_up = assemble_units(scal, pieces_gate_up, shards)
    else:
        stacked = jnp.stack(pieces_gate_up)
        stacked = [
            lax.dynamic_slice_in_dim(stacked, position ^ c, 1, 0)[0] for c in range(blocks)
        ]
        g_gate, g_up = [
            jnp.concatenate(
                [
                    stacked[c][:, n * units + r * unit_rows : n * units + (r + 1) * unit_rows]
                    for r in range(shards)
                    for c in range(blocks)
                ],
                axis=1,
            ).astype(f32)
            for n in range(2)
        ]
    outs_attn = attention_outputs(
        scal, list(pieces_first), 2, shard_rows, each, head_width, False
    )
    *rest, small = attention_outputs(
        scal, list(pieces_second), 1, shard_rows, each, head_width, True
    )
    outs_attn = [*outs_attn, *rest]
    if not strided:
        spot = jnp.zeros((width, width), bf16)
        spot = lax.dynamic_update_slice_in_dim(
            spot,
            dot(attended, jnp.concatenate(all_low, axis=0), 0, 0).astype(bf16),
            position * my_heads * head_width,
            0,
        )
        g_out = lax.psum_scatter(spot, "fsdp", scatter_dimension=0, tiled=True)
        outs_attn.append(lax.psum(g_out, "ctx").astype(f32))
    buckets = relative_bias_table.shape[0]
    return (
        result[None],
        input_grad[None],
        *outs_attn,
        g_gate,
        g_up,
        g_down,
        small[0, :shard_rows],
        small[1, :shard_rows],
        small[2 : 2 + buckets, :heads],
    )


def solution(mesh):
    rows = P("fsdp", None)
    tokens = P("fsdp", "ctx", None)
    in_specs = (tokens, P("fsdp")) + (rows,) * 7 + (P("fsdp"), P("fsdp"), rows, tokens)
    out_specs = (tokens, tokens) + (rows,) * 7 + (P("fsdp"), P("fsdp"), rows)
    return jax.shard_map(
        on_device, mesh=mesh, in_specs=in_specs, out_specs=out_specs, check_vma=False
    )
```
